32 devices in a mesh: section: 2 (over core), batch: 4 (over y, x), tm: 4 (over z).
Axes of the slice: x: 2, y: 2, z: 4, core: 2. Of those that a mesh axis runs over, the one named last changes fastest.
Arguments:
- audio_in: bfloat16 [4, 4, 512, 4096], P(None, 'batch', None, 'tm'), may hold values from -6 to 6
- conditioning: bfloat16 [4, 4, 80, 4096], P(None, 'batch', None, 'tm'), may hold values from -6 to 6
- clip_lengths: int32 [4, 4, 8], P(None, 'batch'), may hold values from 1 to 3584, 4096 in all within a row
- conv_weight: bfloat16 [2, 2, 1024, 512], P('section'), may hold values from -0.1875 to 0.1875
- conv_bias: float32 [2, 1024], P('section'), may hold values from -3 to 3
- cond_weight: bfloat16 [2, 1024, 80], P('section'), may hold values from -0.625 to 0.625
- res_weight: bfloat16 [2, 512, 512], P('section'), may hold values from -0.75 to 0.75
- res_bias: float32 [2, 512], P('section'), may hold values from -3 to 3
- skip_weight: bfloat16 [2, 512, 512], P('section'), may hold values from -0.75 to 0.75
- skip_bias: float32 [2, 512], P('section'), may hold values from -3 to 3
- cot_res: bfloat16 [4, 4, 512, 4096], P(None, 'batch', None, 'tm'), may hold values from -6 to 6
- cot_skip: bfloat16 [4, 4, 512, 4096], P(None, 'batch', None, 'tm'), may hold values from -6 to 6
Outputs:
- res_stream: bfloat16 [2, 4, 4, 512, 4096], P('section', None, 'batch', None, 'tm')
- skip_stream: bfloat16 [2, 4, 4, 512, 4096], P('section', None, 'batch', None, 'tm')
- res_grad: float32 [2, 4, 4, 512, 4096], P('section', None, 'batch', None, 'tm')
- cond_grad: float32 [4, 4, 80, 4096], P(None, 'batch', 'section', 'tm')
- conv_weight_grad: float32 [2, 2, 1024, 512], P('section')
- conv_bias_grad: float32 [2, 1024], P('section')
- cond_weight_grad: float32 [2, 1024, 80], P('section')
- res_weight_grad: float32 [2, 512, 512], P('section')
- res_bias_grad: float32 [2, 512], P('section')
- skip_weight_grad: float32 [2, 512, 512], P('section')
- skip_bias_grad: float32 [2, 512], P('section')
The draws below stay inside these ranges and needn't reach their ends.
Inputs may be any that keep to these rules, and one draw needn't show every extreme that they name: `clip_lengths`: each line of 4096 samples is cut into 8 clips in order; their lengths sum to 4096 and the longest is exactly 3584 samples.
All inputs are finite; a program needn't handle non-finite values.
Results may differ from the reference program's by a relative error of at most 0.0074.
Values may be sent and summed in bfloat16 or wider, within the bound.
A program may use at most 192 MiB of HBM per device.

```python
import math
import jax
import jax.numpy as jnp
import numpy as np
from jax import lax

C = 512
H = 512
S = 512
CC = 80
G = 1024
FIRST_DILATION = 512
CLIPS = 8
M = 4
TL = 1024
B = 4
LEN = 4096


def shard_levels(stream_key, dims, cuts, least, top_value):
    gain, own = 1.0, jax.random.fold_in(stream_key, 6)
    for dim, shards_of in cuts:
        heights = jnp.exp(jax.random.uniform(jax.random.fold_in(own, dim), (shards_of,), jnp.float32, least / len(cuts), top_value / len(cuts)))
        gain = gain * jnp.repeat(heights, dims[dim] // shards_of).reshape([-1 if axis == dim else 1 for axis in range(len(dims))])
    return gain


def split_up(count, total, most, lean):
    weights = [(1 << 20) // math.isqrt(standing ** lean) + 1 for standing in range(2, count + 1)]
    rest, given = total - most - (count - 1), [1] * (count - 1)
    while rest > 0:
        candidates = [i for i in range(count - 1) if given[i] < most]
        mass, budget = sum([weights[i] for i in candidates]), rest
        for i in candidates:
            extra = min(most - given[i], max(1, budget * weights[i] // mass), rest)
            given[i] = given[i] + extra
            rest = rest - extra
    return np.array([most] + given)


def ragged(key, count, total, most, skew):
    if count == 2:
        one = jax.random.randint(key, (), max(1, total - most), min(most, total - 1) + 1)
        return jnp.stack([one, total - one])
    sizes = jnp.asarray(split_up(count, total, most, skew), jnp.int32)
    twos = (count - 1) // 2
    source_of, receiver = sizes[1:1 + 2 * twos:2], sizes[2:2 + 2 * twos:2]
    slack = jnp.minimum(source_of - 1, most - receiver)
    moved = jax.random.randint(jax.random.fold_in(key, 1), (twos,), 0, 1 << 20) % (slack + 1)
    sizes = sizes.at[1:1 + 2 * twos:2].set(source_of - moved).at[2:2 + 2 * twos:2].set(receiver + moved)
    return sizes[jax.random.permutation(jax.random.fold_in(key, 2), count)]


def bell_draw(own_key, shape, spread, limit, cuts=(), kind=jnp.bfloat16):
    drawn = spread * jax.random.normal(own_key, shape, jnp.float32)
    if cuts:
        drawn = drawn * shard_levels(own_key, shape, cuts, -0.22, 0.18)
    return jnp.clip(drawn, -limit, limit).astype(kind)


def setup_inputs(seed: int = 0) -> dict:
    seeds = jax.random.split(jax.random.key(seed), 13)
    audio_in = bell_draw(seeds[0], (M, B, C, LEN), 1.0, 6.0, ((1, 4), (3, 4)))
    conditioning = bell_draw(seeds[1], (M, B, CC, LEN), 1.0, 6.0, ((1, 4), (3, 4)))
    clip_lengths = jax.vmap(lambda own: ragged(own, CLIPS, LEN, LEN - TL // 2, 2))(jax.random.split(seeds[2], M * B)).reshape((M, B, CLIPS)).astype(jnp.int32)
    conv_weight = bell_draw(seeds[3], (2, 2, G, C), (2 * C) ** -0.5, 0.1875, ((0, 2),))
    conv_bias = bell_draw(seeds[4], (2, G), 0.5, 3.0, ((0, 2),), jnp.float32)
    cond_weight = bell_draw(seeds[5], (2, G, CC), CC ** -0.5, 0.625, ((0, 2),))
    res_weight = bell_draw(seeds[6], (2, C, H), (H // 8) ** -0.5, 0.75, ((0, 2),))
    res_bias = bell_draw(seeds[7], (2, C), 0.5, 3.0, ((0, 2),), jnp.float32)
    skip_weight = bell_draw(seeds[8], (2, S, H), (H // 8) ** -0.5, 0.75, ((0, 2),))
    skip_bias = bell_draw(seeds[9], (2, S), 0.5, 3.0, ((0, 2),), jnp.float32)
    cot_res = bell_draw(seeds[10], (M, B, C, LEN), 1.0, 6.0, ((1, 4), (3, 4)))
    cot_skip = bell_draw(seeds[11], (M, B, S, LEN), 1.0, 6.0, ((1, 4), (3, 4)))
    return dict(audio_in=audio_in, conditioning=conditioning, clip_lengths=clip_lengths, conv_weight=conv_weight, conv_bias=conv_bias, cond_weight=cond_weight, res_weight=res_weight, res_bias=res_bias, skip_weight=skip_weight, skip_bias=skip_bias, cot_res=cot_res, cot_skip=cot_skip)


@jax.custom_vjp
def low(v):
    return lax.optimization_barrier(v.astype(jnp.bfloat16)).astype(jnp.float32)

@jax.custom_vjp
def low_back(v):
    return v

def low_keep(v):
    return (low(v), None)

def low_pass(kept, grad):
    return (grad,)

def back_keep(v):
    return (v, None)

def back_low(kept, grad):
    return (low(grad),)
low.defvjp(low_keep, low_pass)
low_back.defvjp(back_keep, back_low)
HIGHEST_PREC = lax.Precision.HIGHEST

def apply_weight(weight, values):
    return jnp.dot(weight, values, precision=HIGHEST_PREC)

def wavenet_layer_fn(present_value, skip_in, condition_sequence, clip_begin_index, sample_position, reach, layer_index, weight_bundle):
    conv_weight, conv_bias, cond_weight, res_weight, res_bias, skip_weight, skip_bias = weight_bundle
    delayed = jnp.pad(present_value, ((0, 0), (reach, 0)))[:, :LEN]
    shifted = jnp.where((sample_position - reach >= clip_begin_index)[None, :], delayed, 0.0)
    pre_act = apply_weight(conv_weight[layer_index, 0], shifted) + apply_weight(conv_weight[layer_index, 1], present_value)
    pre_act = pre_act + apply_weight(cond_weight[layer_index], condition_sequence) + conv_bias[layer_index][:, None]
    pre_act = low_back(pre_act)
    hidden = low(jnp.tanh(pre_act[:H]) * jax.nn.sigmoid(pre_act[H:]))
    res_out = present_value + apply_weight(res_weight[layer_index], hidden) + res_bias[layer_index][:, None]
    skip_out = skip_in + apply_weight(skip_weight[layer_index], hidden) + skip_bias[layer_index][:, None]
    return (res_out, skip_out)

def line_loss(weight_bundle, audio_sequence, condition_sequence, probe, lengths, cot_res_line, cot_skip_line):
    clip_ends = jnp.cumsum(lengths).astype(jnp.int32)
    sample_position = jnp.arange(LEN, dtype=jnp.int32)
    clip_begin_index = lax.optimization_barrier(jnp.max(jnp.where(clip_ends[:, None] <= sample_position[None, :], clip_ends[:, None], 0), axis=0)).astype(jnp.int32)
    skip_zero_fill = jnp.zeros((S, LEN), jnp.float32)
    residual_first_layer, skip_first_layer = wavenet_layer_fn(audio_sequence, skip_zero_fill, condition_sequence, clip_begin_index, sample_position, FIRST_DILATION, 0, weight_bundle)
    second_in = low(low_back(residual_first_layer)) + probe
    skip_kept = low(skip_first_layer)
    res_second, skip_second = wavenet_layer_fn(second_in, skip_kept, condition_sequence, clip_begin_index, sample_position, 1, 1, weight_bundle)
    line_total = jnp.sum(cot_res_line * res_second) + jnp.sum(cot_skip_line * skip_second)
    return (line_total, (low(residual_first_layer), skip_kept, res_second, skip_second))

def reference(audio_in, conditioning, clip_lengths, conv_weight, conv_bias, cond_weight, res_weight, res_bias, skip_weight, skip_bias, cot_res, cot_skip):
    weight_bundle = (conv_weight.astype(jnp.float32), conv_bias.astype(jnp.float32), cond_weight.astype(jnp.float32), res_weight.astype(jnp.float32), res_bias.astype(jnp.float32), skip_weight.astype(jnp.float32), skip_bias.astype(jnp.float32))
    line_count = M * B
    audio_lines = audio_in.astype(jnp.float32).reshape(line_count, C, LEN)
    cond_lines = conditioning.astype(jnp.float32).reshape(line_count, CC, LEN)
    length_lines = clip_lengths.reshape(line_count, CLIPS).astype(jnp.int32)
    cot_res_lines = cot_res.astype(jnp.float32).reshape(line_count, C, LEN)
    cot_skip_lines = cot_skip.astype(jnp.float32).reshape(line_count, S, LEN)

    def one_line(sums, items):
        audio_sequence, condition_sequence, lengths, cot_res_line, cot_skip_line = items

        def line_fn(weight_set, audio_part, cond_part, probe):
            return line_loss(weight_set, audio_part, cond_part, probe, lengths, cot_res_line, cot_skip_line)
        probe = jnp.zeros((C, LEN), jnp.float32)
        line_total, pullback, forward_outs = jax.vjp(line_fn, weight_bundle, audio_sequence, condition_sequence, probe, has_aux=True)
        grads_w, grad_audio, grad_cond, grad_probe = pullback(jnp.ones_like(line_total))
        sums = jax.tree.map(jnp.add, sums, grads_w)
        return (sums, (forward_outs, grad_audio, grad_cond, grad_probe))
    zero_sums = jax.tree.map(jnp.zeros_like, weight_bundle)
    sums, (forward_outs, grad_audio, grad_cond, grad_probe) = lax.scan(one_line, zero_sums, (audio_lines, cond_lines, length_lines, cot_res_lines, cot_skip_lines))
    residual_first_layer, skip_first_layer, res_second, skip_second = forward_outs
    res_stream = jnp.stack([residual_first_layer.reshape(M, B, C, LEN), res_second.reshape(M, B, C, LEN)]).astype(jnp.bfloat16)
    skip_stream = jnp.stack([skip_first_layer.reshape(M, B, S, LEN), skip_second.reshape(M, B, S, LEN)]).astype(jnp.bfloat16)
    res_grad = jnp.stack([grad_audio.reshape(M, B, C, LEN), grad_probe.reshape(M, B, C, LEN)])
    cond_grad = grad_cond.reshape(M, B, CC, LEN)
    return (res_stream, skip_stream, res_grad, cond_grad, sums[0], sums[1], sums[2], sums[3], sums[4], sums[5], sums[6])
```

```python
import functools
import math

import jax
import jax.numpy as jnp
from jax import lax
from jax.experimental import pallas as pl
from jax.experimental.pallas import tpu as pltpu
from jax.sharding import PartitionSpec as P

REACH0 = 512
TC = 256
MESH = pl.DeviceIdType.MESH
BF = jnp.bfloat16
F32 = jnp.float32
PW = 128


def dot(a, b):
    return jnp.dot(a, b, preferred_element_type=F32)


def dot_nt(a, b):
    return lax.dot_general(a, b, (((1,), (1,)), ((), ())), preferred_element_type=F32)


def rows_at(start, size, step):
    return pl.ds(pl.multiple_of(start, step), size)


def kernel(
    nz,
    r,
    cr,
    audio,
    cond,
    clips,
    convw,
    convb,
    condw,
    resw,
    resb,
    skipw,
    skipb,
    cotr,
    cots,
    res_out,
    skip_out,
    rgrad_out,
    cgrad_out,
    wg_out,
    wcat,
    wrs,
    wct,
    wrst,
    cwraw,
    cbraw,
    rbraw,
    sbraw,
    rsbias,
    rh,
    hid,
    gb,
    gr,
    cs,
    sk0,
    r1,
    cg,
    eye,
    erow,
    mkf,
    mkb,
    htile,
    bcar,
    colf_s,
    colf_r,
    colb_s,
    colb_r,
    hb,
    pb,
    prv,
    ra_buf,
    rb_buf,
    rz_buf,
    cacc,
    ld_w,
    ld_x,
    ld_c,
    ld_r,
    ld_s,
    w_snd,
    w_rcv,
    h_snd,
    h_rcv,
    cf_snd,
    cf_rcv,
    cb_snd,
    cb_rcv,
    hb_snd,
    hb_rcv,
    o_loc,
    o_snd,
    o_rcv,
    c_loc,
    p_loc,
    p_snd,
    x_snd,
    x_rcv,
    ar_snd,
    ar_rcv,
    f_loc,
    f_snd,
    f_rcv,
    credit,
):
    C = audio.shape[2]
    TL = audio.shape[3]
    KC = cond.shape[2]
    NJ = TL // TC
    HJ = REACH0 // TC
    G = 2 * C
    KP = rh.shape[3]
    HR = pb.shape[1]
    s = lax.axis_index("section")
    b = lax.axis_index("batch")
    z = lax.axis_index("tm")
    other = (1 - s, b, z)
    zprev = (s, b, z - 1)
    znext = (s, b, z + 1)
    has_prev = z > 0
    has_next = z < nz - 1

    def copy(src, dst, sem):
        return pltpu.make_async_copy(src, dst, sem)

    def rcopy(src, dst, ssem, rsem, dev):
        return pltpu.make_async_remote_copy(
            src_ref=src, dst_ref=dst, send_sem=ssem, recv_sem=rsem, device_id=dev, device_id_type=MESH
        )

    def weight_pairs(layer):
        return [
            (convw.at[0, 0], wcat.at[layer, :, pl.ds(0, C)]),
            (convw.at[0, 1], wcat.at[layer, :, pl.ds(C, C)]),
            (resw.at[0], wrs.at[layer, pl.ds(0, C)]),
            (skipw.at[0], wrs.at[layer, pl.ds(C, C)]),
            (condw.at[0], cwraw.at[layer]),
            (convb, cbraw.at[layer]),
            (resb, rbraw.at[layer]),
            (skipb, sbraw.at[layer]),
        ]

    own_w = [copy(a, d, ld_w.at[k]) for k, (a, d) in enumerate(weight_pairs(s))]
    for c in own_w:
        c.start()
    ldx, ldc, ldr, lds = [], [], [], []
    for i in range(2):
        for j in reversed(range(NJ)):
            cols = pl.ds(j * TC, TC)
            m = 2 * s + i
            ldx.append(copy(audio.at[m, 0, :, cols], rh.at[0, i, j, pl.ds(C, C)], ld_x.at[i, j]))
            ldc.append(copy(cond.at[m, 0, :, cols], rh.at[0, i, j, pl.ds(G, KC)], ld_c.at[i, j]))
            ldr.append(copy(cotr.at[m, 0, :, cols], gr.at[1, i, j], ld_r.at[i, j]))
            lds.append(copy(cots.at[m, 0, :, cols], cs.at[i, j], ld_s.at[i, j]))
    for c in ldx + ldc + ldr + lds:
        c.start()

    bar = pltpu.get_barrier_semaphore()

    def sa_dev(o):
        a2 = lax.rem(amem + o, r)
        return a2, (s, jnp.where(s == 0, bhi * r + a2, a2 * r + blo), z)

    def sb_dev(o):
        b2 = lax.rem(bmem + o, r)
        return b2, (s, jnp.where(s == 0, b2 * r + blo, bhi * r + b2), z)

    def sz_dev(o):
        z2 = lax.rem(z + o, nz)
        return z2, (s, b, z2)

    bhi = b // r
    blo = lax.rem(b, r)
    amem = jnp.where(s == 0, blo, bhi)
    bmem = jnp.where(s == 0, bhi, blo)
    peers = [other]
    peers += [sa_dev(o)[1] for o in range(1, r)]
    peers += [sb_dev(o)[1] for o in range(1, r)]
    peers += [sz_dev(o)[1] for o in range(1, nz)]
    for dev in peers:
        pl.semaphore_signal(bar, inc=1, device_id=dev, device_id_type=MESH)

    ri = lax.broadcasted_iota(jnp.int32, (TC, TC), 0)
    ci = lax.broadcasted_iota(jnp.int32, (TC, TC), 1)
    eye[...] = (ri == ci).astype(F32).astype(BF)
    re = lax.broadcasted_iota(jnp.int32, (PW, TC), 0)
    erow[...] = (re == KC + 3).astype(F32).astype(BF)
    bcar[...] = jnp.zeros(bcar.shape, BF)
    rk = lax.broadcasted_iota(jnp.int32, (KP - G - KC, TC), 0)
    ones_rows = (rk < 3).astype(F32).astype(BF)
    for i in range(2):
        m = 2 * s + i
        for j in range(NJ):
            rh[0, i, j, pl.ds(G + KC, KP - G - KC), :] = ones_rows
            rh[1, i, j, pl.ds(G + KC, KP - G - KC), :] = ones_rows
            pos = z * TL + j * TC + lax.broadcasted_iota(jnp.int32, (16, TC), 1)
            start = jnp.zeros((16, TC), jnp.int32)
            end = jnp.int32(0)
            for k in range(clips.shape[2]):
                end = end + clips[m, 0, k]
                start = jnp.where(end <= pos, end, start)
            for layer, reach in ((0, REACH0), (1, 1)):
                keep = jnp.where(pos - reach >= start, 1.0, 0.0).astype(F32)
                mkf[layer, i, j] = keep[:8]
                mkb[layer, i, j] = keep.astype(BF)

    @pl.when(jnp.logical_not(has_prev))
    def _():
        for i in range(2):
            for j in range(HJ):
                rh[0, i, j, pl.ds(0, C), :] = jnp.zeros((C, TC), BF)
            htile[i] = jnp.zeros((C, PW), BF)

    pl.semaphore_wait(bar, len(peers))

    far_w = [
        rcopy(a, d, w_snd.at[k], w_rcv.at[k], other) for k, (a, d) in enumerate(weight_pairs(s))
    ]
    for c in far_w:
        c.start()

    def halo(i, j):
        return rcopy(
            audio.at[2 * s + i, 0, :, rows_at(TL - REACH0 + j * TC, TC, TC)],
            rh.at[0, i, j, pl.ds(0, C)],
            h_snd.at[i, j],
            h_rcv.at[i, j],
            znext,
        )

    @pl.when(has_next)
    def _():
        for i in range(2):
            for j in reversed(range(HJ)):
                halo(i, j).start()

    def prepare(layer):
        lane = lax.broadcasted_iota(jnp.int32, (G, PW), 1)
        bias = jnp.broadcast_to(cbraw[layer], (PW, G)).T
        hi = bias.astype(BF).astype(F32)
        mid = (bias - hi).astype(BF).astype(F32)
        low = (bias - hi) - mid
        wcat[layer, :, pl.ds(G, PW)] = jnp.zeros((G, PW), BF)
        wcat[layer, :, pl.ds(G, KC)] = cwraw[layer]
        base = wcat[layer, :, pl.ds(G, PW)].astype(F32)
        base = jnp.where(lane == KC, hi, base)
        base = jnp.where(lane == KC + 1, mid, base)
        base = jnp.where(lane == KC + 2, low, base)
        wcat[layer, :, pl.ds(G, PW)] = base.astype(BF)
        rsbias[layer, pl.ds(0, C)] = jnp.broadcast_to(rbraw[layer], (PW, C)).T
        rsbias[layer, pl.ds(C, C)] = jnp.broadcast_to(sbraw[layer], (PW, C)).T

        @pl.loop(0, G // TC)
        def _(k):
            cols = rows_at(k * TC, TC, TC)
            wct[layer, cols, :] = dot_nt(eye[...], wcat[layer, :, cols]).astype(BF)

        wct[layer, pl.ds(G, PW), :] = dot_nt(
            eye[pl.ds(0, PW), pl.ds(0, PW)], wcat[layer, :, pl.ds(G, PW)]
        ).astype(BF)

        @pl.loop(0, C // TC)
        def _(k):
            cols = rows_at(k * TC, TC, TC)
            wrst[layer, cols, :] = dot_nt(eye[...], wrs[layer, :, cols]).astype(BF)

    for c in own_w:
        c.wait()
    prepare(s)
    for c in far_w:
        c.wait()
    prepare(1 - s)
    for c in ldx + ldc:
        c.wait()
    for i in range(2):
        for j in range(NJ):
            rh[1, i, j, pl.ds(G, KC), :] = rh[0, i, j, pl.ds(G, KC), :]

    def wide(tile):
        return jnp.concatenate([tile, tile], axis=1)

    def gate(layer, i, j):
        xx = rh[layer, i, j]
        out = []
        for g in range(2):
            lo = pl.ds(g * TC, TC)
            hi = pl.ds(C + g * TC, TC)
            t = jnp.tanh(dot(wcat[layer, lo, :], xx))
            q = 0.5 * jnp.tanh(0.5 * dot(wcat[layer, hi, :], xx)) + 0.5
            h = t * q
            hid[layer, i, j, lo, :] = h.astype(BF)
            out.append((q - h * t, h - h * q))
        return out

    def out_copy(kind, layer, i, j, src, dst):
        m = 2 * s + i
        return (
            copy(src, dst.at[m, :, rows_at(j * TC, TC, TC)], o_loc.at[kind, i, j]),
            rcopy(
                src,
                dst.at[m, :, rows_at(j * TC, TC, TC)],
                o_snd.at[kind, i, j],
                o_rcv.at[kind],
                other,
            ),
        )

    def out_start(kind, layer, i, j, src, dst):
        near, far = out_copy(kind, layer, i, j, src, dst)
        start_either(layer, near, far)

    def panel(i, j, k):
        return rows_at(((i * NJ + j) * (TC // PW) + k) * C, C, C)

    def panel_copy(i, j, k):
        src = r1.at[panel(i, j, k)]
        dst = res_out.at[2 * s + i, :, rows_at(j * TC + k * PW, PW, PW)]
        return (
            copy(src, dst, p_loc.at[i, j, k]),
            rcopy(src, dst, p_snd.at[i, j, k], o_rcv.at[2], other),
        )

    def start_either(layer, near, far):
        @pl.when(s == layer)
        def _():
            near.start()

        @pl.when(s != layer)
        def _():
            far.start()

    def panels_sent():
        @pl.loop(0, 2 * NJ)
        def _(n):
            for k in range(TC // PW):
                near, far = panel_copy(n // NJ, lax.rem(n, NJ), k)

                @pl.when(s == 1)
                def _():
                    near.wait()

                @pl.when(s != 1)
                def _():
                    far.wait_send()

    def out_sent(kind, layer, i, j, src, dst):
        near, far = out_copy(kind, layer, i, j, src, dst)

        @pl.when(s == layer)
        def _():
            near.wait()

        @pl.when(s != layer)
        def _():
            far.wait_send()

    def out_arrived(kind, layer, dst):
        half = dst.at[pl.ds(0, 2)]

        @pl.when(s == layer)
        def _():
            copy(half, half, o_rcv.at[kind]).wait()

    def col_copy_f(i):
        return rcopy(colf_s.at[i], colf_r.at[i], cf_snd.at[i], cf_rcv.at[i], znext)

    def col_copy_b(i):
        return rcopy(colb_s.at[i], colb_r.at[i], cb_snd.at[i], cb_rcv.at[i], zprev)

    def pick_col(tile, lane):
        li = lax.broadcasted_iota(jnp.int32, (16, PW), 1)
        return dot_nt((li == lane).astype(F32).astype(BF), tile).astype(BF)

    def spread_col(rows):
        full = jnp.concatenate([rows] * (PW // 16), axis=0)
        parts = [
            dot_nt(eye[...], full[:, k * TC : (k + 1) * TC]) for k in range(C // TC)
        ]
        return jnp.concatenate(parts, axis=0)

    def fwd0(i, j):
        far = j >= HJ
        src_j = jnp.where(far, j - HJ, j)
        src_row = jnp.where(far, C, 0)
        mask = jnp.concatenate([mkb[0, i, j]] * (C // 16), axis=0)
        rh[0, i, j, pl.ds(0, C), :] = rh[0, i, src_j, rows_at(src_row, C, C), :] * mask
        parts = gate(0, i, j)
        for g in range(2):
            gb[0, i, j, pl.ds(g * TC, TC), :] = parts[g][0].astype(BF)
            gb[0, i, j, pl.ds(C + g * TC, TC), :] = parts[g][1].astype(BF)
        rs = dot(wrs[0], hid[0, i, j]) + wide(rsbias[0])
        x1 = (rh[0, i, j, pl.ds(C, C), :].astype(F32) + rs[:C]).astype(BF)
        rh[1, i, j, pl.ds(C, C), :] = x1
        sk0[i, j] = rs[C:].astype(BF)
        out_start(0, 0, i, j, rh.at[1, i, j, pl.ds(C, C)], res_out)
        out_start(1, 0, i, j, sk0.at[i, j], skip_out)

        @pl.when(jnp.logical_and(j == NJ - 1, has_next))
        def _():
            colf_s[i] = pick_col(rh[1, i, j, pl.ds(C, C), pl.ds(TC - PW, PW)], PW - 1)
            col_copy_f(i).start()

    lane_c = lax.broadcasted_iota(jnp.int32, (C, PW), 1)

    def layer1(i, j):
        x1 = rh[1, i, j, pl.ds(C, C), :].astype(F32)
        jm = jnp.maximum(j - 1, 0)
        tile = rh[1, i, jm, pl.ds(C, C), pl.ds(TC - PW, PW)].astype(F32)
        tile = jnp.where(j == 0, htile[i].astype(F32), tile)
        turned = pltpu.roll(x1, 1, 1)
        first = jnp.where(lane_c == 0, pltpu.roll(tile, 1, 1), turned[:, :PW])
        shifted = jnp.concatenate([first, turned[:, PW:]], axis=1) * mkf[1, i, j, pl.ds(0, 1), :]
        rh[1, i, j, pl.ds(0, C), :] = shifted.astype(BF)
        gh = dot(wrst[1], jnp.concatenate([gr[1, i, j], cs[i, j]], axis=0))
        parts = gate(1, i, j)
        for g in range(2):
            part = gh[g * TC : (g + 1) * TC]
            gb[1, i, j, pl.ds(g * TC, TC), :] = (part * parts[g][0]).astype(BF)
            gb[1, i, j, pl.ds(C + g * TC, TC), :] = (part * parts[g][1]).astype(BF)
        rs = dot(wrs[1], hid[1, i, j]) + wide(rsbias[1])
        res1 = (rh[1, i, j, pl.ds(C, C), :].astype(F32) + rs[:C]).astype(BF)
        for k in range(TC // PW):
            r1[panel(i, j, k), :] = res1[:, k * PW : (k + 1) * PW]
            near, far = panel_copy(i, j, k)
            start_either(1, near, far)
        out_sent(1, 0, i, j, sk0.at[i, j], skip_out)
        sk0[i, j] = (sk0[i, j].astype(F32) + rs[C:]).astype(BF)
        out_start(3, 1, i, j, sk0.at[i, j], skip_out)
        dg = dot(wct[1], gb[1, i, j])
        past = dg[:C] * mkf[1, i, j, pl.ds(0, 1), :]
        turned = pltpu.roll(past, TC - 1, 1)
        last = jnp.where(lane_c == PW - 1, pltpu.roll(bcar[i].astype(F32), PW - 1, 1), turned[:, TC - PW :])
        back = jnp.concatenate([turned[:, : TC - PW], last], axis=1)
        gr[0, i, j] = (gr[1, i, j].astype(F32) + dg[C:G] + back).astype(BF)
        bcar[i] = past[:, :PW].astype(BF)
        cg[i, j] = dg[G : G + KC]

        @pl.when(jnp.logical_and(j == 0, has_prev))
        def _():
            colb_s[i] = pick_col(past[:, :PW].astype(BF), 0)
            col_copy_b(i).start()

    @pl.loop(0, 2 * (NJ - HJ))
    def _(n):
        fwd0(n // (NJ - HJ), NJ - 1 - lax.rem(n, NJ - HJ))

    for c in ldr + lds:
        c.wait()

    @pl.loop(0, 2 * NJ)
    def _(n):
        q = n - 2
        i = jnp.where(n < 2, n, q // (NJ - 1))
        j = jnp.where(n < 2, NJ - 1, NJ - 2 - lax.rem(q, NJ - 1))

        @pl.when(jnp.logical_and(n >= 2, j >= 1))
        def _():
            @pl.when(jnp.logical_and(has_prev, j <= HJ))
            def _():
                halo(i, j - 1).wait_recv()

            fwd0(i, j - 1)

        @pl.when(jnp.logical_and(j == 0, has_prev))
        def _():
            col_copy_f(i).wait_recv()
            htile[i] = spread_col(colf_r[i]).astype(BF)

        layer1(i, j)

    offs = [0, 2 * G, 4 * G]
    sizes = [2 * G, 2 * G, 2 * G + cr]
    ARA, ARB, ARZ, AGZ, AGB, AGA = range(6)

    def geo(p):
        size, off = sizes[p], offs[p]
        na, nb_, nzr = size // r, size // (r * r), size // (r * r * nz)
        base_a = off + amem * na
        base_b = base_a + bmem * nb_
        base_z = base_b + z * nzr
        return size, off, na, nb_, nzr, base_a, base_b, base_z

    def x_copy(layer, p):
        return rcopy(
            pb.at[0, pl.ds(offs[p], sizes[p])],
            prv.at[pl.ds(offs[p], sizes[p])],
            x_snd.at[layer, p],
            x_rcv.at[layer, p],
            other,
        )

    def gathered(layer, rows):
        return r1.at[rows] if layer == 1 else pb.at[0, rows]

    def wait_rows(count, sem, layer):
        ref = pb.at[1 + layer, pl.ds(0, count)]
        copy(ref, ref, sem).wait()

    def sum_rows(layer, start, count, parts):
        total = pb[1 + layer, rows_at(start, count, 16), :].astype(F32)
        for part in parts:
            total = total + part.astype(F32)
        return total.astype(BF)

    def add_rows(layer, start, count, parts):
        pb[1 + layer, rows_at(start, count, 16), :] = sum_rows(layer, start, count, parts)

    def step0(layer, p):
        size, off, na, nb_, nzr, base_a, base_b, base_z = geo(p)
        x_copy(layer, p).wait()
        add_rows(layer, off, size, [prv[pl.ds(off, size), :]])
        if layer == 1:
            pl.semaphore_signal(credit.at[p], inc=1, device_id=other, device_id_type=MESH)
        for o in range(1, r):
            a2, dev = sa_dev(o)
            rcopy(
                pb.at[1 + layer, rows_at(off + a2 * na, na, 16)],
                ra_buf.at[layer, o - 1, pl.ds(off // r, na)],
                ar_snd.at[ARA, layer, p],
                ar_rcv.at[ARA, layer, p],
                dev,
            ).start()

    def step1(layer, p):
        size, off, na, nb_, nzr, base_a, base_b, base_z = geo(p)
        wait_rows((r - 1) * na, ar_rcv.at[ARA, layer, p], layer)
        wait_rows((r - 1) * na, ar_snd.at[ARA, layer, p], layer)
        add_rows(
            layer, base_a, na, [ra_buf[layer, o, pl.ds(off // r, na), :] for o in range(r - 1)]
        )
        for o in range(1, r):
            b2, dev = sb_dev(o)
            rcopy(
                pb.at[1 + layer, rows_at(base_a + b2 * nb_, nb_, 16)],
                rb_buf.at[layer, o - 1, pl.ds(off // (r * r), nb_)],
                ar_snd.at[ARB, layer, p],
                ar_rcv.at[ARB, layer, p],
                dev,
            ).start()

    def step2(layer, p):
        size, off, na, nb_, nzr, base_a, base_b, base_z = geo(p)
        wait_rows((r - 1) * nb_, ar_rcv.at[ARB, layer, p], layer)
        wait_rows((r - 1) * nb_, ar_snd.at[ARB, layer, p], layer)
        add_rows(
            layer,
            base_b,
            nb_,
            [rb_buf[layer, o, pl.ds(off // (r * r), nb_), :] for o in range(r - 1)],
        )
        for o in range(1, nz):
            z2, dev = sz_dev(o)
            rcopy(
                pb.at[1 + layer, rows_at(base_b + z2 * nzr, nzr, 16)],
                rz_buf.at[layer, o - 1, pl.ds(off // (r * r * nz), nzr)],
                ar_snd.at[ARZ, layer, p],
                ar_rcv.at[ARZ, layer, p],
                dev,
            ).start()

    def spread(layer, p, stage, start, count, devs):
        for dev in devs:
            rcopy(
                gathered(layer, rows_at(start, count, 16)),
                gathered(layer, rows_at(start, count, 16)),
                ar_snd.at[stage, layer, p],
                ar_rcv.at[stage, layer, p],
                dev,
            ).start()

    def step3(layer, p):
        size, off, na, nb_, nzr, base_a, base_b, base_z = geo(p)
        wait_rows((nz - 1) * nzr, ar_rcv.at[ARZ, layer, p], layer)
        wait_rows((nz - 1) * nzr, ar_snd.at[ARZ, layer, p], layer)
        gathered(layer, rows_at(base_z, nzr, 16))[...] = sum_rows(
            layer,
            base_z,
            nzr,
            [rz_buf[layer, o, pl.ds(off // (r * r * nz), nzr), :] for o in range(nz - 1)],
        )
        spread(layer, p, AGZ, base_z, nzr, [sz_dev(o)[1] for o in range(1, nz)])

    def step4(layer, p):
        size, off, na, nb_, nzr, base_a, base_b, base_z = geo(p)
        wait_rows((nz - 1) * nzr, ar_rcv.at[AGZ, layer, p], layer)
        wait_rows((nz - 1) * nzr, ar_snd.at[AGZ, layer, p], layer)
        spread(layer, p, AGB, base_b, nb_, [sb_dev(o)[1] for o in range(1, r)])

    def step5(layer, p):
        size, off, na, nb_, nzr, base_a, base_b, base_z = geo(p)
        wait_rows((r - 1) * nb_, ar_rcv.at[AGB, layer, p], layer)
        wait_rows((r - 1) * nb_, ar_snd.at[AGB, layer, p], layer)
        spread(layer, p, AGA, base_a, na, [sa_dev(o)[1] for o in range(1, r)])

    def final_copies(layer, p):
        src = gathered(layer, pl.ds(offs[p], sizes[p]))
        dst = wg_out.at[s, pl.ds(offs[p], sizes[p])]
        return (
            copy(src, dst, f_loc.at[p]),
            rcopy(src, dst, f_snd.at[p], f_rcv.at[p], other),
        )

    def step6(layer, p):
        size, off, na, nb_, nzr, base_a, base_b, base_z = geo(p)
        wait_rows((r - 1) * na, ar_rcv.at[AGA, layer, p], layer)
        wait_rows((r - 1) * na, ar_snd.at[AGA, layer, p], layer)
        near, far = final_copies(layer, p)

        @pl.when(s == layer)
        def _():
            near.start()

        @pl.when(s != layer)
        def _():
            far.start()

    steps = [step0, step1, step2, step3, step4, step5, step6]

    def at(n, table):
        for k, todo in table.items():

            @pl.when(n == k)
            def _(todo=todo):
                for st, layer, p in todo:
                    steps[st](layer, p)

    def weight_tasks(layer, table_a, table_b):
        @pl.loop(0, 4)
        def _(n):
            p = n // 2
            mine = lax.rem(n, 2)
            half = jnp.where(mine == 1, s, 1 - s)
            dst = mine * (1 + layer)
            if layer == 0:

                @pl.when(mine == 0)
                def _():
                    pl.semaphore_wait(credit.at[p], 1)

            ch = rows_at(half * C + p * TC, TC, TC)
            total = dot_nt(gb[layer, 0, 0], rh[layer, 0, 0, ch, :])
            for i in range(2):
                for j in range(NJ):
                    if i + j > 0:
                        total = total + dot_nt(gb[layer, i, j], rh[layer, i, j, ch, :])
            total = total.astype(BF)
            pb[dst, rows_at(p * 2 * G, G, G), :] = total[:, :PW]
            pb[dst, rows_at(p * 2 * G + G, G, G), :] = total[:, PW:]
            for pp in range(2):

                @pl.when(n == 2 * pp)
                def _():
                    x_copy(layer, pp).start()

            at(n, table_a)

        @pl.loop(0, 2)
        def _(n):
            half = jnp.where(n == 1, s, 1 - s)
            dst = n * (1 + layer)
            if layer == 0:

                @pl.when(n == 0)
                def _():
                    pl.semaphore_wait(credit.at[2], 1)

            ch = rows_at(half * TC, TC, TC)
            for src, row in ((lambda i, j: gr[layer, i, j], 0), (lambda i, j: cs[i, j], C)):
                total = dot_nt(src(0, 0), hid[layer, 0, 0, ch, :])
                for i in range(2):
                    for j in range(NJ):
                        if i + j > 0:
                            total = total + dot_nt(src(i, j), hid[layer, i, j, ch, :])
                total = total.astype(BF)
                pb[dst, pl.ds(4 * G + row, C), :] = total[:, :PW]
                pb[dst, pl.ds(5 * G + row, C), :] = total[:, PW:]
            gp_rows = rows_at(half * C, C, C)
            total = jnp.zeros((C, PW), F32)
            for i in range(2):
                for j in range(NJ):
                    total = total + dot_nt(
                        gb[layer, i, j, gp_rows, :], rh[layer, i, j, pl.ds(G, PW), :]
                    )
            cacc[...] = total

            def add_sums(src):
                total = cacc[...]
                for i in range(2):
                    for j in range(NJ):
                        total = total + dot_nt(src(i, j), erow[...])
                cacc[...] = total

            @pl.when(half == 0)
            def _():
                add_sums(lambda i, j: gr[layer, i, j])

            @pl.when(half == 1)
            def _():
                add_sums(lambda i, j: cs[i, j])

            pb[dst, pl.ds(6 * G, C), :] = cacc[...].astype(BF)
            if cr > C:
                pb[dst, pl.ds(6 * G + C, cr - C), :] = jnp.zeros((cr - C, PW), BF)

            @pl.when(n == 0)
            def _():
                x_copy(layer, 2).start()

            at(n, table_b)

    def fix_last(i):
        @pl.when(has_next)
        def _():
            col_copy_b(i).wait_recv()
            tile = gr[0, i, NJ - 1, :, pl.ds(TC - PW, PW)].astype(F32)
            add = spread_col(colb_r[i])
            gr[0, i, NJ - 1, :, pl.ds(TC - PW, PW)] = (
                tile + jnp.where(lane_c == PW - 1, add, 0.0)
            ).astype(BF)

    panels_sent()
    weight_tasks(1, {1: [(0, 1, 0)], 3: [(0, 1, 1)]}, {0: [(1, 1, 0)], 1: [(0, 1, 2)]})

    for i in range(2):
        fix_last(i)
        for j in range(NJ):
            out_start(4, 1, i, j, gr.at[0, i, j], rgrad_out)

    def hb_copy(i, j):
        return rcopy(sk0.at[i, j], hb.at[i, j], hb_snd.at[i, j], hb_rcv.at[i, j], zprev)

    def back0(n, table):
        far = n // (2 * HJ)
        i = lax.rem(n, 2 * HJ) // HJ
        k = lax.rem(n, HJ)
        j = far * HJ + k
        gh = dot(wrst[0], jnp.concatenate([gr[0, i, j], cs[i, j]], axis=0))
        for g in range(2):
            part = gh[g * TC : (g + 1) * TC]
            for row in (g * TC, C + g * TC):
                rows = pl.ds(row, TC)
                gb[0, i, j, rows, :] = (part * gb[0, i, j, rows, :].astype(F32)).astype(BF)
        dg = dot(wct[0], gb[0, i, j])
        past = dg[:C] * mkf[0, i, j, pl.ds(0, 1), :]
        gr[1, i, j] = (gr[0, i, j].astype(F32) + dg[C:G]).astype(BF)
        cg[i, j] = cg[i, j] + dg[G : G + KC]

        @pl.when(far == 0)
        def _():
            @pl.when(has_prev)
            def _():
                out_sent(3, 1, i, j, sk0.at[i, j], skip_out)
                sk0[i, j] = past.astype(BF)
                hb_copy(i, j).start()

        @pl.when(far > 0)
        def _():
            gr[1, i, k] = (gr[1, i, k].astype(F32) + past).astype(BF)
            out_start(5, 0, i, k, gr.at[1, i, k], rgrad_out)

        m = 2 * s + i
        cols = rows_at(j * TC, TC, TC)
        hc = KC // 2
        copy(
            cg.at[i, j, rows_at(s * hc, hc, 8)], cgrad_out.at[m, :, cols], c_loc.at[0]
        ).start()
        rcopy(
            cg.at[i, j, rows_at((1 - s) * hc, hc, 8)],
            cgrad_out.at[m, :, cols],
            c_loc.at[1],
            c_loc.at[2],
            other,
        ).start()
        at(n, table)

    table4 = {
        1: [(1, 1, 1), (2, 1, 0)],
        2: [(1, 1, 2)],
        3: [(3, 1, 0), (2, 1, 1)],
        4: [(2, 1, 2)],
        5: [(4, 1, 0), (3, 1, 1)],
        6: [(3, 1, 2)],
        7: [(5, 1, 0), (4, 1, 1)],
    }

    @pl.loop(0, 2 * NJ)
    def _(n):
        back0(n, table4)

    weight_tasks(
        0,
        {0: [(4, 1, 2)], 1: [(0, 0, 0), (5, 1, 1)], 2: [(6, 1, 0)], 3: [(0, 0, 1), (5, 1, 2)]},
        {0: [(1, 0, 0), (6, 1, 1)], 1: [(0, 0, 2), (6, 1, 2)]},
    )

    tail = [
        (1, 0, 1),
        (2, 0, 0),
        (1, 0, 2),
        (2, 0, 1),
        (3, 0, 0),
        (2, 0, 2),
        (3, 0, 1),
        (4, 0, 0),
        (3, 0, 2),
        (4, 0, 1),
        (5, 0, 0),
        (4, 0, 2),
        (5, 0, 1),
        (6, 0, 0),
        (5, 0, 2),
        (6, 0, 1),
    ]
    for st, layer, p in tail:
        steps[st](layer, p)

    for i in range(2):
        for k in range(HJ):
            j = NJ - HJ + k

            @pl.when(has_next)
            def _():
                hb_copy(i, k).wait_recv()
                gr[1, i, j] = (gr[1, i, j].astype(F32) + hb[i, k].astype(F32)).astype(BF)

            out_start(5, 0, i, j, gr.at[1, i, j], rgrad_out)
    step6(0, 2)

    @pl.loop(0, 2 * NJ)
    def _(n):
        i, j = n // NJ, lax.rem(n, NJ)
        out_sent(0, 0, i, j, sk0.at[i, j], res_out)
        out_sent(4, 1, i, j, sk0.at[i, j], rgrad_out)
        out_sent(5, 0, i, j, sk0.at[i, j], rgrad_out)

        @pl.when(jnp.logical_or(j >= HJ, jnp.logical_not(has_prev)))
        def _():
            out_sent(3, 1, i, j, sk0.at[i, j], skip_out)

    out_arrived(0, 0, res_out)
    out_arrived(1, 0, skip_out)
    out_arrived(2, 1, res_out)
    out_arrived(3, 1, skip_out)
    out_arrived(4, 1, rgrad_out)
    out_arrived(5, 0, rgrad_out)
    half = cgrad_out.at[pl.ds(0, 2)]
    for k in range(3):
        copy(half, half, c_loc.at[k]).wait()
    for p in range(3):
        near, far = final_copies(0, p)

        near.wait()
        far.wait()

    @pl.when(has_next)
    def _():
        for i in range(2):
            for j in range(HJ):
                halo(i, j).wait_send()
            col_copy_f(i).wait_send()

    @pl.when(has_prev)
    def _():
        for i in range(2):
            col_copy_b(i).wait_send()
            for j in range(HJ):
                hb_copy(i, j).wait_send()


def local(nz, r, *args):
    audio, cond = args[0], args[1]
    M, _, C, TL = audio.shape
    KC = cond.shape[2]
    G = 2 * C
    NJ = TL // TC
    HJ = REACH0 // TC
    KP = G + PW
    parts = r * r * nz
    cr = max(C, 16 * parts)
    HR = 6 * G + cr
    any_ = pl.BlockSpec(memory_space=pl.ANY)
    smem = pl.BlockSpec(memory_space=pltpu.SMEM)
    V = pltpu.VMEM
    D = pltpu.SemaphoreType.DMA
    scratch = [
        V((2, G, KP), BF),
        V((2, G, C), BF),
        V((2, KP, G), BF),
        V((2, C, G), BF),
        V((2, G, KC), BF),
        V((2, 1, G), F32),
        V((2, 1, C), F32),
        V((2, 1, C), F32),
        V((2, G, PW), F32),
        V((2, 2, NJ, KP, TC), BF),
        V((2, 2, NJ, C, TC), BF),
        V((2, 2, NJ, G, TC), BF),
        V((2, 2, NJ, C, TC), BF),
        V((2, NJ, C, TC), BF),
        V((2, NJ, C, TC), BF),
        V((2 * NJ * C * (TC // PW), PW), BF),
        V((2, NJ, KC, TC), F32),
        V((TC, TC), BF),
        V((PW, TC), BF),
        V((2, 2, NJ, 8, TC), F32),
        V((2, 2, NJ, 16, TC), BF),
        V((2, C, PW), BF),
        V((2, C, PW), BF),
        V((2, 16, C), BF),
        V((2, 16, C), BF),
        V((2, 16, C), BF),
        V((2, 16, C), BF),
        V((2, HJ, C, TC), BF),
        V((3, HR, PW), BF),
        V((HR, PW), BF),
        V((2, r - 1, HR // r, PW), BF),
        V((2, r - 1, HR // (r * r), PW), BF),
        V((2, nz - 1, HR // parts, PW), BF),
        V((C, PW), F32),
        D((8,)),
        D((2, NJ)),
        D((2, NJ)),
        D((2, NJ)),
        D((2, NJ)),
        D((8,)),
        D((8,)),
        D((2, HJ)),
        D((2, HJ)),
        D((2,)),
        D((2,)),
        D((2,)),
        D((2,)),
        D((2, HJ)),
        D((2, HJ)),
        D((6, 2, NJ)),
        D((6, 2, NJ)),
        D((6,)),
        D((3,)),
        D((2, NJ, TC // PW)),
        D((2, NJ, TC // PW)),
        D((2, 3)),
        D((2, 3)),
        D((6, 2, 3)),
        D((6, 2, 3)),
        D((3,)),
        D((3,)),
        D((3,)),
        pltpu.SemaphoreType.REGULAR((3,)),
    ]
    res, skip, rgrad, cgrad, wg = pl.pallas_call(
        functools.partial(kernel, nz, r, cr),
        out_shape=(
            jax.ShapeDtypeStruct((M, C, TL), BF),
            jax.ShapeDtypeStruct((M, C, TL), BF),
            jax.ShapeDtypeStruct((M, C, TL), BF),
            jax.ShapeDtypeStruct((M, KC // 2, TL), F32),
            jax.ShapeDtypeStruct((2, HR, PW), BF),
        ),
        in_specs=[any_, any_, smem] + [any_] * 9,
        out_specs=(any_,) * 5,
        scratch_shapes=scratch,
        compiler_params=pltpu.CompilerParams(
            collective_id=0, has_side_effects=True, vmem_limit_bytes=64 * 2**20 - 2**17
        ),
        cost_estimate=pl.CostEstimate(
            flops=40 * 10**9, bytes_accessed=36 * 10**6, transcendentals=4 * 10**6
        ),
    )(*args)
    conv = jnp.transpose(wg[:, : 4 * G].reshape(2, 4, G, PW), (0, 2, 1, 3)).reshape(2, G, C)
    rs = jnp.transpose(wg[:, 4 * G : 6 * G].reshape(2, 2, G, PW), (2, 0, 1, 3)).reshape(G, C)
    cw = wg[:, 6 * G : 6 * G + C].reshape(G, PW)
    up = lambda v: v.astype(F32)[None]
    return (
        res[None, :, None],
        skip[None, :, None],
        rgrad.astype(F32)[None, :, None],
        cgrad[:, None],
        up(conv),
        up(cw[:, KC]),
        up(cw[:, :KC]),
        up(rs[:C]),
        up(cw[:C, KC + 3]),
        up(rs[C:]),
        up(cw[C:, KC + 3]),
    )


def solution(mesh):
    nz = mesh.shape["tm"]
    r = math.isqrt(mesh.shape["batch"])
    in_specs = (
        P(None, "batch", None, "tm"),
        P(None, "batch", None, "tm"),
        P(None, "batch", None),
        P("section", None, None, None),
        P("section", None),
        P("section", None, None),
        P("section", None, None),
        P("section", None),
        P("section", None, None),
        P("section", None),
        P(None, "batch", None, "tm"),
        P(None, "batch", None, "tm"),
    )
    out_specs = (
        P("section", None, "batch", None, "tm"),
        P("section", None, "batch", None, "tm"),
        P("section", None, "batch", None, "tm"),
        P(None, "batch", "section", "tm"),
        P("section", None, None, None),
        P("section", None),
        P("section", None, None),
        P("section", None, None),
        P("section", None),
        P("section", None, None),
        P("section", None),
    )
    return jax.shard_map(
        functools.partial(local, nz, r),
        mesh=mesh,
        in_specs=in_specs,
        out_specs=out_specs,
        check_vma=False,
    )
```

```python
import functools
import math

import jax
import jax.numpy as jnp
from jax import lax
from jax.experimental import pallas as pl
from jax.experimental.pallas import tpu as pltpu
from jax.sharding import PartitionSpec as P

REACH0 = 512
TC = 256
MESH = pl.DeviceIdType.MESH
BF = jnp.bfloat16
F32 = jnp.float32
PW = 128


T_W1A = {1: [(0, 1, 0)], 3: [(0, 1, 1)]}
T_W1B = {1: [(1, 1, 0), (0, 1, 2)]}
T_L1B = {3: [(2, 1, 0)], 7: [(1, 1, 2)]}
T_B0A = {0: [(3, 1, 0)], 1: [(2, 1, 2)]}
T_B0B = {0: [(3, 1, 1)]}
T_W0A = {1: [(0, 0, 0)], 3: [(0, 0, 1), (4, 1, 0)]}
T_W0B = {1: [(1, 0, 0), (0, 0, 2)]}
T_G0 = {1: [(1, 0, 1)], 3: [(5, 1, 0), (3, 1, 2)]}
T_RS = {1: [(2, 0, 0)], 7: [(1, 0, 2)]}
T_P1 = [(1, 1, 1)]
T_P0 = [(2, 1, 1)]
TAIL = [(2, 0, 1), (6, 1, 0), (2, 0, 2), (4, 1, 1), (5, 1, 1), (4, 1, 2), (3, 0, 0), (6, 1, 1), (3, 0, 1), (5, 1, 2), (3, 0, 2), (6, 1, 2), (4, 0, 0), (4, 0, 1), (5, 0, 0), (5, 0, 1), (4, 0, 2), (6, 0, 0)]
LAST = [(6, 0, 1), (5, 0, 2), (6, 0, 2)]


def dot(a, b):
    return jnp.dot(a, b, preferred_element_type=F32)


def dot_nt(a, b):
    return lax.dot_general(a, b, (((1,), (1,)), ((), ())), preferred_element_type=F32)


def rows_at(start, size, step):
    return pl.ds(pl.multiple_of(start, step), size)


def kernel(
    nz,
    r,
    cr,
    audio,
    cond,
    clips,
    convw,
    convb,
    condw,
    resw,
    resb,
    skipw,
    skipb,
    cotr,
    cots,
    res_out,
    skip_out,
    rgrad_out,
    cgrad_out,
    wg_out,
    wcat,
    wrs,
    wct,
    wrst,
    cbraw,
    rbraw,
    sbraw,
    rsbias,
    rh,
    hid,
    gb,
    gr,
    cs,
    ag1,
    cg,
    eye,
    bsum,
    mkf,
    mkb,
    htile,
    bcar,
    colf_s,
    colf_r,
    colb_s,
    colb_r,
    hs,
    hb,
    pb,
    prv,
    ra_buf,
    rb_buf,
    rz_buf,
    cacc,
    ld_w,
    ld_x,
    ld_c,
    ld_r,
    ld_s,
    w_snd,
    w_rcv,
    h_snd,
    h_rcv,
    cf_snd,
    cf_rcv,
    cb_snd,
    cb_rcv,
    hb_snd,
    hb_rcv,
    o_loc,
    o_snd,
    o_rcv,
    c_loc,
    x_snd,
    x_rcv,
    ar_snd,
    ar_rcv,
    f_loc,
    f_snd,
    f_rcv,
    credit,
):
    C = audio.shape[2]
    TL = audio.shape[3]
    KC = cond.shape[2]
    NJ = TL // TC
    HJ = REACH0 // TC
    G = 2 * C
    KP = rh.shape[3]
    HR = pb.shape[1]
    s = lax.axis_index("section")
    b = lax.axis_index("batch")
    z = lax.axis_index("tm")
    other = (1 - s, b, z)
    zprev = (s, b, z - 1)
    znext = (s, b, z + 1)
    has_prev = z > 0
    has_next = z < nz - 1

    def copy(src, dst, sem):
        return pltpu.make_async_copy(src, dst, sem)

    def rcopy(src, dst, ssem, rsem, dev):
        return pltpu.make_async_remote_copy(
            src_ref=src, dst_ref=dst, send_sem=ssem, recv_sem=rsem, device_id=dev, device_id_type=MESH
        )

    def weight_pairs(layer):
        return [
            (convw.at[0, 0], wcat.at[layer, :, pl.ds(0, C)]),
            (convw.at[0, 1], wcat.at[layer, :, pl.ds(C, C)]),
            (resw.at[0], wrs.at[layer, pl.ds(0, C)]),
            (skipw.at[0], wrs.at[layer, pl.ds(C, C)]),
            (condw.at[0], wct.at[layer, pl.ds(G, KC)]),
            (convb, cbraw.at[layer]),
            (resb, rbraw.at[layer]),
            (skipb, sbraw.at[layer]),
        ]

    own_w = [copy(a, d, ld_w.at[k]) for k, (a, d) in enumerate(weight_pairs(s))]
    for c in own_w:
        c.start()
    ldx, ldc, ldr, lds = [], [], [], []
    for i in range(2):
        for j in reversed(range(NJ)):
            cols = pl.ds(j * TC, TC)
            m = 2 * s + i
            ldx.append(copy(audio.at[m, 0, :, cols], rh.at[0, i, j, pl.ds(C, C)], ld_x.at[i, j]))
            ldc.append(copy(cond.at[m, 0, :, cols], rh.at[0, i, j, pl.ds(G, KC)], ld_c.at[i, j]))
            ldr.append(copy(cotr.at[m, 0, :, cols], gr.at[1, i, j], ld_r.at[i, j]))
            lds.append(copy(cots.at[m, 0, :, cols], cs.at[i, j], ld_s.at[i, j]))
    for c in ldx + ldc + ldr + lds:
        c.start()

    bar = pltpu.get_barrier_semaphore()

    def sa_dev(o):
        a2 = lax.rem(amem + o, r)
        return a2, (s, jnp.where(s == 0, bhi * r + a2, a2 * r + blo), z)

    def sb_dev(o):
        b2 = lax.rem(bmem + o, r)
        return b2, (s, jnp.where(s == 0, b2 * r + blo, bhi * r + b2), z)

    def sz_dev(o):
        z2 = lax.rem(z + o, nz)
        return z2, (s, b, z2)

    bhi = b // r
    blo = lax.rem(b, r)
    amem = jnp.where(s == 0, blo, bhi)
    bmem = jnp.where(s == 0, bhi, blo)
    peers = [other]
    peers += [sa_dev(o)[1] for o in range(1, r)]
    peers += [sb_dev(o)[1] for o in range(1, r)]
    peers += [sz_dev(o)[1] for o in range(1, nz)]
    for dev in peers:
        pl.semaphore_signal(bar, inc=1, device_id=dev, device_id_type=MESH)

    ri = lax.broadcasted_iota(jnp.int32, (TC, TC), 0)
    ci = lax.broadcasted_iota(jnp.int32, (TC, TC), 1)
    eye[...] = (ri == ci).astype(F32).astype(BF)
    bsum[...] = jnp.zeros(bsum.shape, F32)
    bcar[...] = jnp.zeros(bcar.shape, BF)
    rk = lax.broadcasted_iota(jnp.int32, (KP - G - KC, TC), 0)
    ones_rows = (rk < 3).astype(F32).astype(BF)
    for i in range(2):
        m = 2 * s + i
        for j in range(NJ):
            rh[0, i, j, pl.ds(G + KC, KP - G - KC), :] = ones_rows
            rh[1, i, j, pl.ds(G + KC, KP - G - KC), :] = ones_rows
            pos = z * TL + j * TC + lax.broadcasted_iota(jnp.int32, (16, TC), 1)
            start = jnp.zeros((16, TC), jnp.int32)
            end = jnp.int32(0)
            for k in range(clips.shape[2]):
                end = end + clips[m, 0, k]
                start = jnp.where(end <= pos, end, start)
            for layer, reach in ((0, REACH0), (1, 1)):
                keep = jnp.where(pos - reach >= start, 1.0, 0.0).astype(F32)
                mkf[layer, i, j] = keep[:8]
                mkb[layer, i, j] = keep.astype(BF)

    @pl.when(jnp.logical_not(has_prev))
    def _():
        for i in range(2):
            for j in range(HJ):
                rh[0, i, j, pl.ds(0, C), :] = jnp.zeros((C, TC), BF)
            htile[i] = jnp.zeros((C, PW), BF)

    pl.semaphore_wait(bar, len(peers))

    far_w = [
        rcopy(a, d, w_snd.at[k], w_rcv.at[k], other) for k, (a, d) in enumerate(weight_pairs(s))
    ]
    for c in far_w:
        c.start()

    def halo(i, j):
        return rcopy(
            audio.at[2 * s + i, 0, :, rows_at(TL - REACH0 + j * TC, TC, TC)],
            rh.at[0, i, j, pl.ds(0, C)],
            h_snd.at[i, j],
            h_rcv.at[i, j],
            znext,
        )

    def halo_start(i):
        @pl.when(has_next)
        def _():
            for j in reversed(range(HJ)):
                halo(i, j).start()

    halo_start(0)

    tail_rows = KP - G - KC

    def prepare_forward(layer):
        row = lax.broadcasted_iota(jnp.int32, (tail_rows, G), 0)
        bias = jnp.broadcast_to(cbraw[layer], (tail_rows, G))
        hi = bias.astype(BF).astype(F32)
        mid = (bias - hi).astype(BF).astype(F32)
        low = (bias - hi) - mid
        part = jnp.where(row == 0, hi, jnp.where(row == 1, mid, jnp.where(row == 2, low, 0.0)))
        wct[layer, pl.ds(G + KC, tail_rows), :] = part.astype(BF)
        for k in range(G // TC):
            wcat[layer, pl.ds(k * TC, TC), pl.ds(G, PW)] = dot_nt(
                eye[...], wct[layer, pl.ds(G, PW), pl.ds(k * TC, TC)]
            ).astype(BF)
        rsbias[layer, pl.ds(0, C)] = jnp.broadcast_to(rbraw[layer], (PW, C)).T
        rsbias[layer, pl.ds(C, C)] = jnp.broadcast_to(sbraw[layer], (PW, C)).T

    def prepare_mix(layer):
        @pl.loop(0, C // TC)
        def _(k):
            cols = rows_at(k * TC, TC, TC)
            wrst[layer, cols, :] = dot_nt(eye[...], wrs[layer, :, cols]).astype(BF)

    def prepare_conv(layer):
        @pl.loop(0, G // TC)
        def _(k):
            cols = rows_at(k * TC, TC, TC)
            wct[layer, cols, :] = dot_nt(eye[...], wcat[layer, :, cols]).astype(BF)

    def phase_ready():
        for c in own_w:
            c.wait()

        @pl.when(s == 1)
        def _():
            prepare_forward(1)
            prepare_mix(1)
            for c in far_w:
                c.wait_recv()

        prepare_forward(0)

    phase_ready()
    for c in ldx + ldc:
        c.wait()

    def wide(tile):
        return jnp.concatenate([tile, tile], axis=1)

    def gate(layer, i, j):
        xx = rh[layer, i, j]
        out = []
        for g in range(2):
            lo = pl.ds(g * TC, TC)
            hi = pl.ds(C + g * TC, TC)
            t = jnp.tanh(dot(wcat[layer, lo, :], xx))
            q = 0.5 * jnp.tanh(0.5 * dot(wcat[layer, hi, :], xx)) + 0.5
            h = t * q
            hid[layer, i, j, lo, :] = h.astype(BF)
            out.append((q - h * t, h - h * q))
        return out

    def out_copy(kind, layer, i, j, src, dst):
        m = 2 * s + i
        return (
            copy(src, dst.at[m, :, rows_at(j * TC, TC, TC)], o_loc.at[kind, i, j]),
            rcopy(
                src,
                dst.at[m, :, rows_at(j * TC, TC, TC)],
                o_snd.at[kind, i, j],
                o_rcv.at[kind],
                other,
            ),
        )

    def out_start(kind, layer, i, j, src, dst):
        near, far = out_copy(kind, layer, i, j, src, dst)
        start_either(layer, near, far)

    def start_either(layer, near, far):
        @pl.when(s == layer)
        def _():
            near.start()

        @pl.when(s != layer)
        def _():
            far.start()

    def out_sent(kind, layer, i, j, src, dst):
        near, far = out_copy(kind, layer, i, j, src, dst)

        @pl.when(s == layer)
        def _():
            near.wait()

        @pl.when(s != layer)
        def _():
            far.wait_send()

    def out_arrived(kind, layer, dst):
        half = dst.at[pl.ds(0, 2)]

        @pl.when(s == layer)
        def _():
            copy(half, half, o_rcv.at[kind]).wait()

    def col_copy_f(i):
        return rcopy(colf_s.at[i], colf_r.at[i], cf_snd.at[i], cf_rcv.at[i], znext)

    def col_copy_b(i):
        return rcopy(colb_s.at[i], colb_r.at[i], cb_snd.at[i], cb_rcv.at[i], zprev)

    def pick_col(tile, lane):
        li = lax.broadcasted_iota(jnp.int32, (16, PW), 1)
        return dot_nt((li == lane).astype(F32).astype(BF), tile).astype(BF)

    def spread_col(rows):
        full = jnp.concatenate([rows] * (PW // 16), axis=0)
        parts = [
            dot_nt(eye[...], full[:, k * TC : (k + 1) * TC]) for k in range(C // TC)
        ]
        return jnp.concatenate(parts, axis=0)

    def fwd0(i, j):
        far = j >= HJ
        src_j = jnp.where(far, j - HJ, j)
        src_row = jnp.where(far, C, 0)
        mask = jnp.concatenate([mkb[0, i, j]] * (C // 16), axis=0)
        rh[0, i, j, pl.ds(0, C), :] = rh[0, i, src_j, rows_at(src_row, C, C), :] * mask
        parts = gate(0, i, j)
        for g in range(2):
            gb[0, i, j, pl.ds(g * TC, TC), :] = parts[g][0].astype(BF)
            gb[0, i, j, pl.ds(C + g * TC, TC), :] = parts[g][1].astype(BF)
        rs = dot(wrs[0, pl.ds(0, C)], hid[0, i, j]) + wide(rsbias[0, pl.ds(0, C)])
        x1 = (rh[0, i, j, pl.ds(C, C), :].astype(F32) + rs).astype(BF)
        rh[1, i, j, pl.ds(C, C), :] = x1
        rh[1, i, j, pl.ds(G, KC), :] = rh[0, i, j, pl.ds(G, KC), :]
        out_start(0, 0, i, j, rh.at[1, i, j, pl.ds(C, C)], res_out)

        @pl.when(jnp.logical_and(j == NJ - 1, has_next))
        def _():
            colf_s[i] = pick_col(rh[1, i, j, pl.ds(C, C), pl.ds(TC - PW, PW)], PW - 1)
            col_copy_f(i).start()

    lane_c = lax.broadcasted_iota(jnp.int32, (C, PW), 1)

    def add_sum(which, block):
        total = bsum[which]
        for k in range(TC // PW):
            total = total + block[:, k * PW : (k + 1) * PW].astype(F32)
        bsum[which] = total

    def layer1(i, j):
        x1 = rh[1, i, j, pl.ds(C, C), :].astype(F32)
        jm = jnp.maximum(j - 1, 0)
        tile = rh[1, i, jm, pl.ds(C, C), pl.ds(TC - PW, PW)].astype(F32)
        tile = jnp.where(j == 0, htile[i].astype(F32), tile)
        turned = pltpu.roll(x1, 1, 1)
        first = jnp.where(lane_c == 0, pltpu.roll(tile, 1, 1), turned[:, :PW])
        shifted = jnp.concatenate([first, turned[:, PW:]], axis=1) * mkf[1, i, j, pl.ds(0, 1), :]
        rh[1, i, j, pl.ds(0, C), :] = shifted.astype(BF)
        gh = dot(wrst[1], jnp.concatenate([gr[1, i, j], cs[i, j]], axis=0))
        add_sum(0, gr[1, i, j])
        add_sum(1, cs[i, j])
        parts = gate(1, i, j)
        for g in range(2):
            part = gh[g * TC : (g + 1) * TC]
            gb[1, i, j, pl.ds(g * TC, TC), :] = (part * parts[g][0]).astype(BF)
            gb[1, i, j, pl.ds(C + g * TC, TC), :] = (part * parts[g][1]).astype(BF)

    def layer1_back(i, j):
        dg = dot(wct[1], gb[1, i, j])
        past = dg[:C] * mkf[1, i, j, pl.ds(0, 1), :]
        turned = pltpu.roll(past, TC - 1, 1)
        last = jnp.where(lane_c == PW - 1, pltpu.roll(bcar[i].astype(F32), PW - 1, 1), turned[:, TC - PW :])
        back = jnp.concatenate([turned[:, : TC - PW], last], axis=1)
        gres = (gr[1, i, j].astype(F32) + dg[C:G] + back).astype(BF)
        gr[0, i, j] = gres
        add_sum(2, gres)
        bcar[i] = past[:, :PW].astype(BF)
        cg[i, j] = dg[G : G + KC]

        @pl.when(jnp.logical_and(j == 0, has_prev))
        def _():
            colb_s[i] = pick_col(past[:, :PW].astype(BF), 0)
            col_copy_b(i).start()

    def phase_near():
        @pl.loop(0, 2 * (NJ - HJ))
        def _(n):
            fwd0(n // (NJ - HJ), NJ - 1 - lax.rem(n, NJ - HJ))

    phase_near()
    halo_start(1)

    @pl.when(s == 0)
    def _():
        for c in far_w:
            c.wait_recv()
        prepare_forward(1)
        prepare_mix(1)

    for c in ldr + lds:
        c.wait()

    def phase_main():
        @pl.loop(0, 2 * NJ)
        def _(n):
            q = n - 2
            i = jnp.where(n < 2, n, q // (NJ - 1))
            j = jnp.where(n < 2, NJ - 1, NJ - 2 - lax.rem(q, NJ - 1))

            @pl.when(jnp.logical_and(n >= 2, j >= 1))
            def _():
                @pl.when(jnp.logical_and(has_prev, j <= HJ))
                def _():
                    halo(i, j - 1).wait_recv()

                fwd0(i, j - 1)

            @pl.when(jnp.logical_and(j == 0, has_prev))
            def _():
                col_copy_f(i).wait_recv()
                htile[i] = spread_col(colf_r[i]).astype(BF)

            layer1(i, j)

    phase_main()

    offs = [0, 2 * G, 4 * G]
    sizes = [2 * G, 2 * G, 2 * G + cr]
    ARA, ARB, ARZ, AGZ, AGB, AGA = range(6)

    def geo(p):
        size, off = sizes[p], offs[p]
        na, nb_, nzr = size // r, size // (r * r), size // (r * r * nz)
        base_a = off + amem * na
        base_b = base_a + bmem * nb_
        base_z = base_b + z * nzr
        return size, off, na, nb_, nzr, base_a, base_b, base_z

    def x_copy(layer, p):
        return rcopy(
            pb.at[0, pl.ds(offs[p], sizes[p])],
            prv.at[pl.ds(offs[p], sizes[p])],
            x_snd.at[layer, p],
            x_rcv.at[layer, p],
            other,
        )

    def gathered(layer, rows):
        return ag1.at[rows] if layer == 1 else pb.at[0, rows]

    def wait_rows(count, sem, layer):
        ref = pb.at[1 + layer, pl.ds(0, count)]
        copy(ref, ref, sem).wait()

    def sum_rows(layer, start, count, parts):
        total = pb[1 + layer, rows_at(start, count, 16), :].astype(F32)
        for part in parts:
            total = total + part.astype(F32)
        return total.astype(BF)

    def add_rows(layer, start, count, parts):
        pb[1 + layer, rows_at(start, count, 16), :] = sum_rows(layer, start, count, parts)

    def step0(layer, p):
        size, off, na, nb_, nzr, base_a, base_b, base_z = geo(p)
        x_copy(layer, p).wait()
        add_rows(layer, off, size, [prv[pl.ds(off, size), :]])
        if layer == 1:
            pl.semaphore_signal(credit.at[p], inc=1, device_id=other, device_id_type=MESH)
        for o in range(1, r):
            a2, dev = sa_dev(o)
            rcopy(
                pb.at[1 + layer, rows_at(off + a2 * na, na, 16)],
                ra_buf.at[layer, o - 1, pl.ds(off // r, na)],
                ar_snd.at[ARA, layer, p],
                ar_rcv.at[ARA, layer, p],
                dev,
            ).start()

    def step1(layer, p):
        size, off, na, nb_, nzr, base_a, base_b, base_z = geo(p)
        wait_rows((r - 1) * na, ar_rcv.at[ARA, layer, p], layer)
        wait_rows((r - 1) * na, ar_snd.at[ARA, layer, p], layer)
        add_rows(
            layer, base_a, na, [ra_buf[layer, o, pl.ds(off // r, na), :] for o in range(r - 1)]
        )
        for o in range(1, r):
            b2, dev = sb_dev(o)
            rcopy(
                pb.at[1 + layer, rows_at(base_a + b2 * nb_, nb_, 16)],
                rb_buf.at[layer, o - 1, pl.ds(off // (r * r), nb_)],
                ar_snd.at[ARB, layer, p],
                ar_rcv.at[ARB, layer, p],
                dev,
            ).start()

    def step2(layer, p):
        size, off, na, nb_, nzr, base_a, base_b, base_z = geo(p)
        wait_rows((r - 1) * nb_, ar_rcv.at[ARB, layer, p], layer)
        wait_rows((r - 1) * nb_, ar_snd.at[ARB, layer, p], layer)
        add_rows(
            layer,
            base_b,
            nb_,
            [rb_buf[layer, o, pl.ds(off // (r * r), nb_), :] for o in range(r - 1)],
        )
        for o in range(1, nz):
            z2, dev = sz_dev(o)
            rcopy(
                pb.at[1 + layer, rows_at(base_b + z2 * nzr, nzr, 16)],
                rz_buf.at[layer, o - 1, pl.ds(off // (r * r * nz), nzr)],
                ar_snd.at[ARZ, layer, p],
                ar_rcv.at[ARZ, layer, p],
                dev,
            ).start()

    def spread(layer, p, stage, start, count, devs):
        for dev in devs:
            rcopy(
                gathered(layer, rows_at(start, count, 16)),
                gathered(layer, rows_at(start, count, 16)),
                ar_snd.at[stage, layer, p],
                ar_rcv.at[stage, layer, p],
                dev,
            ).start()

    def step3(layer, p):
        size, off, na, nb_, nzr, base_a, base_b, base_z = geo(p)
        wait_rows((nz - 1) * nzr, ar_rcv.at[ARZ, layer, p], layer)
        wait_rows((nz - 1) * nzr, ar_snd.at[ARZ, layer, p], layer)
        gathered(layer, rows_at(base_z, nzr, 16))[...] = sum_rows(
            layer,
            base_z,
            nzr,
            [rz_buf[layer, o, pl.ds(off // (r * r * nz), nzr), :] for o in range(nz - 1)],
        )
        spread(layer, p, AGZ, base_z, nzr, [sz_dev(o)[1] for o in range(1, nz)])

    def step4(layer, p):
        size, off, na, nb_, nzr, base_a, base_b, base_z = geo(p)
        wait_rows((nz - 1) * nzr, ar_rcv.at[AGZ, layer, p], layer)
        wait_rows((nz - 1) * nzr, ar_snd.at[AGZ, layer, p], layer)
        spread(layer, p, AGB, base_b, nb_, [sb_dev(o)[1] for o in range(1, r)])

    def step5(layer, p):
        size, off, na, nb_, nzr, base_a, base_b, base_z = geo(p)
        wait_rows((r - 1) * nb_, ar_rcv.at[AGB, layer, p], layer)
        wait_rows((r - 1) * nb_, ar_snd.at[AGB, layer, p], layer)
        spread(layer, p, AGA, base_a, na, [sa_dev(o)[1] for o in range(1, r)])

    def final_copies(layer, p):
        src = gathered(layer, pl.ds(offs[p], sizes[p]))
        dst = wg_out.at[s, pl.ds(offs[p], sizes[p])]
        return (
            copy(src, dst, f_loc.at[p]),
            rcopy(src, dst, f_snd.at[p], f_rcv.at[p], other),
        )

    def step6(layer, p):
        size, off, na, nb_, nzr, base_a, base_b, base_z = geo(p)
        wait_rows((r - 1) * na, ar_rcv.at[AGA, layer, p], layer)
        wait_rows((r - 1) * na, ar_snd.at[AGA, layer, p], layer)
        near, far = final_copies(layer, p)

        @pl.when(s == layer)
        def _():
            near.start()

        @pl.when(s != layer)
        def _():
            far.start()

    steps = [step0, step1, step2, step3, step4, step5, step6]

    def at(n, table):
        for k, todo in table.items():

            @pl.when(n == k)
            def _(todo=todo):
                for st, layer, p in todo:
                    steps[st](layer, p)

    def weight_tasks(layer, table_a, table_b):
        @pl.loop(0, 4)
        def _(n):
            p = n // 2
            mine = lax.rem(n, 2)
            half = jnp.where(mine == 1, s, 1 - s)
            dst = mine * (1 + layer)
            if layer == 0:

                @pl.when(mine == 0)
                def _():
                    pl.semaphore_wait(credit.at[p], 1)

            ch = rows_at(half * C + p * TC, TC, TC)
            total = dot_nt(gb[layer, 0, 0], rh[layer, 0, 0, ch, :])
            for i in range(2):
                for j in range(NJ):
                    if i + j > 0:
                        total = total + dot_nt(gb[layer, i, j], rh[layer, i, j, ch, :])
            total = total.astype(BF)
            pb[dst, rows_at(p * 2 * G, G, G), :] = total[:, :PW]
            pb[dst, rows_at(p * 2 * G + G, G, G), :] = total[:, PW:]
            for pp in range(2):

                @pl.when(n == 2 * pp)
                def _():
                    x_copy(layer, pp).start()

            at(n, table_a)

        @pl.loop(0, 2)
        def _(n):
            half = jnp.where(n == 1, s, 1 - s)
            dst = n * (1 + layer)
            if layer == 0:

                @pl.when(n == 0)
                def _():
                    pl.semaphore_wait(credit.at[2], 1)

            ch = rows_at(half * TC, TC, TC)
            for src, row in ((lambda i, j: gr[layer, i, j], 0), (lambda i, j: cs[i, j], C)):
                total = dot_nt(src(0, 0), hid[layer, 0, 0, ch, :])
                for i in range(2):
                    for j in range(NJ):
                        if i + j > 0:
                            total = total + dot_nt(src(i, j), hid[layer, i, j, ch, :])
                total = total.astype(BF)
                pb[dst, pl.ds(4 * G + row, C), :] = total[:, :PW]
                pb[dst, pl.ds(5 * G + row, C), :] = total[:, PW:]
            gp_rows = rows_at(half * C, C, C)
            total = jnp.zeros((PW, C), F32)
            for i in range(2):
                for j in range(NJ):
                    total = total + dot_nt(
                        rh[layer, i, j, pl.ds(G, PW), :], gb[layer, i, j, gp_rows, :]
                    )
            cacc[...] = total
            which = jnp.where(half == 1, 1, 2 - 2 * layer)
            cacc[pl.ds(KC + 3, 1), :] = jnp.sum(bsum[which].T, axis=0, keepdims=True)
            for k in range(C // PW):
                pb[dst, pl.ds(6 * G + k * PW, PW), :] = cacc[:, k * PW : (k + 1) * PW].astype(BF)
            if cr > C:
                pb[dst, pl.ds(6 * G + C, cr - C), :] = jnp.zeros((cr - C, PW), BF)

            @pl.when(n == 0)
            def _():
                x_copy(layer, 2).start()

            at(n, table_b)

    def fix_last(i):
        @pl.when(has_next)
        def _():
            col_copy_b(i).wait_recv()
            tile = gr[0, i, NJ - 1, :, pl.ds(TC - PW, PW)].astype(F32)
            add = jnp.where(lane_c == PW - 1, spread_col(colb_r[i]), 0.0)
            bsum[2] = bsum[2] + add
            gr[0, i, NJ - 1, :, pl.ds(TC - PW, PW)] = (tile + add).astype(BF)

    def phase_w1():
        weight_tasks(1, T_W1A, T_W1B)

    phase_w1()

    def run_steps(todo):
        for st, layer, p in todo:
            steps[st](layer, p)

    def phase_l1b():
        prepare_conv(1)
        run_steps(T_P1)

        @pl.loop(0, 2 * NJ)
        def _(n):
            layer1_back(n // NJ, NJ - 1 - lax.rem(n, NJ))
            at(n, T_L1B)

        prepare_mix(0)
        prepare_conv(0)
        run_steps(T_P0)

    phase_l1b()

    def hb_copy(i, j):
        return rcopy(hs.at[i, j], hb.at[i, j], hb_snd.at[i, j], hb_rcv.at[i, j], zprev)

    def back0(i, j):
        gh = dot(wrst[0], jnp.concatenate([gr[0, i, j], cs[i, j]], axis=0))
        for g in range(2):
            part = gh[g * TC : (g + 1) * TC]
            for row in (g * TC, C + g * TC):
                rows = pl.ds(row, TC)
                gb[0, i, j, rows, :] = (part * gb[0, i, j, rows, :].astype(F32)).astype(BF)

    def grad0(i, j):
        dg = dot(wct[0], gb[0, i, j])
        past = dg[:C] * mkf[0, i, j, pl.ds(0, 1), :]
        gr[1, i, j] = (gr[0, i, j].astype(F32) + dg[C:G]).astype(BF)
        cg[i, j] = cg[i, j] + dg[G : G + KC]
        m = 2 * s + i
        cols = rows_at(j * TC, TC, TC)
        hc = KC // 2
        copy(
            cg.at[i, j, rows_at(s * hc, hc, 8)], cgrad_out.at[m, :, cols], c_loc.at[0]
        ).start()
        rcopy(
            cg.at[i, j, rows_at((1 - s) * hc, hc, 8)],
            cgrad_out.at[m, :, cols],
            c_loc.at[1],
            c_loc.at[2],
            other,
        ).start()
        return past

    def phase_b0a():
        @pl.loop(0, 2 * HJ)
        def _(n):
            i, j = n // HJ, lax.rem(n, HJ)
            back0(i, j)
            past = grad0(i, j)

            @pl.when(has_prev)
            def _():
                hs[i, j] = past.astype(BF)
                hb_copy(i, j).start()

            at(n, T_B0A)

    phase_b0a()

    for i in range(2):
        fix_last(i)
        for j in range(NJ):
            out_start(4, 1, i, j, gr.at[0, i, j], rgrad_out)

    def phase_b0b():
        @pl.loop(0, 2 * (NJ - HJ))
        def _(n):
            back0(n // (NJ - HJ), HJ + lax.rem(n, NJ - HJ))
            at(n, T_B0B)

    phase_b0b()

    def phase_w0():
        weight_tasks(0, T_W0A, T_W0B)

    phase_w0()

    def phase_g0():
        @pl.loop(0, 2 * (NJ - HJ))
        def _(n):
            i, k = n // (NJ - HJ), lax.rem(n, NJ - HJ)
            past = grad0(i, HJ + k)
            gr[1, i, k] = (gr[1, i, k].astype(F32) + past).astype(BF)
            out_start(5, 0, i, k, gr.at[1, i, k], rgrad_out)
            at(n, T_G0)

    phase_g0()

    def phase_rs():
        @pl.loop(0, 2 * NJ)
        def _(n):
            i, j = n // NJ, lax.rem(n, NJ)
            x1 = rh.at[1, i, j, pl.ds(C, C)]
            sk0 = rh.at[1, i, j, pl.ds(0, C)]
            sk1 = hid.at[1, i, j]
            skip = dot(wrs[0, pl.ds(C, C)], hid[0, i, j]) + wide(rsbias[0, pl.ds(C, C)])
            skip = skip.astype(BF)
            sk0[...] = skip
            out_start(1, 0, i, j, sk0, skip_out)
            rs = dot(wrs[1], sk1[...]) + wide(rsbias[1])
            sk1[...] = (skip.astype(F32) + rs[C:]).astype(BF)
            out_start(3, 1, i, j, sk1, skip_out)
            out_sent(0, 0, i, j, x1, res_out)
            x1[...] = (x1[...].astype(F32) + rs[:C]).astype(BF)
            out_start(2, 1, i, j, x1, res_out)
            at(n, T_RS)

    phase_rs()

    def phase_tail():
        run_steps(TAIL)

    phase_tail()

    for i in range(2):
        for k in range(HJ):
            j = NJ - HJ + k

            @pl.when(has_next)
            def _():
                hb_copy(i, k).wait_recv()
                gr[1, i, j] = (gr[1, i, j].astype(F32) + hb[i, k].astype(F32)).astype(BF)

            out_start(5, 0, i, j, gr.at[1, i, j], rgrad_out)

    def phase_last():
        run_steps(LAST)

    phase_last()

    @pl.loop(0, 2 * NJ)
    def _(n):
        i, j = n // NJ, lax.rem(n, NJ)
        blk = gr.at[0, i, j]
        out_sent(1, 0, i, j, blk, skip_out)
        out_sent(2, 1, i, j, blk, res_out)
        out_sent(3, 1, i, j, blk, skip_out)
        out_sent(4, 1, i, j, blk, rgrad_out)
        out_sent(5, 0, i, j, blk, rgrad_out)

    out_arrived(0, 0, res_out)
    out_arrived(1, 0, skip_out)
    out_arrived(2, 1, res_out)
    out_arrived(3, 1, skip_out)
    out_arrived(4, 1, rgrad_out)
    out_arrived(5, 0, rgrad_out)
    half = cgrad_out.at[pl.ds(0, 2)]
    for k in range(3):
        copy(half, half, c_loc.at[k]).wait()
    for p in range(3):
        near, far = final_copies(0, p)
        near.wait()
        far.wait()
    for c in far_w:
        c.wait_send()

    @pl.when(has_next)
    def _():
        for i in range(2):
            for j in range(HJ):
                halo(i, j).wait_send()
            col_copy_f(i).wait_send()

    @pl.when(has_prev)
    def _():
        for i in range(2):
            col_copy_b(i).wait_send()
            for j in range(HJ):
                hb_copy(i, j).wait_send()


def finalize(
    res, skip, rgrad, cgrad, wg,
    res_o, skip_o, rgrad_o, cgrad_o, conv_o, convb_o, condw_o, resw_o, resb_o, skipw_o, skipb_o,
    rbuf, sbuf, cbuf, rin, rwide, win, convf, mixf, condf, cbf, rbf, sbf, sem_in, sem_cp, sem_out,
):
    M, C, TL = res.shape
    G = 2 * C
    KC = condw_o.shape[0]
    copies = []
    loads = [pltpu.make_async_copy(wg.at[h], win.at[h], sem_in.at[h]) for h in range(2)]
    reads = [pltpu.make_async_copy(rgrad.at[m], rin.at[m], sem_in.at[2 + m]) for m in range(M)]
    for c in loads + reads:
        c.start()
    passing = []
    for k, (a, buf, o) in enumerate(
        ((res, rbuf, res_o), (skip, sbuf, skip_o), (cgrad, cbuf, cgrad_o))
    ):
        for m in range(M):
            c = pltpu.make_async_copy(a.at[m], buf.at[m], sem_cp.at[k, m])
            c.start()
            passing.append((c, buf.at[m], o.at[m], 8 + M + k * M + m))

    def put(src, dst, k):
        c = pltpu.make_async_copy(src, dst, sem_out.at[k])
        c.start()
        copies.append(c)

    for h in range(2):
        loads[h].wait()
        for q in range(C // PW):
            convf[h, :, q * PW : (q + 1) * PW] = win[h, pl.ds(q * G, G), :].astype(F32)
        put(convf.at[h], conv_o.at[h], h)
        for q in range(2):
            lanes = slice(h * 2 * PW + q * PW, h * 2 * PW + (q + 1) * PW)
            mixf[:, lanes] = win[h, pl.ds((4 + q) * G, G), :].astype(F32)
        for q in range(C // PW):
            blk = win[h, pl.ds(6 * G + q * PW, PW), :].astype(F32)
            lanes = slice(h * C + q * PW, h * C + (q + 1) * PW)
            condf[:, lanes] = blk[:KC]
            cbf[:, lanes] = blk[KC : KC + 1]
            (sbf if h else rbf)[:, q * PW : (q + 1) * PW] = blk[KC + 3 : KC + 4]
    put(mixf.at[pl.ds(0, C)], resw_o, 2)
    put(mixf.at[pl.ds(C, C)], skipw_o, 3)
    put(condf, condw_o, 4)
    put(cbf, convb_o, 5)
    put(rbf, resb_o, 6)
    put(sbf, skipb_o, 7)
    for c, src, dst, k in passing:
        c.wait()
        put(src, dst, k)
    for m in range(M):
        reads[m].wait()
        rwide[m] = rin[m].astype(F32)
        put(rwide.at[m], rgrad_o.at[m], 8 + m)
    for c in copies:
        c.wait()


def local(nz, r, *args):
    audio, cond = args[0], args[1]
    M, _, C, TL = audio.shape
    KC = cond.shape[2]
    G = 2 * C
    NJ = TL // TC
    HJ = REACH0 // TC
    KP = G + PW
    parts = r * r * nz
    cr = max(C, 16 * parts)
    HR = 6 * G + cr
    any_ = pl.BlockSpec(memory_space=pl.ANY)
    smem = pl.BlockSpec(memory_space=pltpu.SMEM)
    V = pltpu.VMEM
    D = pltpu.SemaphoreType.DMA
    scratch = [
        V((2, G, KP), BF),
        V((2, G, C), BF),
        V((2, KP, G), BF),
        V((2, C, G), BF),
        V((2, 1, G), F32),
        V((2, 1, C), F32),
        V((2, 1, C), F32),
        V((2, G, PW), F32),
        V((2, 2, NJ, KP, TC), BF),
        V((2, 2, NJ, C, TC), BF),
        V((2, 2, NJ, G, TC), BF),
        V((2, 2, NJ, C, TC), BF),
        V((2, NJ, C, TC), BF),
        V((HR, PW), BF),
        V((2, NJ, KC, TC), F32),
        V((TC, TC), BF),
        V((3, C, PW), F32),
        V((2, 2, NJ, 8, TC), F32),
        V((2, 2, NJ, 16, TC), BF),
        V((2, C, PW), BF),
        V((2, C, PW), BF),
        V((2, 16, C), BF),
        V((2, 16, C), BF),
        V((2, 16, C), BF),
        V((2, 16, C), BF),
        V((2, HJ, C, TC), BF),
        V((2, HJ, C, TC), BF),
        V((3, HR, PW), BF),
        V((HR, PW), BF),
        V((2, r - 1, HR // r, PW), BF),
        V((2, r - 1, HR // (r * r), PW), BF),
        V((2, nz - 1, HR // parts, PW), BF),
        V((PW, C), F32),
        D((8,)),
        D((2, NJ)),
        D((2, NJ)),
        D((2, NJ)),
        D((2, NJ)),
        D((8,)),
        D((8,)),
        D((2, HJ)),
        D((2, HJ)),
        D((2,)),
        D((2,)),
        D((2,)),
        D((2,)),
        D((2, HJ)),
        D((2, HJ)),
        D((6, 2, NJ)),
        D((6, 2, NJ)),
        D((6,)),
        D((3,)),
        D((2, 3)),
        D((2, 3)),
        D((6, 2, 3)),
        D((6, 2, 3)),
        D((3,)),
        D((3,)),
        D((3,)),
        pltpu.SemaphoreType.REGULAR((3,)),
    ]
    res, skip, rgrad, cgrad, wg = pl.pallas_call(
        functools.partial(kernel, nz, r, cr),
        out_shape=(
            jax.ShapeDtypeStruct((M, C, TL), BF),
            jax.ShapeDtypeStruct((M, C, TL), BF),
            jax.ShapeDtypeStruct((M, C, TL), BF),
            jax.ShapeDtypeStruct((M, KC // 2, TL), F32),
            jax.ShapeDtypeStruct((2, HR, PW), BF),
        ),
        in_specs=[any_, any_, smem] + [any_] * 9,
        out_specs=(any_,) * 5,
        scratch_shapes=scratch,
        compiler_params=pltpu.CompilerParams(
            collective_id=0, has_side_effects=True, vmem_limit_bytes=64 * 2**20 - 2**17
        ),
        cost_estimate=pl.CostEstimate(
            flops=40 * 10**9, bytes_accessed=36 * 10**6, transcendentals=4 * 10**6
        ),
    )(*args[:5], jnp.swapaxes(args[5], 1, 2), *args[6:])
    shapes = [
        ((M, C, TL), BF),
        ((M, C, TL), BF),
        ((M, C, TL), F32),
        ((M, KC // 2, TL), F32),
        ((2, G, C), F32),
        ((1, G), F32),
        ((KC, G), F32),
        ((C, C), F32),
        ((1, C), F32),
        ((C, C), F32),
        ((1, C), F32),
    ]
    done = pl.pallas_call(
        finalize,
        out_shape=tuple(jax.ShapeDtypeStruct(a, d) for a, d in shapes),
        in_specs=[any_] * 5,
        out_specs=(any_,) * len(shapes),
        scratch_shapes=[
            V((M, C, TL), BF),
            V((M, C, TL), BF),
            V((M, KC // 2, TL), F32),
            V((M, C, TL), BF),
            V((M, C, TL), F32),
            V((2, HR, PW), BF),
            V((2, G, C), F32),
            V((G, C), F32),
            V((KC, G), F32),
            V((1, G), F32),
            V((1, C), F32),
            V((1, C), F32),
            D((2 + M,)),
            D((3, M)),
            D((8 + 4 * M,)),
        ],
        compiler_params=pltpu.CompilerParams(vmem_limit_bytes=64 * 2**20 - 2**17),
    )(res, skip, rgrad, cgrad, wg)
    out = [v[None] for v in done]
    out[0], out[1], out[2] = (done[k][None, :, None] for k in range(3))
    out[3] = done[3][:, None]
    out[5], out[8], out[10] = done[5], done[8], done[10]
    out[6] = jnp.swapaxes(out[6], 1, 2)
    return tuple(out)


def solution(mesh):
    nz = mesh.shape["tm"]
    r = math.isqrt(mesh.shape["batch"])
    in_specs = (
        P(None, "batch", None, "tm"),
        P(None, "batch", None, "tm"),
        P(None, "batch", None),
        P("section", None, None, None),
        P("section", None),
        P("section", None, None),
        P("section", None, None),
        P("section", None),
        P("section", None, None),
        P("section", None),
        P(None, "batch", None, "tm"),
        P(None, "batch", None, "tm"),
    )
    out_specs = (
        P("section", None, "batch", None, "tm"),
        P("section", None, "batch", None, "tm"),
        P("section", None, "batch", None, "tm"),
        P(None, "batch", "section", "tm"),
        P("section", None, None, None),
        P("section", None),
        P("section", None, None),
        P("section", None, None),
        P("section", None),
        P("section", None, None),
        P("section", None),
    )
    return jax.shard_map(
        functools.partial(local, nz, r),
        mesh=mesh,
        in_specs=in_specs,
        out_specs=out_specs,
        check_vma=False,
    )
```

```python
import functools
import math

import jax
import jax.numpy as jnp
from jax import lax
from jax.experimental import pallas as pl
from jax.experimental.pallas import tpu as pltpu
from jax.sharding import PartitionSpec as P

REACH0 = 512
TC = 256
MESH = pl.DeviceIdType.MESH
BF = jnp.bfloat16
F32 = jnp.float32
PW = 128


T_W1A = {1: [(0, 1, 0)], 3: [(0, 1, 1)]}
T_W1B = {0: [(1, 1, 0)], 1: [(0, 1, 2)]}
T_L1B = {0: [(1, 1, 1)], 1: [(2, 1, 0)], 6: [(1, 1, 2)]}
T_B0A = {0: [(2, 1, 2)], 2: [(4, 1, 0), (3, 1, 1)]}
T_B0B = {}
T_W0A = {1: [(0, 0, 0)], 2: [(3, 1, 2)], 3: [(0, 0, 1)]}
T_W0B = {0: [(1, 0, 0)], 1: [(0, 0, 2)]}
T_G0 = {0: [(1, 0, 1)], 1: [(2, 0, 0), (5, 1, 0)], 3: [(4, 1, 1)]}
T_RS = {3: [(1, 0, 2)], 5: [(2, 0, 1)], 7: [(6, 1, 0)]}
T_P0 = [(3, 1, 0), (2, 1, 1)]
TAIL = [(5, 1, 1), (2, 0, 2), (4, 1, 2), (3, 0, 0), (7, 1, 0), (3, 0, 1), (6, 1, 1), (4, 0, 0), (5, 1, 2), (3, 0, 2), (4, 0, 1), (7, 1, 1), (5, 0, 0), (6, 1, 2), (4, 0, 2), (5, 0, 1), (6, 0, 0), (7, 1, 2), (5, 0, 2), (6, 0, 1), (7, 0, 0)]
LAST = [(6, 0, 2), (7, 0, 1), (7, 0, 2)]


def dot(a, b):
    return jnp.dot(a, b, preferred_element_type=F32)


def dot_nt(a, b):
    return lax.dot_general(a, b, (((1,), (1,)), ((), ())), preferred_element_type=F32)


def rows_at(start, size, step):
    return pl.ds(pl.multiple_of(start, step), size)


def kernel(
    nz,
    r,
    cr,
    audio,
    cond,
    clips,
    convw,
    convb,
    condw,
    resw,
    resb,
    skipw,
    skipb,
    cotr,
    cots,
    res_out,
    skip_out,
    rgrad_out,
    cgrad_out,
    wg_out,
    wcat,
    wrs,
    wct,
    wrst,
    cbraw,
    rbraw,
    sbraw,
    rsbias,
    rh,
    hid,
    gb,
    gr,
    cs,
    ag1,
    cg,
    eye,
    bsum,
    mkf,
    mkb,
    htile,
    bcar,
    colf_s,
    colf_r,
    colb_s,
    colb_r,
    hs,
    hb,
    pb,
    prv,
    ra_buf,
    rb_buf,
    rz_buf,
    cacc,
    ld_w,
    ld_x,
    ld_c,
    ld_r,
    ld_s,
    w_snd,
    w_rcv,
    h_snd,
    h_rcv,
    cf_snd,
    cf_rcv,
    cb_snd,
    cb_rcv,
    hb_snd,
    hb_rcv,
    o_loc,
    o_snd,
    o_rcv,
    c_loc,
    x_snd,
    x_rcv,
    ar_snd,
    ar_rcv,
    f_loc,
    f_snd,
    f_rcv,
    credit,
):
    C = audio.shape[2]
    TL = audio.shape[3]
    KC = cond.shape[2]
    NJ = TL // TC
    HJ = REACH0 // TC
    G = 2 * C
    KP = rh.shape[3]
    HR = pb.shape[1]
    s = lax.axis_index("section")
    b = lax.axis_index("batch")
    z = lax.axis_index("tm")
    other = (1 - s, b, z)
    zprev = (s, b, z - 1)
    znext = (s, b, z + 1)
    has_prev = z > 0
    has_next = z < nz - 1

    def copy(src, dst, sem):
        return pltpu.make_async_copy(src, dst, sem)

    def rcopy(src, dst, ssem, rsem, dev):
        return pltpu.make_async_remote_copy(
            src_ref=src, dst_ref=dst, send_sem=ssem, recv_sem=rsem, device_id=dev, device_id_type=MESH
        )

    def weight_pairs(layer):
        return [
            (convw.at[0, 0], wcat.at[layer, :, pl.ds(0, C)]),
            (convw.at[0, 1], wcat.at[layer, :, pl.ds(C, C)]),
            (resw.at[0], wrs.at[layer, pl.ds(0, C)]),
            (skipw.at[0], wrs.at[layer, pl.ds(C, C)]),
            (condw.at[0], wct.at[layer, pl.ds(G, KC)]),
            (convb, cbraw.at[layer]),
            (resb, rbraw.at[layer]),
            (skipb, sbraw.at[layer]),
        ]

    own_w = [copy(a, d, ld_w.at[k]) for k, (a, d) in enumerate(weight_pairs(s))]
    for c in own_w:
        c.start()
    ldx, ldc, ldr, lds = [], [], [], []
    for i in range(2):
        for j in reversed(range(NJ)):
            cols = pl.ds(j * TC, TC)
            m = 2 * s + i
            ldx.append(copy(audio.at[m, 0, :, cols], rh.at[0, i, j, pl.ds(C, C)], ld_x.at[i, j]))
            ldc.append(copy(cond.at[m, 0, :, cols], rh.at[0, i, j, pl.ds(G, KC)], ld_c.at[i, j]))
            ldr.append(copy(cotr.at[m, 0, :, cols], gr.at[1, i, j], ld_r.at[i, j]))
            lds.append(copy(cots.at[m, 0, :, cols], cs.at[i, j], ld_s.at[i, j]))
    for c in ldx + ldc + ldr + lds:
        c.start()

    bar = pltpu.get_barrier_semaphore()

    def sa_dev(o):
        a2 = lax.rem(amem + o, r)
        return a2, (s, jnp.where(s == 0, bhi * r + a2, a2 * r + blo), z)

    def sb_dev(o):
        b2 = lax.rem(bmem + o, r)
        return b2, (s, jnp.where(s == 0, b2 * r + blo, bhi * r + b2), z)

    hops = nz // 2
    left = z < hops
    depth = jnp.where(left, z, nz - 1 - z)
    inner = (s, b, jnp.where(left, z + 1, z - 1))
    outer = (s, b, jnp.where(left, z - 1, z + 1))

    bhi = b // r
    blo = lax.rem(b, r)
    amem = jnp.where(s == 0, blo, bhi)
    bmem = jnp.where(s == 0, bhi, blo)
    peers = [other]
    peers += [sa_dev(o)[1] for o in range(1, r)]
    peers += [sb_dev(o)[1] for o in range(1, r)]
    for dev in peers:
        pl.semaphore_signal(bar, inc=1, device_id=dev, device_id_type=MESH)

    @pl.when(has_prev)
    def _():
        pl.semaphore_signal(bar, inc=1, device_id=zprev, device_id_type=MESH)

    @pl.when(has_next)
    def _():
        pl.semaphore_signal(bar, inc=1, device_id=znext, device_id_type=MESH)

    greetings = len(peers) + has_prev.astype(jnp.int32) + has_next.astype(jnp.int32)

    ri = lax.broadcasted_iota(jnp.int32, (TC, TC), 0)
    ci = lax.broadcasted_iota(jnp.int32, (TC, TC), 1)
    eye[...] = (ri == ci).astype(F32).astype(BF)
    bsum[...] = jnp.zeros(bsum.shape, F32)
    bcar[...] = jnp.zeros(bcar.shape, BF)
    rk = lax.broadcasted_iota(jnp.int32, (KP - G - KC, TC), 0)
    ones_rows = (rk < 3).astype(F32).astype(BF)
    for i in range(2):
        m = 2 * s + i
        for j in range(NJ):
            rh[0, i, j, pl.ds(G + KC, KP - G - KC), :] = ones_rows
            rh[1, i, j, pl.ds(G + KC, KP - G - KC), :] = ones_rows
            pos = z * TL + j * TC + lax.broadcasted_iota(jnp.int32, (16, TC), 1)
            start = jnp.zeros((16, TC), jnp.int32)
            end = jnp.int32(0)
            for k in range(clips.shape[2]):
                end = end + clips[m, 0, k]
                start = jnp.where(end <= pos, end, start)
            for layer, reach in ((0, REACH0), (1, 1)):
                keep = jnp.where(pos - reach >= start, 1.0, 0.0).astype(F32)
                mkf[layer, i, j] = keep[:8]
                mkb[layer, i, j] = keep.astype(BF)

    @pl.when(jnp.logical_not(has_prev))
    def _():
        for i in range(2):
            for j in range(HJ):
                rh[0, i, j, pl.ds(0, C), :] = jnp.zeros((C, TC), BF)
            htile[i] = jnp.zeros((C, PW), BF)


    tail_rows = KP - G - KC

    def prepare_forward(layer):
        row = lax.broadcasted_iota(jnp.int32, (tail_rows, G), 0)
        bias = jnp.broadcast_to(cbraw[layer], (tail_rows, G))
        hi = bias.astype(BF).astype(F32)
        mid = (bias - hi).astype(BF).astype(F32)
        low = (bias - hi) - mid
        part = jnp.where(row == 0, hi, jnp.where(row == 1, mid, jnp.where(row == 2, low, 0.0)))
        wct[layer, pl.ds(G + KC, tail_rows), :] = part.astype(BF)
        for k in range(G // TC):
            wcat[layer, pl.ds(k * TC, TC), pl.ds(G, PW)] = dot_nt(
                eye[...], wct[layer, pl.ds(G, PW), pl.ds(k * TC, TC)]
            ).astype(BF)
        rsbias[layer, pl.ds(0, C)] = jnp.broadcast_to(rbraw[layer], (PW, C)).T
        rsbias[layer, pl.ds(C, C)] = jnp.broadcast_to(sbraw[layer], (PW, C)).T

    def prepare_mix(layer):
        @pl.loop(0, C // TC)
        def _(k):
            cols = rows_at(k * TC, TC, TC)
            wrst[layer, cols, :] = dot_nt(eye[...], wrs[layer, :, cols]).astype(BF)

    def prepare_conv(layer):
        @pl.loop(0, G // TC)
        def _(k):
            cols = rows_at(k * TC, TC, TC)
            wct[layer, cols, :] = dot_nt(eye[...], wcat[layer, :, cols]).astype(BF)

    for c in own_w:
        c.wait()

    @pl.when(s == 1)
    def _():
        prepare_forward(1)
        prepare_mix(1)

    @pl.when(s == 0)
    def _():
        prepare_forward(0)
        prepare_mix(0)

    pl.semaphore_wait(bar, greetings)

    far_w = [
        rcopy(a, d, w_snd.at[k], w_rcv.at[k], other) for k, (a, d) in enumerate(weight_pairs(s))
    ]
    for c in far_w:
        c.start()

    def halo(i, j):
        return rcopy(
            audio.at[2 * s + i, 0, :, rows_at(TL - REACH0 + j * TC, TC, TC)],
            rh.at[0, i, j, pl.ds(0, C)],
            h_snd.at[i, j],
            h_rcv.at[i, j],
            znext,
        )

    def halo_start(i):
        @pl.when(has_next)
        def _():
            for j in reversed(range(HJ)):
                halo(i, j).start()

    halo_start(0)

    def phase_ready():
        @pl.when(s == 0)
        def _():
            prepare_conv(0)

        @pl.when(s == 1)
        def _():
            prepare_conv(1)
            for c in far_w:
                c.wait_recv()
            prepare_forward(0)

    phase_ready()
    for c in ldx + ldc:
        c.wait()

    def wide(tile):
        return jnp.concatenate([tile, tile], axis=1)

    def gate(layer, i, j):
        xx = rh[layer, i, j]
        out = []
        for g in range(2):
            lo = pl.ds(g * TC, TC)
            hi = pl.ds(C + g * TC, TC)
            t = jnp.tanh(dot(wcat[layer, lo, :], xx))
            q = 0.5 * jnp.tanh(0.5 * dot(wcat[layer, hi, :], xx)) + 0.5
            h = t * q
            hid[layer, i, j, lo, :] = h.astype(BF)
            out.append((q - h * t, h - h * q))
        return out

    def out_copy(kind, layer, i, j, src, dst):
        m = 2 * s + i
        return (
            copy(src, dst.at[m, :, rows_at(j * TC, TC, TC)], o_loc.at[kind, i, j]),
            rcopy(
                src,
                dst.at[m, :, rows_at(j * TC, TC, TC)],
                o_snd.at[kind, i, j],
                o_rcv.at[kind],
                other,
            ),
        )

    def out_start(kind, layer, i, j, src, dst):
        near, far = out_copy(kind, layer, i, j, src, dst)
        start_either(layer, near, far)

    def start_either(layer, near, far):
        @pl.when(s == layer)
        def _():
            near.start()

        @pl.when(s != layer)
        def _():
            far.start()

    def out_sent(kind, layer, i, j, src, dst):
        near, far = out_copy(kind, layer, i, j, src, dst)

        @pl.when(s == layer)
        def _():
            near.wait()

        @pl.when(s != layer)
        def _():
            far.wait_send()

    def out_arrived(kind, layer, dst):
        half = dst.at[pl.ds(0, 2)]

        @pl.when(s == layer)
        def _():
            copy(half, half, o_rcv.at[kind]).wait()

    def col_copy_f(i):
        return rcopy(colf_s.at[i], colf_r.at[i], cf_snd.at[i], cf_rcv.at[i], znext)

    def col_copy_b(i):
        return rcopy(colb_s.at[i], colb_r.at[i], cb_snd.at[i], cb_rcv.at[i], zprev)

    def pick_col(tile, lane):
        li = lax.broadcasted_iota(jnp.int32, (16, PW), 1)
        return dot_nt((li == lane).astype(F32).astype(BF), tile).astype(BF)

    def spread_col(rows):
        full = jnp.concatenate([rows] * (PW // 16), axis=0)
        parts = [
            dot_nt(eye[...], full[:, k * TC : (k + 1) * TC]) for k in range(C // TC)
        ]
        return jnp.concatenate(parts, axis=0)

    def fwd0(i, j):
        far = j >= HJ
        src_j = jnp.where(far, j - HJ, j)
        src_row = jnp.where(far, C, 0)
        mask = jnp.concatenate([mkb[0, i, j]] * (C // 16), axis=0)
        rh[0, i, j, pl.ds(0, C), :] = rh[0, i, src_j, rows_at(src_row, C, C), :] * mask
        parts = gate(0, i, j)
        for g in range(2):
            gb[0, i, j, pl.ds(g * TC, TC), :] = parts[g][0].astype(BF)
            gb[0, i, j, pl.ds(C + g * TC, TC), :] = parts[g][1].astype(BF)
        rs = dot(wrs[0, pl.ds(0, C)], hid[0, i, j]) + wide(rsbias[0, pl.ds(0, C)])
        x1 = (rh[0, i, j, pl.ds(C, C), :].astype(F32) + rs).astype(BF)
        rh[1, i, j, pl.ds(C, C), :] = x1
        rh[1, i, j, pl.ds(G, KC), :] = rh[0, i, j, pl.ds(G, KC), :]
        out_start(0, 0, i, j, rh.at[1, i, j, pl.ds(C, C)], res_out)

        @pl.when(jnp.logical_and(j == NJ - 1, has_next))
        def _():
            colf_s[i] = pick_col(rh[1, i, j, pl.ds(C, C), pl.ds(TC - PW, PW)], PW - 1)
            col_copy_f(i).start()

    lane_c = lax.broadcasted_iota(jnp.int32, (C, PW), 1)

    def add_sum(which, block):
        total = bsum[which]
        for k in range(TC // PW):
            total = total + block[:, k * PW : (k + 1) * PW].astype(F32)
        bsum[which] = total

    def layer1(i, j):
        x1 = rh[1, i, j, pl.ds(C, C), :].astype(F32)
        jm = jnp.maximum(j - 1, 0)
        tile = rh[1, i, jm, pl.ds(C, C), pl.ds(TC - PW, PW)].astype(F32)
        tile = jnp.where(j == 0, htile[i].astype(F32), tile)
        turned = pltpu.roll(x1, 1, 1)
        first = jnp.where(lane_c == 0, pltpu.roll(tile, 1, 1), turned[:, :PW])
        shifted = jnp.concatenate([first, turned[:, PW:]], axis=1) * mkf[1, i, j, pl.ds(0, 1), :]
        rh[1, i, j, pl.ds(0, C), :] = shifted.astype(BF)
        gh = dot(wrst[1], jnp.concatenate([gr[1, i, j], cs[i, j]], axis=0))
        add_sum(0, gr[1, i, j])
        add_sum(1, cs[i, j])
        parts = gate(1, i, j)
        for g in range(2):
            part = gh[g * TC : (g + 1) * TC]
            gb[1, i, j, pl.ds(g * TC, TC), :] = (part * parts[g][0]).astype(BF)
            gb[1, i, j, pl.ds(C + g * TC, TC), :] = (part * parts[g][1]).astype(BF)

    def layer1_back(i, j):
        dg = dot(wct[1], gb[1, i, j])
        past = dg[:C] * mkf[1, i, j, pl.ds(0, 1), :]
        turned = pltpu.roll(past, TC - 1, 1)
        last = jnp.where(lane_c == PW - 1, pltpu.roll(bcar[i].astype(F32), PW - 1, 1), turned[:, TC - PW :])
        back = jnp.concatenate([turned[:, : TC - PW], last], axis=1)
        gres = (gr[1, i, j].astype(F32) + dg[C:G] + back).astype(BF)
        gr[0, i, j] = gres
        add_sum(2, gres)
        bcar[i] = past[:, :PW].astype(BF)
        cg[i, j] = dg[G : G + KC]

        @pl.when(jnp.logical_and(j == 0, has_prev))
        def _():
            colb_s[i] = pick_col(past[:, :PW].astype(BF), 0)
            col_copy_b(i).start()

    def phase_near():
        @pl.loop(0, 2 * (NJ - HJ))
        def _(n):
            fwd0(n // (NJ - HJ), NJ - 1 - lax.rem(n, NJ - HJ))

    phase_near()
    halo_start(1)

    @pl.when(s == 0)
    def _():
        for c in far_w:
            c.wait_recv()
        prepare_forward(1)
        prepare_mix(1)
        prepare_conv(1)

    for c in ldr + lds:
        c.wait()

    def phase_main():
        @pl.loop(0, 2 * NJ)
        def _(n):
            q = n - 2
            i = jnp.where(n < 2, n, q // (NJ - 1))
            j = jnp.where(n < 2, NJ - 1, NJ - 2 - lax.rem(q, NJ - 1))

            @pl.when(jnp.logical_and(n >= 2, j >= 1))
            def _():
                @pl.when(jnp.logical_and(has_prev, j <= HJ))
                def _():
                    halo(i, j - 1).wait_recv()

                fwd0(i, j - 1)

            @pl.when(jnp.logical_and(j == 0, has_prev))
            def _():
                col_copy_f(i).wait_recv()
                htile[i] = spread_col(colf_r[i]).astype(BF)

            layer1(i, j)

    phase_main()

    offs = [0, 2 * G, 4 * G]
    sizes = [2 * G, 2 * G, 2 * G + cr]
    ARA, ARB, ARZ, ARM, AGZ, AGB, AGA = range(7)

    def geo(p):
        size, off = sizes[p], offs[p]
        na, nb_ = size // r, size // (r * r)
        base_a = off + amem * na
        base_b = base_a + bmem * nb_
        return size, off, na, nb_, base_a, base_b

    def x_copy(layer, p):
        return rcopy(
            pb.at[0, pl.ds(offs[p], sizes[p])],
            prv.at[pl.ds(offs[p], sizes[p])],
            x_snd.at[layer, p],
            x_rcv.at[layer, p],
            other,
        )

    def gathered(layer, rows):
        return ag1.at[rows] if layer == 1 else pb.at[0, rows]

    def wait_rows(count, sem, layer):
        ref = pb.at[1 + layer, pl.ds(0, count)]
        copy(ref, ref, sem).wait()

    def sum_rows(layer, start, count, parts):
        total = pb[1 + layer, rows_at(start, count, 16), :].astype(F32)
        for part in parts:
            total = total + part.astype(F32)
        return total.astype(BF)

    def add_rows(layer, start, count, parts):
        pb[1 + layer, rows_at(start, count, 16), :] = sum_rows(layer, start, count, parts)

    def step0(layer, p):
        size, off, na, nb_, base_a, base_b = geo(p)
        x_copy(layer, p).wait()
        add_rows(layer, off, size, [prv[pl.ds(off, size), :]])
        if layer == 1:
            pl.semaphore_signal(credit.at[p], inc=1, device_id=other, device_id_type=MESH)
        for o in range(1, r):
            a2, dev = sa_dev(o)
            rcopy(
                pb.at[1 + layer, rows_at(off + a2 * na, na, 16)],
                ra_buf.at[layer, o - 1, pl.ds(off // r, na)],
                ar_snd.at[ARA, layer, p],
                ar_rcv.at[ARA, layer, p],
                dev,
            ).start()

    def step1(layer, p):
        size, off, na, nb_, base_a, base_b = geo(p)
        wait_rows((r - 1) * na, ar_rcv.at[ARA, layer, p], layer)
        wait_rows((r - 1) * na, ar_snd.at[ARA, layer, p], layer)
        add_rows(
            layer, base_a, na, [ra_buf[layer, o, pl.ds(off // r, na), :] for o in range(r - 1)]
        )
        for o in range(1, r):
            b2, dev = sb_dev(o)
            rcopy(
                pb.at[1 + layer, rows_at(base_a + b2 * nb_, nb_, 16)],
                rb_buf.at[layer, o - 1, pl.ds(off // (r * r), nb_)],
                ar_snd.at[ARB, layer, p],
                ar_rcv.at[ARB, layer, p],
                dev,
            ).start()

    def step2(layer, p):
        size, off, na, nb_, base_a, base_b = geo(p)
        wait_rows((r - 1) * nb_, ar_rcv.at[ARB, layer, p], layer)
        wait_rows((r - 1) * nb_, ar_snd.at[ARB, layer, p], layer)
        add_rows(
            layer,
            base_b,
            nb_,
            [rb_buf[layer, o, pl.ds(off // (r * r), nb_), :] for o in range(r - 1)],
        )

        @pl.when(depth == 0)
        def _():
            inward(layer, p, hops == 1)

    def arrived(layer, p, slot):
        size, off, na, nb_, base_a, base_b = geo(p)
        return rz_buf.at[layer, slot, pl.ds(off // (r * r), nb_)]

    def inward(layer, p, at_middle):
        size, off, na, nb_, base_a, base_b = geo(p)
        stage = ARM if at_middle else ARZ
        rcopy(
            pb.at[1 + layer, rows_at(base_b, nb_, 16)],
            arrived(layer, p, int(at_middle)),
            ar_snd.at[stage, layer, p],
            ar_rcv.at[stage, layer, p],
            inner,
        ).start()

    def spread(layer, p, stage, start, count, devs):
        for dev in devs:
            rcopy(
                gathered(layer, rows_at(start, count, 16)),
                gathered(layer, rows_at(start, count, 16)),
                ar_snd.at[stage, layer, p],
                ar_rcv.at[stage, layer, p],
                dev,
            ).start()

    def step3(layer, p):
        size, off, na, nb_, base_a, base_b = geo(p)
        for k in range(1, hops):

            @pl.when(depth == k)
            def _():
                wait_rows(nb_, ar_rcv.at[ARZ, layer, p], layer)
                add_rows(layer, base_b, nb_, [arrived(layer, p, 0)[...]])
                inward(layer, p, k == hops - 1)

    def outward(layer, p):
        size, off, na, nb_, base_a, base_b = geo(p)
        spread(layer, p, AGZ, base_b, nb_, [outer])

    def share(layer, p):
        size, off, na, nb_, base_a, base_b = geo(p)
        spread(layer, p, AGB, base_b, nb_, [sb_dev(o)[1] for o in range(1, r)])

    def step4(layer, p):
        size, off, na, nb_, base_a, base_b = geo(p)

        @pl.when(depth == hops - 1)
        def _():
            wait_rows(nb_, ar_rcv.at[ARM, layer, p], layer)
            wait_rows(nb_, ar_snd.at[ARM, layer, p], layer)
            gathered(layer, rows_at(base_b, nb_, 16))[...] = sum_rows(
                layer, base_b, nb_, [arrived(layer, p, 1)[...]]
            )
            if hops > 1:
                outward(layer, p)
            share(layer, p)

    def step5(layer, p):
        size, off, na, nb_, base_a, base_b = geo(p)
        for k in reversed(range(hops - 1)):

            @pl.when(depth == k)
            def _():
                wait_rows(nb_, ar_rcv.at[AGZ, layer, p], layer)
                wait_rows(nb_, ar_snd.at[ARZ, layer, p], layer)
                if k > 0:
                    outward(layer, p)
                share(layer, p)

    def step6(layer, p):
        size, off, na, nb_, base_a, base_b = geo(p)
        wait_rows((r - 1) * nb_, ar_rcv.at[AGB, layer, p], layer)
        wait_rows((r - 1) * nb_, ar_snd.at[AGB, layer, p], layer)

        @pl.when(depth > 0)
        def _():
            wait_rows(nb_, ar_snd.at[AGZ, layer, p], layer)

        spread(layer, p, AGA, base_a, na, [sa_dev(o)[1] for o in range(1, r)])

    def final_copies(layer, p):
        src = gathered(layer, pl.ds(offs[p], sizes[p]))
        dst = wg_out.at[s, pl.ds(offs[p], sizes[p])]
        return (
            copy(src, dst, f_loc.at[p]),
            rcopy(src, dst, f_snd.at[p], f_rcv.at[p], other),
        )

    def step7(layer, p):
        size, off, na, nb_, base_a, base_b = geo(p)
        wait_rows((r - 1) * na, ar_rcv.at[AGA, layer, p], layer)
        wait_rows((r - 1) * na, ar_snd.at[AGA, layer, p], layer)
        near, far = final_copies(layer, p)

        @pl.when(s == layer)
        def _():
            near.start()

        @pl.when(s != layer)
        def _():
            far.start()

    steps = [step0, step1, step2, step3, step4, step5, step6, step7]

    def at(n, table):
        for k, todo in table.items():

            @pl.when(n == k)
            def _(todo=todo):
                for st, layer, p in todo:
                    steps[st](layer, p)

    def weight_tasks(layer, table_a, table_b):
        @pl.loop(0, 4)
        def _(n):
            p = n // 2
            mine = lax.rem(n, 2)
            half = jnp.where(mine == 1, s, 1 - s)
            dst = mine * (1 + layer)
            if layer == 0:

                @pl.when(mine == 0)
                def _():
                    pl.semaphore_wait(credit.at[p], 1)

            ch = rows_at(half * C + p * TC, TC, TC)
            total = dot_nt(gb[layer, 0, 0], rh[layer, 0, 0, ch, :])
            for i in range(2):
                for j in range(NJ):
                    if i + j > 0:
                        total = total + dot_nt(gb[layer, i, j], rh[layer, i, j, ch, :])
            total = total.astype(BF)
            pb[dst, rows_at(p * 2 * G, G, G), :] = total[:, :PW]
            pb[dst, rows_at(p * 2 * G + G, G, G), :] = total[:, PW:]
            for pp in range(2):

                @pl.when(n == 2 * pp)
                def _():
                    x_copy(layer, pp).start()

            at(n, table_a)

        @pl.loop(0, 2)
        def _(n):
            half = jnp.where(n == 1, s, 1 - s)
            dst = n * (1 + layer)
            if layer == 0:

                @pl.when(n == 0)
                def _():
                    pl.semaphore_wait(credit.at[2], 1)

            ch = rows_at(half * TC, TC, TC)
            for src, row in ((lambda i, j: gr[layer, i, j], 0), (lambda i, j: cs[i, j], C)):
                total = dot_nt(src(0, 0), hid[layer, 0, 0, ch, :])
                for i in range(2):
                    for j in range(NJ):
                        if i + j > 0:
                            total = total + dot_nt(src(i, j), hid[layer, i, j, ch, :])
                total = total.astype(BF)
                pb[dst, pl.ds(4 * G + row, C), :] = total[:, :PW]
                pb[dst, pl.ds(5 * G + row, C), :] = total[:, PW:]
            gp_rows = rows_at(half * C, C, C)
            total = jnp.zeros((PW, C), F32)
            for i in range(2):
                for j in range(NJ):
                    total = total + dot_nt(
                        rh[layer, i, j, pl.ds(G, PW), :], gb[layer, i, j, gp_rows, :]
                    )
            cacc[...] = total
            which = jnp.where(half == 1, 1, 2 - 2 * layer)
            cacc[pl.ds(KC + 3, 1), :] = jnp.sum(bsum[which].T, axis=0, keepdims=True)
            for k in range(C // PW):
                pb[dst, pl.ds(6 * G + k * PW, PW), :] = cacc[:, k * PW : (k + 1) * PW].astype(BF)
            if cr > C:
                pb[dst, pl.ds(6 * G + C, cr - C), :] = jnp.zeros((cr - C, PW), BF)

            @pl.when(n == 0)
            def _():
                x_copy(layer, 2).start()

            at(n, table_b)

    def fix_last(i):
        @pl.when(has_next)
        def _():
            col_copy_b(i).wait_recv()
            tile = gr[0, i, NJ - 1, :, pl.ds(TC - PW, PW)].astype(F32)
            add = jnp.where(lane_c == PW - 1, spread_col(colb_r[i]), 0.0)
            bsum[2] = bsum[2] + add
            gr[0, i, NJ - 1, :, pl.ds(TC - PW, PW)] = (tile + add).astype(BF)

    def phase_w1():
        weight_tasks(1, T_W1A, T_W1B)

    phase_w1()

    def run_steps(todo):
        for st, layer, p in todo:
            steps[st](layer, p)

    def phase_l1b():

        @pl.loop(0, 2 * NJ)
        def _(n):
            layer1_back(n // NJ, NJ - 1 - lax.rem(n, NJ))
            at(n, T_L1B)

        @pl.when(s == 1)
        def _():
            prepare_mix(0)
            prepare_conv(0)

        run_steps(T_P0)

    phase_l1b()

    def hb_copy(i, j):
        return rcopy(hs.at[i, j], hb.at[i, j], hb_snd.at[i, j], hb_rcv.at[i, j], zprev)

    def back0(i, j):
        gh = dot(wrst[0], jnp.concatenate([gr[0, i, j], cs[i, j]], axis=0))
        for g in range(2):
            part = gh[g * TC : (g + 1) * TC]
            for row in (g * TC, C + g * TC):
                rows = pl.ds(row, TC)
                gb[0, i, j, rows, :] = (part * gb[0, i, j, rows, :].astype(F32)).astype(BF)

    def grad0(i, j):
        dg = dot(wct[0], gb[0, i, j])
        past = dg[:C] * mkf[0, i, j, pl.ds(0, 1), :]
        gr[1, i, j] = (gr[0, i, j].astype(F32) + dg[C:G]).astype(BF)
        cg[i, j] = cg[i, j] + dg[G : G + KC]
        m = 2 * s + i
        cols = rows_at(j * TC, TC, TC)
        hc = KC // 2
        copy(
            cg.at[i, j, rows_at(s * hc, hc, 8)], cgrad_out.at[m, :, cols], c_loc.at[0]
        ).start()
        rcopy(
            cg.at[i, j, rows_at((1 - s) * hc, hc, 8)],
            cgrad_out.at[m, :, cols],
            c_loc.at[1],
            c_loc.at[2],
            other,
        ).start()
        return past

    def phase_b0a():
        @pl.loop(0, 2 * HJ)
        def _(n):
            i, j = n // HJ, lax.rem(n, HJ)
            back0(i, j)
            past = grad0(i, j)

            @pl.when(has_prev)
            def _():
                hs[i, j] = past.astype(BF)
                hb_copy(i, j).start()

            at(n, T_B0A)

    phase_b0a()

    for i in range(2):
        fix_last(i)
        for j in range(NJ):
            out_start(4, 1, i, j, gr.at[0, i, j], rgrad_out)

    def phase_b0b():
        @pl.loop(0, 2 * (NJ - HJ))
        def _(n):
            back0(n // (NJ - HJ), HJ + lax.rem(n, NJ - HJ))
            at(n, T_B0B)

    phase_b0b()

    def phase_w0():
        weight_tasks(0, T_W0A, T_W0B)

    phase_w0()

    def phase_g0():
        @pl.loop(0, 2 * (NJ - HJ))
        def _(n):
            i, k = n // (NJ - HJ), lax.rem(n, NJ - HJ)
            past = grad0(i, HJ + k)
            gr[1, i, k] = (gr[1, i, k].astype(F32) + past).astype(BF)
            out_start(5, 0, i, k, gr.at[1, i, k], rgrad_out)
            at(n, T_G0)

    phase_g0()

    def phase_rs():
        @pl.loop(0, 2 * NJ)
        def _(n):
            i, j = n // NJ, lax.rem(n, NJ)
            x1 = rh.at[1, i, j, pl.ds(C, C)]
            sk0 = rh.at[1, i, j, pl.ds(0, C)]
            sk1 = hid.at[1, i, j]
            skip = dot(wrs[0, pl.ds(C, C)], hid[0, i, j]) + wide(rsbias[0, pl.ds(C, C)])
            skip = skip.astype(BF)
            sk0[...] = skip
            out_start(1, 0, i, j, sk0, skip_out)
            rs = dot(wrs[1], sk1[...]) + wide(rsbias[1])
            sk1[...] = (skip.astype(F32) + rs[C:]).astype(BF)
            out_start(3, 1, i, j, sk1, skip_out)
            out_sent(0, 0, i, j, x1, res_out)
            x1[...] = (x1[...].astype(F32) + rs[:C]).astype(BF)
            out_start(2, 1, i, j, x1, res_out)
            at(n, T_RS)

    phase_rs()

    def phase_tail():
        run_steps(TAIL)

    phase_tail()

    for i in range(2):
        for k in range(HJ):
            j = NJ - HJ + k

            @pl.when(has_next)
            def _():
                hb_copy(i, k).wait_recv()
                gr[1, i, j] = (gr[1, i, j].astype(F32) + hb[i, k].astype(F32)).astype(BF)

            out_start(5, 0, i, j, gr.at[1, i, j], rgrad_out)

    def phase_last():
        run_steps(LAST)

    phase_last()

    @pl.loop(0, 2 * NJ)
    def _(n):
        i, j = n // NJ, lax.rem(n, NJ)
        blk = gr.at[0, i, j]
        out_sent(1, 0, i, j, blk, skip_out)
        out_sent(2, 1, i, j, blk, res_out)
        out_sent(3, 1, i, j, blk, skip_out)
        out_sent(4, 1, i, j, blk, rgrad_out)
        out_sent(5, 0, i, j, blk, rgrad_out)

    out_arrived(0, 0, res_out)
    out_arrived(1, 0, skip_out)
    out_arrived(2, 1, res_out)
    out_arrived(3, 1, skip_out)
    out_arrived(4, 1, rgrad_out)
    out_arrived(5, 0, rgrad_out)
    half = cgrad_out.at[pl.ds(0, 2)]
    for k in range(3):
        copy(half, half, c_loc.at[k]).wait()
    for p in range(3):
        near, far = final_copies(0, p)
        near.wait()
        far.wait()
    for c in far_w:
        c.wait_send()

    @pl.when(has_next)
    def _():
        for i in range(2):
            for j in range(HJ):
                halo(i, j).wait_send()
            col_copy_f(i).wait_send()

    @pl.when(has_prev)
    def _():
        for i in range(2):
            col_copy_b(i).wait_send()
            for j in range(HJ):
                hb_copy(i, j).wait_send()


def finalize(
    res, skip, rgrad, cgrad, wg,
    res_o, skip_o, rgrad_o, cgrad_o, conv_o, convb_o, condw_o, resw_o, resb_o, skipw_o, skipb_o,
    rbuf, sbuf, cbuf, rin, rwide, win, convf, mixf, condf, cbf, rbf, sbf, sem_in, sem_cp, sem_out,
):
    M, C, TL = res.shape
    G = 2 * C
    KC = condw_o.shape[0]
    copies = []
    loads = [pltpu.make_async_copy(wg.at[h], win.at[h], sem_in.at[h]) for h in range(2)]
    reads = [pltpu.make_async_copy(rgrad.at[m], rin.at[m], sem_in.at[2 + m]) for m in range(M)]
    for c in loads + reads:
        c.start()
    passing = []
    for k, (a, buf, o) in enumerate(
        ((res, rbuf, res_o), (skip, sbuf, skip_o), (cgrad, cbuf, cgrad_o))
    ):
        for m in range(M):
            c = pltpu.make_async_copy(a.at[m], buf.at[m], sem_cp.at[k, m])
            c.start()
            passing.append((c, buf.at[m], o.at[m], 8 + M + k * M + m))

    def put(src, dst, k):
        c = pltpu.make_async_copy(src, dst, sem_out.at[k])
        c.start()
        copies.append(c)

    for h in range(2):
        loads[h].wait()
        for q in range(C // PW):
            convf[h, :, q * PW : (q + 1) * PW] = win[h, pl.ds(q * G, G), :].astype(F32)
        put(convf.at[h], conv_o.at[h], h)
        for q in range(2):
            lanes = slice(h * 2 * PW + q * PW, h * 2 * PW + (q + 1) * PW)
            mixf[:, lanes] = win[h, pl.ds((4 + q) * G, G), :].astype(F32)
        for q in range(C // PW):
            blk = win[h, pl.ds(6 * G + q * PW, PW), :].astype(F32)
            lanes = slice(h * C + q * PW, h * C + (q + 1) * PW)
            condf[:, lanes] = blk[:KC]
            cbf[:, lanes] = blk[KC : KC + 1]
            (sbf if h else rbf)[:, q * PW : (q + 1) * PW] = blk[KC + 3 : KC + 4]
    put(mixf.at[pl.ds(0, C)], resw_o, 2)
    put(mixf.at[pl.ds(C, C)], skipw_o, 3)
    put(condf, condw_o, 4)
    put(cbf, convb_o, 5)
    put(rbf, resb_o, 6)
    put(sbf, skipb_o, 7)
    for c, src, dst, k in passing:
        c.wait()
        put(src, dst, k)
    for m in range(M):
        reads[m].wait()
        rwide[m] = rin[m].astype(F32)
        put(rwide.at[m], rgrad_o.at[m], 8 + m)
    for c in copies:
        c.wait()


def local(nz, r, *args):
    audio, cond = args[0], args[1]
    M, _, C, TL = audio.shape
    KC = cond.shape[2]
    G = 2 * C
    NJ = TL // TC
    HJ = REACH0 // TC
    KP = G + PW
    parts = r * r * nz
    cr = max(C, 16 * parts)
    HR = 6 * G + cr
    any_ = pl.BlockSpec(memory_space=pl.ANY)
    smem = pl.BlockSpec(memory_space=pltpu.SMEM)
    V = pltpu.VMEM
    D = pltpu.SemaphoreType.DMA
    scratch = [
        V((2, G, KP), BF),
        V((2, G, C), BF),
        V((2, KP, G), BF),
        V((2, C, G), BF),
        V((2, 1, G), F32),
        V((2, 1, C), F32),
        V((2, 1, C), F32),
        V((2, G, PW), F32),
        V((2, 2, NJ, KP, TC), BF),
        V((2, 2, NJ, C, TC), BF),
        V((2, 2, NJ, G, TC), BF),
        V((2, 2, NJ, C, TC), BF),
        V((2, NJ, C, TC), BF),
        V((HR, PW), BF),
        V((2, NJ, KC, TC), F32),
        V((TC, TC), BF),
        V((3, C, PW), F32),
        V((2, 2, NJ, 8, TC), F32),
        V((2, 2, NJ, 16, TC), BF),
        V((2, C, PW), BF),
        V((2, C, PW), BF),
        V((2, 16, C), BF),
        V((2, 16, C), BF),
        V((2, 16, C), BF),
        V((2, 16, C), BF),
        V((2, HJ, C, TC), BF),
        V((2, HJ, C, TC), BF),
        V((3, HR, PW), BF),
        V((HR, PW), BF),
        V((2, r - 1, HR // r, PW), BF),
        V((2, r - 1, HR // (r * r), PW), BF),
        V((2, 2, HR // (r * r), PW), BF),
        V((PW, C), F32),
        D((8,)),
        D((2, NJ)),
        D((2, NJ)),
        D((2, NJ)),
        D((2, NJ)),
        D((8,)),
        D((8,)),
        D((2, HJ)),
        D((2, HJ)),
        D((2,)),
        D((2,)),
        D((2,)),
        D((2,)),
        D((2, HJ)),
        D((2, HJ)),
        D((6, 2, NJ)),
        D((6, 2, NJ)),
        D((6,)),
        D((3,)),
        D((2, 3)),
        D((2, 3)),
        D((7, 2, 3)),
        D((7, 2, 3)),
        D((3,)),
        D((3,)),
        D((3,)),
        pltpu.SemaphoreType.REGULAR((3,)),
    ]
    res, skip, rgrad, cgrad, wg = pl.pallas_call(
        functools.partial(kernel, nz, r, cr),
        out_shape=(
            jax.ShapeDtypeStruct((M, C, TL), BF),
            jax.ShapeDtypeStruct((M, C, TL), BF),
            jax.ShapeDtypeStruct((M, C, TL), BF),
            jax.ShapeDtypeStruct((M, KC // 2, TL), F32),
            jax.ShapeDtypeStruct((2, HR, PW), BF),
        ),
        in_specs=[any_, any_, smem] + [any_] * 9,
        out_specs=(any_,) * 5,
        scratch_shapes=scratch,
        compiler_params=pltpu.CompilerParams(
            collective_id=0, has_side_effects=True, vmem_limit_bytes=64 * 2**20 - 2**17
        ),
        cost_estimate=pl.CostEstimate(
            flops=40 * 10**9, bytes_accessed=36 * 10**6, transcendentals=4 * 10**6
        ),
    )(*args[:5], jnp.swapaxes(args[5], 1, 2), *args[6:])
    shapes = [
        ((M, C, TL), BF),
        ((M, C, TL), BF),
        ((M, C, TL), F32),
        ((M, KC // 2, TL), F32),
        ((2, G, C), F32),
        ((1, G), F32),
        ((KC, G), F32),
        ((C, C), F32),
        ((1, C), F32),
        ((C, C), F32),
        ((1, C), F32),
    ]
    done = pl.pallas_call(
        finalize,
        out_shape=tuple(jax.ShapeDtypeStruct(a, d) for a, d in shapes),
        in_specs=[any_] * 5,
        out_specs=(any_,) * len(shapes),
        scratch_shapes=[
            V((M, C, TL), BF),
            V((M, C, TL), BF),
            V((M, KC // 2, TL), F32),
            V((M, C, TL), BF),
            V((M, C, TL), F32),
            V((2, HR, PW), BF),
            V((2, G, C), F32),
            V((G, C), F32),
            V((KC, G), F32),
            V((1, G), F32),
            V((1, C), F32),
            V((1, C), F32),
            D((2 + M,)),
            D((3, M)),
            D((8 + 4 * M,)),
        ],
        compiler_params=pltpu.CompilerParams(vmem_limit_bytes=64 * 2**20 - 2**17),
    )(res, skip, rgrad, cgrad, wg)
    out = [v[None] for v in done]
    out[0], out[1], out[2] = (done[k][None, :, None] for k in range(3))
    out[3] = done[3][:, None]
    out[5], out[8], out[10] = done[5], done[8], done[10]
    out[6] = jnp.swapaxes(out[6], 1, 2)
    return tuple(out)


def solution(mesh):
    nz = mesh.shape["tm"]
    r = math.isqrt(mesh.shape["batch"])
    in_specs = (
        P(None, "batch", None, "tm"),
        P(None, "batch", None, "tm"),
        P(None, "batch", None),
        P("section", None, None, None),
        P("section", None),
        P("section", None, None),
        P("section", None, None),
        P("section", None),
        P("section", None, None),
        P("section", None),
        P(None, "batch", None, "tm"),
        P(None, "batch", None, "tm"),
    )
    out_specs = (
        P("section", None, "batch", None, "tm"),
        P("section", None, "batch", None, "tm"),
        P("section", None, "batch", None, "tm"),
        P(None, "batch", "section", "tm"),
        P("section", None, None, None),
        P("section", None),
        P("section", None, None),
        P("section", None, None),
        P("section", None),
        P("section", None, None),
        P("section", None),
    )
    return jax.shard_map(
        functools.partial(local, nz, r),
        mesh=mesh,
        in_specs=in_specs,
        out_specs=out_specs,
        check_vma=False,
    )
```

```python
import functools
import math

import jax
import jax.numpy as jnp
from jax import lax
from jax.experimental import pallas as pl
from jax.experimental.pallas import tpu as pltpu
from jax.sharding import PartitionSpec as P

REACH0 = 512
TC = 256
MESH = pl.DeviceIdType.MESH
BF = jnp.bfloat16
F32 = jnp.float32
PW = 128
CROWS = 96


T_W1C = {1: [(0, 1, 0), (0, 1, 1)], 3: [(0, 1, 2), (0, 1, 3)]}
T_SK1 = {1: [(1, 1, 0)]}
T_RE1 = {0: [(0, 1, 4), (1, 1, 1)], 1: [(0, 1, 5)]}
T_CO1 = {0: [(1, 1, 2)], 1: [(1, 1, 3), (0, 1, 6), (2, 1, 0)]}
T_SK0 = {1: [(1, 1, 4), (2, 1, 1)]}
T_L1B = {0: [(0, 0, 4), (1, 1, 5)], 1: [(2, 1, 2)], 2: [(2, 1, 3), (1, 1, 6)], 3: [(3, 1, 0)], 4: [(2, 1, 4)], 5: [(3, 1, 1)], 6: [(1, 0, 4)], 7: [(2, 1, 5), (2, 1, 6), (3, 1, 2)]}
T_B0A = {1: [(3, 1, 3)], 2: [(4, 1, 0)]}
T_RE0 = {0: [(5, 1, 1), (3, 0, 4)]}
T_B0B = {0: [(3, 1, 4)], 2: [(4, 1, 1), (2, 0, 4)]}
T_GH = {0: [(3, 1, 5), (4, 1, 2)], 1: [(3, 1, 6)], 2: [(4, 1, 3), (5, 1, 0)], 3: [(4, 1, 4)]}
T_W0C = {0: [(0, 0, 5)], 1: [(6, 1, 0), (0, 0, 0), (6, 1, 1), (0, 0, 1)], 3: [(5, 1, 2), (4, 1, 5), (1, 0, 5), (0, 0, 2), (0, 0, 3)]}
T_CO0 = {0: [(7, 1, 0)], 1: [(0, 0, 6), (1, 0, 0)]}
T_G0 = {0: [(7, 1, 1)], 1: [(4, 1, 6), (1, 0, 1)], 2: [(6, 1, 2)], 3: [(2, 0, 5)]}
T_RS = {1: [(1, 0, 2)], 3: [(1, 0, 3), (1, 0, 6)], 4: [(2, 0, 0)], 5: [(5, 1, 3), (2, 0, 1)], 7: [(7, 1, 2)]}
TAIL = [(2, 0, 2), (2, 0, 3), (2, 0, 6), (3, 0, 5), (6, 1, 3), (3, 0, 0), (4, 0, 4), (5, 1, 4), (3, 0, 1), (4, 0, 5), (5, 1, 5), (3, 0, 2), (7, 1, 3), (5, 1, 6), (4, 0, 0), (3, 0, 3), (6, 1, 4), (5, 0, 4), (3, 0, 6), (4, 0, 1), (6, 1, 5), (6, 1, 6), (5, 0, 5), (4, 0, 2), (5, 0, 0), (4, 0, 3), (7, 1, 4), (4, 0, 6), (6, 0, 4), (5, 0, 1), (7, 1, 5), (5, 0, 2), (7, 1, 6), (6, 0, 5), (5, 0, 3), (6, 0, 0), (5, 0, 6), (7, 0, 4), (6, 0, 1), (6, 0, 2), (7, 0, 5), (6, 0, 3), (7, 0, 0), (6, 0, 6)]
LAST = [(7, 0, 1), (7, 0, 2), (7, 0, 3), (7, 0, 6)]


def dot(a, b):
    return jnp.dot(a, b, preferred_element_type=F32)


def dot_nt(a, b):
    return lax.dot_general(a, b, (((1,), (1,)), ((), ())), preferred_element_type=F32)


def rows_at(start, size, step):
    return pl.ds(pl.multiple_of(start, step), size)


def kernel(
    nz,
    r,
    cr,
    audio,
    cond,
    clips,
    convw,
    convb,
    condw,
    resw,
    resb,
    skipw,
    skipb,
    cotr,
    cots,
    res_out,
    skip_out,
    rgrad_out,
    cgrad_out,
    wg_out,
    wcat,
    wrs,
    wct,
    wrst,
    cbraw,
    rbraw,
    sbraw,
    rsbias,
    rh,
    hid,
    gb,
    gr,
    cs,
    ag1,
    cg,
    eye,
    bsum,
    mkf,
    mkb,
    htile,
    bcar,
    colf_s,
    colf_r,
    colb_s,
    colb_r,
    hs,
    hb,
    pb,
    prv,
    ra_buf,
    rb_buf,
    rz_buf,
    cacc,
    ld_w,
    ld_x,
    ld_c,
    ld_r,
    ld_s,
    w_snd,
    w_rcv,
    t_snd,
    t_rcv,
    h_snd,
    h_rcv,
    cf_snd,
    cf_rcv,
    cb_snd,
    cb_rcv,
    hb_snd,
    hb_rcv,
    o_loc,
    o_snd,
    o_rcv,
    c_loc,
    x_snd,
    x_rcv,
    ar_snd,
    ar_rcv,
    f_loc,
    f_snd,
    f_rcv,
    credit,
):
    C = audio.shape[2]
    TL = audio.shape[3]
    KC = cond.shape[2]
    NJ = TL // TC
    HJ = REACH0 // TC
    G = 2 * C
    KP = rh.shape[3]
    HR = pb.shape[1]
    s = lax.axis_index("section")
    b = lax.axis_index("batch")
    z = lax.axis_index("tm")
    other = (1 - s, b, z)
    zprev = (s, b, z - 1)
    znext = (s, b, z + 1)
    has_prev = z > 0
    has_next = z < nz - 1

    def copy(src, dst, sem):
        return pltpu.make_async_copy(src, dst, sem)

    def rcopy(src, dst, ssem, rsem, dev):
        return pltpu.make_async_remote_copy(
            src_ref=src, dst_ref=dst, send_sem=ssem, recv_sem=rsem, device_id=dev, device_id_type=MESH
        )

    def weight_pairs(layer):
        return [
            (convw.at[0, 0], wcat.at[layer, :, pl.ds(0, C)]),
            (convw.at[0, 1], wcat.at[layer, :, pl.ds(C, C)]),
            (condw.at[0], wct.at[layer, pl.ds(G, KC)]),
            (convb, cbraw.at[layer]),
            (resb, rbraw.at[layer]),
            (skipb, sbraw.at[layer]),
            (resw.at[0], wrs.at[layer, pl.ds(0, C)]),
            (skipw.at[0], wrs.at[layer, pl.ds(C, C)]),
        ]

    own_w = [copy(a, d, ld_w.at[k]) for k, (a, d) in enumerate(weight_pairs(s))]
    for c in own_w:
        c.start()
    ldx, ldc, ldr, lds = [], [], [], []
    for i in range(2):
        for j in reversed(range(NJ)):
            cols = pl.ds(j * TC, TC)
            m = 2 * s + i
            ldx.append(copy(audio.at[m, 0, :, cols], rh.at[0, i, j, pl.ds(C, C)], ld_x.at[i, j]))
            ldc.append(copy(cond.at[m, 0, :, cols], rh.at[0, i, j, pl.ds(G, KC)], ld_c.at[i, j]))
            ldr.append(copy(cotr.at[m, 0, :, cols], gr.at[1, i, j], ld_r.at[i, j]))
            lds.append(copy(cots.at[m, 0, :, cols], cs.at[i, j], ld_s.at[i, j]))
    for c in ldx + ldc + ldr + lds:
        c.start()

    bar = pltpu.get_barrier_semaphore()

    def sa_dev(o):
        a2 = lax.rem(amem + o, r)
        return a2, (s, jnp.where(s == 0, bhi * r + a2, a2 * r + blo), z)

    def sb_dev(o):
        b2 = lax.rem(bmem + o, r)
        return b2, (s, jnp.where(s == 0, b2 * r + blo, bhi * r + b2), z)

    hops = nz // 2
    left = z < hops
    depth = jnp.where(left, z, nz - 1 - z)
    inner = (s, b, jnp.where(left, z + 1, z - 1))
    outer = (s, b, jnp.where(left, z - 1, z + 1))

    bhi = b // r
    blo = lax.rem(b, r)
    amem = jnp.where(s == 0, blo, bhi)
    bmem = jnp.where(s == 0, bhi, blo)
    peers = [other]
    peers += [sa_dev(o)[1] for o in range(1, r)]
    peers += [sb_dev(o)[1] for o in range(1, r)]
    for dev in peers:
        pl.semaphore_signal(bar, inc=1, device_id=dev, device_id_type=MESH)

    @pl.when(has_prev)
    def _():
        pl.semaphore_signal(bar, inc=1, device_id=zprev, device_id_type=MESH)

    @pl.when(has_next)
    def _():
        pl.semaphore_signal(bar, inc=1, device_id=znext, device_id_type=MESH)

    greetings = len(peers) + has_prev.astype(jnp.int32) + has_next.astype(jnp.int32)

    ri = lax.broadcasted_iota(jnp.int32, (TC, TC), 0)
    ci = lax.broadcasted_iota(jnp.int32, (TC, TC), 1)
    eye[...] = (ri == ci).astype(F32).astype(BF)
    bsum[...] = jnp.zeros(bsum.shape, F32)
    bcar[...] = jnp.zeros(bcar.shape, BF)
    rk = lax.broadcasted_iota(jnp.int32, (KP - G - KC, TC), 0)
    ones_rows = (rk < 3).astype(F32).astype(BF)
    for i in range(2):
        m = 2 * s + i
        for j in range(NJ):
            rh[0, i, j, pl.ds(G + KC, KP - G - KC), :] = ones_rows
            rh[1, i, j, pl.ds(G + KC, KP - G - KC), :] = ones_rows
            pos = z * TL + j * TC + lax.broadcasted_iota(jnp.int32, (16, TC), 1)
            start = jnp.zeros((16, TC), jnp.int32)
            end = jnp.int32(0)
            for k in range(clips.shape[2]):
                end = end + clips[m, 0, k]
                start = jnp.where(end <= pos, end, start)
            for layer, reach in ((0, REACH0), (1, 1)):
                keep = jnp.where(pos - reach >= start, 1.0, 0.0).astype(F32)
                mkf[layer, i, j] = keep[:8]
                mkb[layer, i, j] = keep.astype(BF)

    @pl.when(jnp.logical_not(has_prev))
    def _():
        for i in range(2):
            for j in range(HJ):
                rh[0, i, j, pl.ds(0, C), :] = jnp.zeros((C, TC), BF)
            htile[i] = jnp.zeros((C, PW), BF)


    tail_rows = KP - G - KC

    def prepare_forward(layer):
        row = lax.broadcasted_iota(jnp.int32, (tail_rows, G), 0)
        bias = jnp.broadcast_to(cbraw[layer], (tail_rows, G))
        hi = bias.astype(BF).astype(F32)
        mid = (bias - hi).astype(BF).astype(F32)
        low = (bias - hi) - mid
        part = jnp.where(row == 0, hi, jnp.where(row == 1, mid, jnp.where(row == 2, low, 0.0)))
        wct[layer, pl.ds(G + KC, tail_rows), :] = part.astype(BF)
        for k in range(G // TC):
            wcat[layer, pl.ds(k * TC, TC), pl.ds(G, PW)] = dot_nt(
                eye[...], wct[layer, pl.ds(G, PW), pl.ds(k * TC, TC)]
            ).astype(BF)
        rsbias[layer, pl.ds(0, C)] = jnp.broadcast_to(rbraw[layer], (PW, C)).T
        rsbias[layer, pl.ds(C, C)] = jnp.broadcast_to(sbraw[layer], (PW, C)).T

    def prepare_mix(layer):
        @pl.loop(0, C // TC)
        def _(k):
            cols = rows_at(k * TC, TC, TC)
            wrst[layer, cols, :] = dot_nt(eye[...], wrs[layer, :, cols]).astype(BF)

    def prepare_conv(layer):
        @pl.loop(0, G // TC)
        def _(k):
            cols = rows_at(k * TC, TC, TC)
            wct[layer, cols, :] = dot_nt(eye[...], wcat[layer, :, cols]).astype(BF)

    for c in own_w:
        c.wait()

    prepare_forward(s)
    prepare_mix(s)
    pl.semaphore_wait(bar, greetings)

    far_w = [
        rcopy(a, d, w_snd.at[k], w_rcv.at[k], other) for k, (a, d) in enumerate(weight_pairs(s))
    ]
    for c in far_w:
        c.start()

    def halo(i, j):
        return rcopy(
            audio.at[2 * s + i, 0, :, rows_at(TL - REACH0 + j * TC, TC, TC)],
            rh.at[0, i, j, pl.ds(0, C)],
            h_snd.at[i, j],
            h_rcv.at[i, j],
            znext,
        )

    def halo_start(i):
        @pl.when(has_next)
        def _():
            for j in reversed(range(HJ)):
                halo(i, j).start()

    halo_start(0)

    mix_w = rcopy(wrst.at[s], wrst.at[s], t_snd.at[0], t_rcv.at[0], other)
    conv_w = rcopy(
        wct.at[s, pl.ds(0, G)], wct.at[s, pl.ds(0, G)], t_snd.at[1], t_rcv.at[1], other
    )
    mix_w.start()

    def phase_ready():
        prepare_conv(s)

    phase_ready()
    conv_w.start()

    for c in ldr + lds:
        c.wait()

    def mix_back():
        @pl.loop(0, 2 * NJ)
        def _(n):
            i, j = n // NJ, lax.rem(n, NJ)
            gh = dot(wrst[1], jnp.concatenate([gr[1, i, j], cs[i, j]], axis=0))
            high = gh.astype(BF)
            gb[1, i, j, pl.ds(0, C), :] = high
            gb[1, i, j, pl.ds(C, C), :] = (gh - high.astype(F32)).astype(BF)
            add_sum(0, gr[1, i, j])
            add_sum(1, cs[i, j])

    def add_sum(which, block):
        total = bsum[which]
        for k in range(TC // PW):
            total = total + block[:, k * PW : (k + 1) * PW].astype(F32)
        bsum[which] = total

    @pl.when(s == 1)
    def _():
        mix_back()
        for c in far_w[:6]:
            c.wait_recv()
        prepare_forward(0)

    for c in ldx + ldc:
        c.wait()

    def wide(tile):
        return jnp.concatenate([tile, tile], axis=1)

    def gate(layer, i, j):
        xx = rh[layer, i, j]
        out = []
        for g in range(2):
            lo = pl.ds(g * TC, TC)
            hi = pl.ds(C + g * TC, TC)
            t = jnp.tanh(dot(wcat[layer, lo, :], xx))
            q = 0.5 * jnp.tanh(0.5 * dot(wcat[layer, hi, :], xx)) + 0.5
            h = t * q
            hid[layer, i, j, lo, :] = h.astype(BF)
            out.append((q - h * t, h - h * q))
        return out

    def out_copy(kind, layer, i, j, src, dst):
        m = 2 * s + i
        return (
            copy(src, dst.at[m, :, rows_at(j * TC, TC, TC)], o_loc.at[kind, i, j]),
            rcopy(
                src,
                dst.at[m, :, rows_at(j * TC, TC, TC)],
                o_snd.at[kind, i, j],
                o_rcv.at[kind],
                other,
            ),
        )

    def out_start(kind, layer, i, j, src, dst):
        near, far = out_copy(kind, layer, i, j, src, dst)
        start_either(layer, near, far)

    def start_either(layer, near, far):
        @pl.when(s == layer)
        def _():
            near.start()

        @pl.when(s != layer)
        def _():
            far.start()

    def out_sent(kind, layer, i, j, src, dst):
        near, far = out_copy(kind, layer, i, j, src, dst)

        @pl.when(s == layer)
        def _():
            near.wait()

        @pl.when(s != layer)
        def _():
            far.wait_send()

    def out_arrived(kind, layer, dst):
        half = dst.at[pl.ds(0, 2)]

        @pl.when(s == layer)
        def _():
            copy(half, half, o_rcv.at[kind]).wait()

    def col_copy_f(i):
        return rcopy(colf_s.at[i], colf_r.at[i], cf_snd.at[i], cf_rcv.at[i], znext)

    def col_copy_b(i):
        return rcopy(colb_s.at[i], colb_r.at[i], cb_snd.at[i], cb_rcv.at[i], zprev)

    def pick_col(tile, lane):
        li = lax.broadcasted_iota(jnp.int32, (16, PW), 1)
        return dot_nt((li == lane).astype(F32).astype(BF), tile).astype(BF)

    def spread_col(rows):
        full = jnp.concatenate([rows] * (PW // 16), axis=0)
        parts = [
            dot_nt(eye[...], full[:, k * TC : (k + 1) * TC]) for k in range(C // TC)
        ]
        return jnp.concatenate(parts, axis=0)

    def fwd0(i, j, first=None):
        far = j >= HJ
        src_j = jnp.where(far, j - HJ, j)
        src_row = jnp.where(far, C, 0)
        mask = jnp.concatenate([mkb[0, i, j]] * (C // 16), axis=0)
        rh[0, i, j, pl.ds(0, C), :] = rh[0, i, src_j, rows_at(src_row, C, C), :] * mask
        parts = gate(0, i, j)
        for g in range(2):
            gb[0, i, j, pl.ds(g * TC, TC), :] = parts[g][0].astype(BF)
            gb[0, i, j, pl.ds(C + g * TC, TC), :] = parts[g][1].astype(BF)
        if first is not None:

            @pl.when(jnp.logical_and(first, s == 1))
            def _():
                for c in far_w[6:]:
                    c.wait_recv()

        rs = dot(wrs[0, pl.ds(0, C)], hid[0, i, j]) + wide(rsbias[0, pl.ds(0, C)])
        x1 = (rh[0, i, j, pl.ds(C, C), :].astype(F32) + rs).astype(BF)
        rh[1, i, j, pl.ds(C, C), :] = x1
        rh[1, i, j, pl.ds(G, KC), :] = rh[0, i, j, pl.ds(G, KC), :]
        out_start(0, 0, i, j, rh.at[1, i, j, pl.ds(C, C)], res_out)

        @pl.when(jnp.logical_and(j == NJ - 1, has_next))
        def _():
            colf_s[i] = pick_col(rh[1, i, j, pl.ds(C, C), pl.ds(TC - PW, PW)], PW - 1)
            col_copy_f(i).start()

    lane_c = lax.broadcasted_iota(jnp.int32, (C, PW), 1)

    def layer1(i, j):
        x1 = rh[1, i, j, pl.ds(C, C), :].astype(F32)
        jm = jnp.maximum(j - 1, 0)
        tile = rh[1, i, jm, pl.ds(C, C), pl.ds(TC - PW, PW)].astype(F32)
        tile = jnp.where(j == 0, htile[i].astype(F32), tile)
        turned = pltpu.roll(x1, 1, 1)
        first = jnp.where(lane_c == 0, pltpu.roll(tile, 1, 1), turned[:, :PW])
        shifted = jnp.concatenate([first, turned[:, PW:]], axis=1) * mkf[1, i, j, pl.ds(0, 1), :]
        rh[1, i, j, pl.ds(0, C), :] = shifted.astype(BF)
        gh = gb[1, i, j, pl.ds(0, C), :].astype(F32) + gb[1, i, j, pl.ds(C, C), :].astype(F32)
        parts = gate(1, i, j)
        for g in range(2):
            part = gh[g * TC : (g + 1) * TC]
            gb[1, i, j, pl.ds(g * TC, TC), :] = (part * parts[g][0]).astype(BF)
            gb[1, i, j, pl.ds(C + g * TC, TC), :] = (part * parts[g][1]).astype(BF)

    def layer1_back(i, j):
        dg = dot(wct[1], gb[1, i, j])
        past = dg[:C] * mkf[1, i, j, pl.ds(0, 1), :]
        turned = pltpu.roll(past, TC - 1, 1)
        last = jnp.where(lane_c == PW - 1, pltpu.roll(bcar[i].astype(F32), PW - 1, 1), turned[:, TC - PW :])
        back = jnp.concatenate([turned[:, : TC - PW], last], axis=1)
        gres = (gr[1, i, j].astype(F32) + dg[C:G] + back).astype(BF)
        gr[0, i, j] = gres
        add_sum(2, gres)
        bcar[i] = past[:, :PW].astype(BF)
        cg[i, j] = dg[G : G + KC]

        @pl.when(jnp.logical_and(j == 0, has_prev))
        def _():
            colb_s[i] = pick_col(past[:, :PW].astype(BF), 0)
            col_copy_b(i).start()

    def phase_near():
        @pl.loop(0, 2 * (NJ - HJ))
        def _(n):
            fwd0(n // (NJ - HJ), NJ - 1 - lax.rem(n, NJ - HJ), n == 0)

    phase_near()
    halo_start(1)

    @pl.when(s == 0)
    def _():
        for c in far_w:
            c.wait_recv()
        prepare_forward(1)

    mix_w.wait_recv()

    @pl.when(s == 0)
    def _():
        mix_back()

    def phase_main():
        @pl.loop(0, 2 * NJ)
        def _(n):
            q = n - 2
            i = jnp.where(n < 2, n, q // (NJ - 1))
            j = jnp.where(n < 2, NJ - 1, NJ - 2 - lax.rem(q, NJ - 1))

            @pl.when(jnp.logical_and(n >= 2, j >= 1))
            def _():
                @pl.when(jnp.logical_and(has_prev, j <= HJ))
                def _():
                    halo(i, j - 1).wait_recv()

                fwd0(i, j - 1)

            @pl.when(jnp.logical_and(j == 0, has_prev))
            def _():
                col_copy_f(i).wait_recv()
                htile[i] = spread_col(colf_r[i]).astype(BF)

            layer1(i, j)

    phase_main()

    sizes = [G, G, G, G, G, G, cr]
    offs = [G * k for k in range(7)]
    SKIP, RES, COND = 4, 5, 6
    ARA, ARB, ARZ, ARM, AGZ, AGB, AGA = range(7)

    def geo(p):
        size, off = sizes[p], offs[p]
        na, nb_ = size // r, size // (r * r)
        base_a = off + amem * na
        base_b = base_a + bmem * nb_
        return size, off, na, nb_, base_a, base_b

    def x_copy(layer, p):
        return rcopy(
            pb.at[0, pl.ds(offs[p], sizes[p])],
            prv.at[pl.ds(offs[p], sizes[p])],
            x_snd.at[layer, p],
            x_rcv.at[layer, p],
            other,
        )

    def gathered(layer, rows):
        return ag1.at[rows] if layer == 1 else pb.at[0, rows]

    def wait_rows(count, sem, layer):
        ref = pb.at[1 + layer, pl.ds(0, count)]
        copy(ref, ref, sem).wait()

    def sum_rows(layer, start, count, parts):
        total = pb[1 + layer, rows_at(start, count, 16), :].astype(F32)
        for part in parts:
            total = total + part.astype(F32)
        return total.astype(BF)

    def add_rows(layer, start, count, parts):
        pb[1 + layer, rows_at(start, count, 16), :] = sum_rows(layer, start, count, parts)

    def step0(layer, p):
        size, off, na, nb_, base_a, base_b = geo(p)
        x_copy(layer, p).wait()
        add_rows(layer, off, size, [prv[pl.ds(off, size), :]])
        if layer == 1:
            pl.semaphore_signal(credit.at[p], inc=1, device_id=other, device_id_type=MESH)
        for o in range(1, r):
            a2, dev = sa_dev(o)
            rcopy(
                pb.at[1 + layer, rows_at(off + a2 * na, na, 16)],
                ra_buf.at[layer, o - 1, pl.ds(off // r, na)],
                ar_snd.at[ARA, layer, p],
                ar_rcv.at[ARA, layer, p],
                dev,
            ).start()

    def step1(layer, p):
        size, off, na, nb_, base_a, base_b = geo(p)
        wait_rows((r - 1) * na, ar_rcv.at[ARA, layer, p], layer)
        wait_rows((r - 1) * na, ar_snd.at[ARA, layer, p], layer)
        add_rows(
            layer, base_a, na, [ra_buf[layer, o, pl.ds(off // r, na), :] for o in range(r - 1)]
        )
        for o in range(1, r):
            b2, dev = sb_dev(o)
            rcopy(
                pb.at[1 + layer, rows_at(base_a + b2 * nb_, nb_, 16)],
                rb_buf.at[layer, o - 1, pl.ds(off // (r * r), nb_)],
                ar_snd.at[ARB, layer, p],
                ar_rcv.at[ARB, layer, p],
                dev,
            ).start()

    def step2(layer, p):
        size, off, na, nb_, base_a, base_b = geo(p)
        wait_rows((r - 1) * nb_, ar_rcv.at[ARB, layer, p], layer)
        wait_rows((r - 1) * nb_, ar_snd.at[ARB, layer, p], layer)
        add_rows(
            layer,
            base_b,
            nb_,
            [rb_buf[layer, o, pl.ds(off // (r * r), nb_), :] for o in range(r - 1)],
        )

        @pl.when(depth == 0)
        def _():
            inward(layer, p, hops == 1)

    def arrived(layer, p, slot):
        size, off, na, nb_, base_a, base_b = geo(p)
        return rz_buf.at[layer, slot, pl.ds(off // (r * r), nb_)]

    def inward(layer, p, at_middle):
        size, off, na, nb_, base_a, base_b = geo(p)
        stage = ARM if at_middle else ARZ
        rcopy(
            pb.at[1 + layer, rows_at(base_b, nb_, 16)],
            arrived(layer, p, int(at_middle)),
            ar_snd.at[stage, layer, p],
            ar_rcv.at[stage, layer, p],
            inner,
        ).start()

    def spread(layer, p, stage, start, count, devs):
        for dev in devs:
            rcopy(
                gathered(layer, rows_at(start, count, 16)),
                gathered(layer, rows_at(start, count, 16)),
                ar_snd.at[stage, layer, p],
                ar_rcv.at[stage, layer, p],
                dev,
            ).start()

    def step3(layer, p):
        size, off, na, nb_, base_a, base_b = geo(p)
        for k in range(1, hops):

            @pl.when(depth == k)
            def _():
                wait_rows(nb_, ar_rcv.at[ARZ, layer, p], layer)
                add_rows(layer, base_b, nb_, [arrived(layer, p, 0)[...]])
                inward(layer, p, k == hops - 1)

    def outward(layer, p):
        size, off, na, nb_, base_a, base_b = geo(p)
        spread(layer, p, AGZ, base_b, nb_, [outer])

    def share(layer, p):
        size, off, na, nb_, base_a, base_b = geo(p)
        spread(layer, p, AGB, base_b, nb_, [sb_dev(o)[1] for o in range(1, r)])

    def step4(layer, p):
        size, off, na, nb_, base_a, base_b = geo(p)

        @pl.when(depth == hops - 1)
        def _():
            wait_rows(nb_, ar_rcv.at[ARM, layer, p], layer)
            wait_rows(nb_, ar_snd.at[ARM, layer, p], layer)
            gathered(layer, rows_at(base_b, nb_, 16))[...] = sum_rows(
                layer, base_b, nb_, [arrived(layer, p, 1)[...]]
            )
            if hops > 1:
                outward(layer, p)
            share(layer, p)

    def step5(layer, p):
        size, off, na, nb_, base_a, base_b = geo(p)
        for k in reversed(range(hops - 1)):

            @pl.when(depth == k)
            def _():
                wait_rows(nb_, ar_rcv.at[AGZ, layer, p], layer)
                wait_rows(nb_, ar_snd.at[ARZ, layer, p], layer)
                if k > 0:
                    outward(layer, p)
                share(layer, p)

    def step6(layer, p):
        size, off, na, nb_, base_a, base_b = geo(p)
        wait_rows((r - 1) * nb_, ar_rcv.at[AGB, layer, p], layer)
        wait_rows((r - 1) * nb_, ar_snd.at[AGB, layer, p], layer)

        @pl.when(depth > 0)
        def _():
            wait_rows(nb_, ar_snd.at[AGZ, layer, p], layer)

        spread(layer, p, AGA, base_a, na, [sa_dev(o)[1] for o in range(1, r)])

    def final_copies(layer, p):
        src = gathered(layer, pl.ds(offs[p], sizes[p]))
        dst = wg_out.at[s, pl.ds(offs[p], sizes[p])]
        return (
            copy(src, dst, f_loc.at[p]),
            rcopy(src, dst, f_snd.at[p], f_rcv.at[p], other),
        )

    def step7(layer, p):
        size, off, na, nb_, base_a, base_b = geo(p)
        wait_rows((r - 1) * na, ar_rcv.at[AGA, layer, p], layer)
        wait_rows((r - 1) * na, ar_snd.at[AGA, layer, p], layer)
        near, far = final_copies(layer, p)

        @pl.when(s == layer)
        def _():
            near.start()

        @pl.when(s != layer)
        def _():
            far.start()

    steps = [step0, step1, step2, step3, step4, step5, step6, step7]

    def at(n, table):
        for k, todo in table.items():

            @pl.when(n == k)
            def _(todo=todo):
                for st, layer, p in todo:
                    steps[st](layer, p)

    def task_start(layer, mine, pieces):
        if layer == 0:

            @pl.when(mine == 0)
            def _():
                for p in pieces:
                    pl.semaphore_wait(credit.at[p], 1)

        return jnp.where(mine == 1, s, 1 - s), mine * (1 + layer)

    def task_end(layer, mine, pieces):
        @pl.when(mine == 0)
        def _():
            for p in pieces:
                x_copy(layer, p).start()

    def conv_tasks(layer, table):
        @pl.loop(0, 4)
        def _(n):
            k = n // 2
            mine = lax.rem(n, 2)
            half = jnp.where(mine == 1, s, 1 - s)
            dst = mine * (1 + layer)
            for kk in range(2):
                if layer == 0:

                    @pl.when(n == 2 * kk)
                    def _():
                        for p in (2 * kk, 2 * kk + 1):
                            pl.semaphore_wait(credit.at[p], 1)

            ch = rows_at(half * C + k * TC, TC, TC)
            total = dot_nt(gb[layer, 0, 0], rh[layer, 0, 0, ch, :])
            for i in range(2):
                for j in range(NJ):
                    if i + j > 0:
                        total = total + dot_nt(gb[layer, i, j], rh[layer, i, j, ch, :])
            total = total.astype(BF)
            pb[dst, rows_at(k * 2 * G, G, G), :] = total[:, :PW]
            pb[dst, rows_at(k * 2 * G + G, G, G), :] = total[:, PW:]
            for kk in range(2):

                @pl.when(n == 2 * kk)
                def _():
                    for p in (2 * kk, 2 * kk + 1):
                        x_copy(layer, p).start()

            at(n, table)

    def mix_tasks(layer, piece, src, table):
        @pl.loop(0, 2)
        def _(n):
            half, dst = task_start(layer, n, [piece])
            ch = rows_at(half * TC, TC, TC)
            total = dot_nt(src(0, 0), hid[layer, 0, 0, ch, :])
            for i in range(2):
                for j in range(NJ):
                    if i + j > 0:
                        total = total + dot_nt(src(i, j), hid[layer, i, j, ch, :])
            total = total.astype(BF)
            pb[dst, pl.ds(offs[piece], C), :] = total[:, :PW]
            pb[dst, pl.ds(offs[piece] + C, C), :] = total[:, PW:]
            task_end(layer, n, [piece])
            at(n, table)

    def cond_tasks(layer, table):
        @pl.loop(0, 2)
        def _(n):
            half, dst = task_start(layer, n, [COND])
            gp_rows = rows_at(half * C, C, C)
            total = jnp.zeros((PW, C), F32)
            for i in range(2):
                for j in range(NJ):
                    total = total + dot_nt(
                        rh[layer, i, j, pl.ds(G, PW), :], gb[layer, i, j, gp_rows, :]
                    )
            cacc[...] = total
            which = jnp.where(half == 1, 1, 2 - 2 * layer)
            cacc[pl.ds(KC + 3, 1), :] = jnp.sum(bsum[which].T, axis=0, keepdims=True)
            for k in range(C // PW):
                pb[dst, pl.ds(offs[COND] + k * CROWS, CROWS), :] = cacc[
                    pl.ds(0, CROWS), k * PW : (k + 1) * PW
                ].astype(BF)
            if cr > 4 * CROWS:
                pb[dst, pl.ds(offs[COND] + 4 * CROWS, cr - 4 * CROWS), :] = jnp.zeros(
                    (cr - 4 * CROWS, PW), BF
                )
            task_end(layer, n, [COND])
            at(n, table)

    def fix_last(i):
        @pl.when(has_next)
        def _():
            col_copy_b(i).wait_recv()
            tile = gr[0, i, NJ - 1, :, pl.ds(TC - PW, PW)].astype(F32)
            add = jnp.where(lane_c == PW - 1, spread_col(colb_r[i]), 0.0)
            bsum[2] = bsum[2] + add
            gr[0, i, NJ - 1, :, pl.ds(TC - PW, PW)] = (tile + add).astype(BF)

    def skip_src(i, j):
        return cs[i, j]

    def phase_w1():
        conv_tasks(1, T_W1C)
        mix_tasks(1, SKIP, skip_src, T_SK1)
        mix_tasks(1, RES, lambda i, j: gr[1, i, j], T_RE1)
        cond_tasks(1, T_CO1)
        mix_tasks(0, SKIP, skip_src, T_SK0)

    phase_w1()

    def run_steps(todo):
        for st, layer, p in todo:
            steps[st](layer, p)

    conv_w.wait_recv()

    def phase_l1b():

        @pl.loop(0, 2 * NJ)
        def _(n):
            layer1_back(n // NJ, NJ - 1 - lax.rem(n, NJ))
            at(n, T_L1B)

    phase_l1b()

    def hb_copy(i, j):
        return rcopy(hs.at[i, j], hb.at[i, j], hb_snd.at[i, j], hb_rcv.at[i, j], zprev)

    def back0(i, j):
        gh = dot(wrst[0], jnp.concatenate([gr[0, i, j], cs[i, j]], axis=0))
        for g in range(2):
            part = gh[g * TC : (g + 1) * TC]
            for row in (g * TC, C + g * TC):
                rows = pl.ds(row, TC)
                gb[0, i, j, rows, :] = (part * gb[0, i, j, rows, :].astype(F32)).astype(BF)

    def grad0(i, j):
        dg = dot(wct[0], gb[0, i, j])
        past = dg[:C] * mkf[0, i, j, pl.ds(0, 1), :]
        gr[1, i, j] = (gr[0, i, j].astype(F32) + dg[C:G]).astype(BF)
        cg[i, j] = cg[i, j] + dg[G : G + KC]
        m = 2 * s + i
        cols = rows_at(j * TC, TC, TC)
        hc = KC // 2
        copy(
            cg.at[i, j, rows_at(s * hc, hc, 8)], cgrad_out.at[m, :, cols], c_loc.at[0]
        ).start()
        rcopy(
            cg.at[i, j, rows_at((1 - s) * hc, hc, 8)],
            cgrad_out.at[m, :, cols],
            c_loc.at[1],
            c_loc.at[2],
            other,
        ).start()
        return past

    def phase_b0a():
        @pl.loop(0, 2 * HJ)
        def _(n):
            back0(n // HJ, lax.rem(n, HJ))
            at(n, T_B0A)

    phase_b0a()

    for i in range(2):
        fix_last(i)
        for j in range(NJ):
            out_start(4, 1, i, j, gr.at[0, i, j], rgrad_out)

    def phase_b0b():
        @pl.loop(0, 2 * (NJ - HJ))
        def _(n):
            back0(n // (NJ - HJ), HJ + lax.rem(n, NJ - HJ))
            at(n, T_B0B)

    phase_b0b()

    def phase_gh():
        @pl.loop(0, 2 * HJ)
        def _(n):
            i, j = n // HJ, lax.rem(n, HJ)
            past = grad0(i, j)

            @pl.when(has_prev)
            def _():
                hs[i, j] = past.astype(BF)
                hb_copy(i, j).start()

            at(n, T_GH)

    phase_gh()

    def phase_re0():
        mix_tasks(0, RES, lambda i, j: gr[0, i, j], T_RE0)

    phase_re0()

    def phase_w0():
        conv_tasks(0, T_W0C)
        cond_tasks(0, T_CO0)

    phase_w0()

    def phase_g0():
        @pl.loop(0, 2 * (NJ - HJ))
        def _(n):
            i, k = n // (NJ - HJ), lax.rem(n, NJ - HJ)
            past = grad0(i, HJ + k)
            gr[1, i, k] = (gr[1, i, k].astype(F32) + past).astype(BF)
            out_start(5, 0, i, k, gr.at[1, i, k], rgrad_out)
            at(n, T_G0)

    phase_g0()

    def phase_rs():
        @pl.loop(0, 2 * NJ)
        def _(n):
            i, j = n // NJ, lax.rem(n, NJ)
            x1 = rh.at[1, i, j, pl.ds(C, C)]
            sk0 = rh.at[1, i, j, pl.ds(0, C)]
            sk1 = hid.at[1, i, j]
            skip = dot(wrs[0, pl.ds(C, C)], hid[0, i, j]) + wide(rsbias[0, pl.ds(C, C)])
            skip = skip.astype(BF)
            sk0[...] = skip
            out_start(1, 0, i, j, sk0, skip_out)
            rs = dot(wrs[1], sk1[...]) + wide(rsbias[1])
            sk1[...] = (skip.astype(F32) + rs[C:]).astype(BF)
            out_start(3, 1, i, j, sk1, skip_out)
            out_sent(0, 0, i, j, x1, res_out)
            x1[...] = (x1[...].astype(F32) + rs[:C]).astype(BF)
            out_start(2, 1, i, j, x1, res_out)
            at(n, T_RS)

    phase_rs()

    def phase_tail():
        run_steps(TAIL)

    phase_tail()

    for i in range(2):
        for k in range(HJ):
            j = NJ - HJ + k

            @pl.when(has_next)
            def _():
                hb_copy(i, k).wait_recv()
                gr[1, i, j] = (gr[1, i, j].astype(F32) + hb[i, k].astype(F32)).astype(BF)

            out_start(5, 0, i, j, gr.at[1, i, j], rgrad_out)

    def phase_last():
        run_steps(LAST)

    phase_last()

    @pl.loop(0, 2 * NJ)
    def _(n):
        i, j = n // NJ, lax.rem(n, NJ)
        blk = gr.at[0, i, j]
        out_sent(1, 0, i, j, blk, skip_out)
        out_sent(2, 1, i, j, blk, res_out)
        out_sent(3, 1, i, j, blk, skip_out)
        out_sent(4, 1, i, j, blk, rgrad_out)
        out_sent(5, 0, i, j, blk, rgrad_out)

    out_arrived(0, 0, res_out)
    out_arrived(1, 0, skip_out)
    out_arrived(2, 1, res_out)
    out_arrived(3, 1, skip_out)
    out_arrived(4, 1, rgrad_out)
    out_arrived(5, 0, rgrad_out)
    half = cgrad_out.at[pl.ds(0, 2)]
    for k in range(3):
        copy(half, half, c_loc.at[k]).wait()
    for p in range(7):
        near, far = final_copies(0, p)
        near.wait()
        far.wait()
    for c in far_w + [mix_w, conv_w]:
        c.wait_send()

    @pl.when(has_next)
    def _():
        for i in range(2):
            for j in range(HJ):
                halo(i, j).wait_send()
            col_copy_f(i).wait_send()

    @pl.when(has_prev)
    def _():
        for i in range(2):
            col_copy_b(i).wait_send()
            for j in range(HJ):
                hb_copy(i, j).wait_send()


def finalize(
    res, skip, rgrad, cgrad, wg,
    res_o, skip_o, rgrad_o, cgrad_o, conv_o, convb_o, condw_o, resw_o, resb_o, skipw_o, skipb_o,
    rbuf, sbuf, cbuf, rin, rwide, win, convf, mixf, condf, cbf, rbf, sbf, sem_in, sem_cp, sem_out,
):
    M, C, TL = res.shape
    G = 2 * C
    KC = condw_o.shape[0]
    copies = []
    loads = [pltpu.make_async_copy(wg.at[h], win.at[h], sem_in.at[h]) for h in range(2)]
    reads = [pltpu.make_async_copy(rgrad.at[m], rin.at[m], sem_in.at[2 + m]) for m in range(M)]
    for c in loads + reads:
        c.start()
    passing = []
    for k, (a, buf, o) in enumerate(
        ((res, rbuf, res_o), (skip, sbuf, skip_o), (cgrad, cbuf, cgrad_o))
    ):
        for m in range(M):
            c = pltpu.make_async_copy(a.at[m], buf.at[m], sem_cp.at[k, m])
            c.start()
            passing.append((c, buf.at[m], o.at[m], 8 + M + k * M + m))

    def put(src, dst, k):
        c = pltpu.make_async_copy(src, dst, sem_out.at[k])
        c.start()
        copies.append(c)

    for h in range(2):
        loads[h].wait()
        for q in range(C // PW):
            convf[h, :, q * PW : (q + 1) * PW] = win[h, pl.ds(q * G, G), :].astype(F32)
        put(convf.at[h], conv_o.at[h], h)
        for q in range(2):
            lanes = slice(h * 2 * PW + q * PW, h * 2 * PW + (q + 1) * PW)
            mixf[pl.ds(0, C), lanes] = win[h, pl.ds(5 * G + q * C, C), :].astype(F32)
            mixf[pl.ds(C, C), lanes] = win[h, pl.ds(4 * G + q * C, C), :].astype(F32)
        for q in range(C // PW):
            blk = win[h, pl.ds(6 * G + q * CROWS, CROWS), :].astype(F32)
            lanes = slice(h * C + q * PW, h * C + (q + 1) * PW)
            condf[:, lanes] = blk[:KC]
            cbf[:, lanes] = blk[KC : KC + 1]
            (sbf if h else rbf)[:, q * PW : (q + 1) * PW] = blk[KC + 3 : KC + 4]
    put(mixf.at[pl.ds(0, C)], resw_o, 2)
    put(mixf.at[pl.ds(C, C)], skipw_o, 3)
    put(condf, condw_o, 4)
    put(cbf, convb_o, 5)
    put(rbf, resb_o, 6)
    put(sbf, skipb_o, 7)
    for c, src, dst, k in passing:
        c.wait()
        put(src, dst, k)
    for m in range(M):
        reads[m].wait()
        rwide[m] = rin[m].astype(F32)
        put(rwide.at[m], rgrad_o.at[m], 8 + m)
    for c in copies:
        c.wait()


def local(nz, r, *args):
    audio, cond = args[0], args[1]
    M, _, C, TL = audio.shape
    KC = cond.shape[2]
    G = 2 * C
    NJ = TL // TC
    HJ = REACH0 // TC
    KP = G + PW
    cr = -(-4 * CROWS // (16 * r * r)) * 16 * r * r
    HR = 6 * G + cr
    any_ = pl.BlockSpec(memory_space=pl.ANY)
    smem = pl.BlockSpec(memory_space=pltpu.SMEM)
    V = pltpu.VMEM
    D = pltpu.SemaphoreType.DMA
    scratch = [
        V((2, G, KP), BF),
        V((2, G, C), BF),
        V((2, KP, G), BF),
        V((2, C, G), BF),
        V((2, 1, G), F32),
        V((2, 1, C), F32),
        V((2, 1, C), F32),
        V((2, G, PW), F32),
        V((2, 2, NJ, KP, TC), BF),
        V((2, 2, NJ, C, TC), BF),
        V((2, 2, NJ, G, TC), BF),
        V((2, 2, NJ, C, TC), BF),
        V((2, NJ, C, TC), BF),
        V((HR, PW), BF),
        V((2, NJ, KC, TC), F32),
        V((TC, TC), BF),
        V((3, C, PW), F32),
        V((2, 2, NJ, 8, TC), F32),
        V((2, 2, NJ, 16, TC), BF),
        V((2, C, PW), BF),
        V((2, C, PW), BF),
        V((2, 16, C), BF),
        V((2, 16, C), BF),
        V((2, 16, C), BF),
        V((2, 16, C), BF),
        V((2, HJ, C, TC), BF),
        V((2, HJ, C, TC), BF),
        V((3, HR, PW), BF),
        V((HR, PW), BF),
        V((2, r - 1, HR // r, PW), BF),
        V((2, r - 1, HR // (r * r), PW), BF),
        V((2, 2, HR // (r * r), PW), BF),
        V((PW, C), F32),
        D((8,)),
        D((2, NJ)),
        D((2, NJ)),
        D((2, NJ)),
        D((2, NJ)),
        D((8,)),
        D((8,)),
        D((2,)),
        D((2,)),
        D((2, HJ)),
        D((2, HJ)),
        D((2,)),
        D((2,)),
        D((2,)),
        D((2,)),
        D((2, HJ)),
        D((2, HJ)),
        D((6, 2, NJ)),
        D((6, 2, NJ)),
        D((6,)),
        D((3,)),
        D((2, 7)),
        D((2, 7)),
        D((7, 2, 7)),
        D((7, 2, 7)),
        D((7,)),
        D((7,)),
        D((7,)),
        pltpu.SemaphoreType.REGULAR((7,)),
    ]
    res, skip, rgrad, cgrad, wg = pl.pallas_call(
        functools.partial(kernel, nz, r, cr),
        out_shape=(
            jax.ShapeDtypeStruct((M, C, TL), BF),
            jax.ShapeDtypeStruct((M, C, TL), BF),
            jax.ShapeDtypeStruct((M, C, TL), BF),
            jax.ShapeDtypeStruct((M, KC // 2, TL), F32),
            jax.ShapeDtypeStruct((2, HR, PW), BF),
        ),
        in_specs=[any_, any_, smem] + [any_] * 9,
        out_specs=(any_,) * 5,
        scratch_shapes=scratch,
        compiler_params=pltpu.CompilerParams(
            collective_id=0, has_side_effects=True, vmem_limit_bytes=64 * 2**20 - 2**17
        ),
        cost_estimate=pl.CostEstimate(
            flops=40 * 10**9, bytes_accessed=36 * 10**6, transcendentals=4 * 10**6
        ),
    )(*args[:5], jnp.swapaxes(args[5], 1, 2), *args[6:])
    shapes = [
        ((M, C, TL), BF),
        ((M, C, TL), BF),
        ((M, C, TL), F32),
        ((M, KC // 2, TL), F32),
        ((2, G, C), F32),
        ((1, G), F32),
        ((KC, G), F32),
        ((C, C), F32),
        ((1, C), F32),
        ((C, C), F32),
        ((1, C), F32),
    ]
    done = pl.pallas_call(
        finalize,
        out_shape=tuple(jax.ShapeDtypeStruct(a, d) for a, d in shapes),
        in_specs=[any_] * 5,
        out_specs=(any_,) * len(shapes),
        scratch_shapes=[
            V((M, C, TL), BF),
            V((M, C, TL), BF),
            V((M, KC // 2, TL), F32),
            V((M, C, TL), BF),
            V((M, C, TL), F32),
            V((2, HR, PW), BF),
            V((2, G, C), F32),
            V((G, C), F32),
            V((KC, G), F32),
            V((1, G), F32),
            V((1, C), F32),
            V((1, C), F32),
            D((2 + M,)),
            D((3, M)),
            D((8 + 4 * M,)),
        ],
        compiler_params=pltpu.CompilerParams(vmem_limit_bytes=64 * 2**20 - 2**17),
    )(res, skip, rgrad, cgrad, wg)
    out = [v[None] for v in done]
    out[0], out[1], out[2] = (done[k][None, :, None] for k in range(3))
    out[3] = done[3][:, None]
    out[5], out[8], out[10] = done[5], done[8], done[10]
    out[6] = jnp.swapaxes(out[6], 1, 2)
    return tuple(out)


def solution(mesh):
    nz = mesh.shape["tm"]
    r = math.isqrt(mesh.shape["batch"])
    in_specs = (
        P(None, "batch", None, "tm"),
        P(None, "batch", None, "tm"),
        P(None, "batch", None),
        P("section", None, None, None),
        P("section", None),
        P("section", None, None),
        P("section", None, None),
        P("section", None),
        P("section", None, None),
        P("section", None),
        P(None, "batch", None, "tm"),
        P(None, "batch", None, "tm"),
    )
    out_specs = (
        P("section", None, "batch", None, "tm"),
        P("section", None, "batch", None, "tm"),
        P("section", None, "batch", None, "tm"),
        P(None, "batch", "section", "tm"),
        P("section", None, None, None),
        P("section", None),
        P("section", None, None),
        P("section", None, None),
        P("section", None),
        P("section", None, None),
        P("section", None),
    )
    return jax.shard_map(
        functools.partial(local, nz, r),
        mesh=mesh,
        in_specs=in_specs,
        out_specs=out_specs,
        check_vma=False,
    )
```

```python
import functools
import math

import jax
import jax.numpy as jnp
from jax import lax
from jax.experimental import pallas as pl
from jax.experimental.pallas import tpu as pltpu
from jax.sharding import PartitionSpec as P

REACH0 = 512
TC = 256
MESH = pl.DeviceIdType.MESH
BF = jnp.bfloat16
F32 = jnp.float32
PW = 128
CROWS = 96


T_W1C = {0: [(0, 1, 5)], 1: [(0, 1, 0), (0, 1, 1)], 3: [(0, 1, 2), (0, 1, 3)]}
T_SK1 = {0: [(2, 1, 2)], 1: [(2, 1, 3), (0, 1, 4)]}
T_RE1 = {}
T_CO1 = {0: [(2, 1, 1)], 1: [(0, 1, 6)]}
T_SK0 = {}
T_L1B = {1: [(1, 1, 5)], 3: [(1, 1, 0)], 5: [(1, 1, 1)], 7: [(1, 1, 2)]}
T_B0A = {2: [(1, 1, 3)], 3: [(2, 1, 5)]}
T_B0B = {0: [(3, 1, 5)]}
T_GHA = {1: [(3, 1, 0), (1, 1, 4)]}
T_GHB = {0: [(2, 1, 0)]}
T_RE0 = {0: [(1, 1, 6)], 1: [(0, 0, 5)]}
T_W0C = {0: [(2, 1, 6), (0, 0, 4)], 1: [(4, 1, 5), (0, 0, 0), (0, 0, 1)], 2: [(1, 0, 5), (3, 1, 1), (2, 1, 4)], 3: [(3, 1, 2), (0, 0, 2), (0, 0, 3)]}
T_CO0 = {0: [(3, 1, 3)], 1: [(1, 0, 4), (0, 0, 6)]}
T_G0 = {1: [(1, 0, 0)], 2: [(1, 0, 1)], 3: [(2, 0, 5)]}
T_RS = {1: [(1, 0, 2)], 3: [(1, 0, 3), (4, 1, 0), (5, 1, 5), (2, 0, 4)], 4: [(1, 0, 6), (4, 1, 1)], 6: [(2, 0, 0), (4, 1, 2)], 7: [(3, 1, 6), (2, 0, 1)]}
TAIL = [(4, 1, 3), (3, 1, 4), (2, 0, 2), (3, 0, 5), (2, 0, 3), (6, 1, 5), (5, 1, 0), (3, 0, 4), (2, 0, 6), (5, 1, 1), (4, 1, 6), (3, 0, 0), (5, 1, 2), (4, 1, 4), (3, 0, 1), (5, 1, 3), (7, 1, 5), (4, 0, 5), (3, 0, 2), (6, 1, 0), (6, 1, 1), (5, 1, 6), (4, 0, 4), (3, 0, 3), (6, 1, 2), (3, 0, 6), (4, 0, 0), (6, 1, 3), (5, 1, 4), (4, 0, 1), (5, 0, 5), (7, 1, 0), (4, 0, 2), (5, 0, 4), (7, 1, 1), (6, 1, 6), (4, 0, 3), (4, 0, 6), (5, 0, 0), (7, 1, 2), (5, 0, 1), (7, 1, 3), (6, 1, 4), (5, 0, 2), (6, 0, 5), (6, 0, 4), (5, 0, 3), (7, 1, 6), (5, 0, 6), (6, 0, 0), (6, 0, 1), (7, 1, 4), (6, 0, 2), (7, 0, 5), (7, 0, 4), (6, 0, 3), (6, 0, 6), (7, 0, 0)]
LAST = [(7, 0, 1), (7, 0, 2), (7, 0, 3), (7, 0, 6)]
ORDER = ['RE1', 'W1C', 'L1B', 'B0A', 'GHB', 'CO1', 'SK1', 'FIX', 'B0B', 'RE0', 'GHA', 'SK0', 'W0C', 'CO0']


def dot(a, b):
    return jnp.dot(a, b, preferred_element_type=F32)


def dot_nt(a, b):
    return lax.dot_general(a, b, (((1,), (1,)), ((), ())), preferred_element_type=F32)


def rows_at(start, size, step):
    return pl.ds(pl.multiple_of(start, step), size)


def kernel(
    nz,
    r,
    cr,
    audio,
    cond,
    clips,
    convw,
    convb,
    condw,
    resw,
    resb,
    skipw,
    skipb,
    cotr,
    cots,
    res_out,
    skip_out,
    rgrad_out,
    cgrad_out,
    wg_out,
    wcat,
    wrs,
    wct,
    wrst,
    cbraw,
    rbraw,
    sbraw,
    rsbias,
    rh,
    hid,
    gb,
    gr,
    cs,
    ag1,
    cg,
    eye,
    bsum,
    mkf,
    mkb,
    htile,
    bcar,
    colf_s,
    colf_r,
    colb_s,
    colb_r,
    hs,
    hb,
    pb,
    prv,
    ra_buf,
    rb_buf,
    rz_buf,
    cacc,
    ld_w,
    ld_x,
    ld_c,
    ld_r,
    ld_s,
    w_snd,
    w_rcv,
    t_snd,
    t_rcv,
    h_snd,
    h_rcv,
    cf_snd,
    cf_rcv,
    cb_snd,
    cb_rcv,
    hb_snd,
    hb_rcv,
    o_loc,
    o_snd,
    o_rcv,
    c_loc,
    x_snd,
    x_rcv,
    ar_snd,
    ar_rcv,
    f_loc,
    f_snd,
    f_rcv,
    credit,
):
    C = audio.shape[2]
    TL = audio.shape[3]
    KC = cond.shape[2]
    NJ = TL // TC
    HJ = REACH0 // TC
    G = 2 * C
    KP = rh.shape[3]
    HR = pb.shape[1]
    s = lax.axis_index("section")
    b = lax.axis_index("batch")
    z = lax.axis_index("tm")
    other = (1 - s, b, z)
    zprev = (s, b, z - 1)
    znext = (s, b, z + 1)
    has_prev = z > 0
    has_next = z < nz - 1

    def copy(src, dst, sem):
        return pltpu.make_async_copy(src, dst, sem)

    def rcopy(src, dst, ssem, rsem, dev):
        return pltpu.make_async_remote_copy(
            src_ref=src, dst_ref=dst, send_sem=ssem, recv_sem=rsem, device_id=dev, device_id_type=MESH
        )

    def weight_pairs(layer):
        return [
            (convw.at[0, 0], wcat.at[layer, :, pl.ds(0, C)]),
            (convw.at[0, 1], wcat.at[layer, :, pl.ds(C, C)]),
            (condw.at[0], wct.at[layer, pl.ds(G, KC)]),
            (convb, cbraw.at[layer]),
            (resb, rbraw.at[layer]),
            (skipb, sbraw.at[layer]),
            (resw.at[0], wrs.at[layer, pl.ds(0, C)]),
            (skipw.at[0], wrs.at[layer, pl.ds(C, C)]),
        ]

    own_w = [copy(a, d, ld_w.at[k]) for k, (a, d) in enumerate(weight_pairs(s))]
    for c in own_w:
        c.start()
    ldx, ldc, ldr, lds = [], [], [], []
    for i in range(2):
        for j in reversed(range(NJ)):
            cols = pl.ds(j * TC, TC)
            m = 2 * s + i
            ldx.append(copy(audio.at[m, 0, :, cols], rh.at[0, i, j, pl.ds(C, C)], ld_x.at[i, j]))
            ldc.append(copy(cond.at[m, 0, :, cols], rh.at[0, i, j, pl.ds(G, KC)], ld_c.at[i, j]))
            ldr.append(copy(cotr.at[m, 0, :, cols], gr.at[1, i, j], ld_r.at[i, j]))
            lds.append(copy(cots.at[m, 0, :, cols], cs.at[i, j], ld_s.at[i, j]))
    for c in ldx + ldc + ldr + lds:
        c.start()

    bar = pltpu.get_barrier_semaphore()

    def sa_dev(o):
        a2 = lax.rem(amem + o, r)
        return a2, (s, jnp.where(s == 0, bhi * r + a2, a2 * r + blo), z)

    def sb_dev(o):
        b2 = lax.rem(bmem + o, r)
        return b2, (s, jnp.where(s == 0, b2 * r + blo, bhi * r + b2), z)

    hops = nz // 2
    left = z < hops
    depth = jnp.where(left, z, nz - 1 - z)
    inner = (s, b, jnp.where(left, z + 1, z - 1))
    outer = (s, b, jnp.where(left, z - 1, z + 1))

    bhi = b // r
    blo = lax.rem(b, r)
    amem = jnp.where(s == 0, blo, bhi)
    bmem = jnp.where(s == 0, bhi, blo)
    peers = [other]
    peers += [sa_dev(o)[1] for o in range(1, r)]
    peers += [sb_dev(o)[1] for o in range(1, r)]
    for dev in peers:
        pl.semaphore_signal(bar, inc=1, device_id=dev, device_id_type=MESH)

    @pl.when(has_prev)
    def _():
        pl.semaphore_signal(bar, inc=1, device_id=zprev, device_id_type=MESH)

    @pl.when(has_next)
    def _():
        pl.semaphore_signal(bar, inc=1, device_id=znext, device_id_type=MESH)

    greetings = len(peers) + has_prev.astype(jnp.int32) + has_next.astype(jnp.int32)

    ri = lax.broadcasted_iota(jnp.int32, (TC, TC), 0)
    ci = lax.broadcasted_iota(jnp.int32, (TC, TC), 1)
    eye[...] = (ri == ci).astype(F32).astype(BF)
    bsum[...] = jnp.zeros(bsum.shape, F32)
    bcar[...] = jnp.zeros(bcar.shape, BF)
    rk = lax.broadcasted_iota(jnp.int32, (KP - G - KC, TC), 0)
    ones_rows = (rk < 3).astype(F32).astype(BF)
    for i in range(2):
        m = 2 * s + i
        for j in range(NJ):
            rh[0, i, j, pl.ds(G + KC, KP - G - KC), :] = ones_rows
            rh[1, i, j, pl.ds(G + KC, KP - G - KC), :] = ones_rows
            pos = z * TL + j * TC + lax.broadcasted_iota(jnp.int32, (16, TC), 1)
            start = jnp.zeros((16, TC), jnp.int32)
            end = jnp.int32(0)
            for k in range(clips.shape[2]):
                end = end + clips[m, 0, k]
                start = jnp.where(end <= pos, end, start)
            for layer, reach in ((0, REACH0), (1, 1)):
                keep = jnp.where(pos - reach >= start, 1.0, 0.0).astype(F32)
                mkf[layer, i, j] = keep[:8]
                mkb[layer, i, j] = keep.astype(BF)

    @pl.when(jnp.logical_not(has_prev))
    def _():
        for i in range(2):
            for j in range(HJ):
                rh[0, i, j, pl.ds(0, C), :] = jnp.zeros((C, TC), BF)
            htile[i] = jnp.zeros((C, PW), BF)


    tail_rows = KP - G - KC

    def prepare_forward(layer):
        row = lax.broadcasted_iota(jnp.int32, (tail_rows, G), 0)
        bias = jnp.broadcast_to(cbraw[layer], (tail_rows, G))
        hi = bias.astype(BF).astype(F32)
        mid = (bias - hi).astype(BF).astype(F32)
        low = (bias - hi) - mid
        part = jnp.where(row == 0, hi, jnp.where(row == 1, mid, jnp.where(row == 2, low, 0.0)))
        wct[layer, pl.ds(G + KC, tail_rows), :] = part.astype(BF)
        for k in range(G // TC):
            wcat[layer, pl.ds(k * TC, TC), pl.ds(G, PW)] = dot_nt(
                eye[...], wct[layer, pl.ds(G, PW), pl.ds(k * TC, TC)]
            ).astype(BF)
        rsbias[layer, pl.ds(0, C)] = jnp.broadcast_to(rbraw[layer], (PW, C)).T
        rsbias[layer, pl.ds(C, C)] = jnp.broadcast_to(sbraw[layer], (PW, C)).T

    def prepare_mix(layer):
        @pl.loop(0, C // TC)
        def _(k):
            cols = rows_at(k * TC, TC, TC)
            wrst[layer, cols, :] = dot_nt(eye[...], wrs[layer, :, cols]).astype(BF)

    def prepare_conv(layer):
        @pl.loop(0, G // TC)
        def _(k):
            cols = rows_at(k * TC, TC, TC)
            wct[layer, cols, :] = dot_nt(eye[...], wcat[layer, :, cols]).astype(BF)

    for c in own_w:
        c.wait()

    prepare_forward(s)
    prepare_mix(s)
    pl.semaphore_wait(bar, greetings)

    far_w = [
        rcopy(a, d, w_snd.at[k], w_rcv.at[k], other) for k, (a, d) in enumerate(weight_pairs(s))
    ]
    for c in far_w:
        c.start()

    def halo(i, j):
        return rcopy(
            audio.at[2 * s + i, 0, :, rows_at(TL - REACH0 + j * TC, TC, TC)],
            rh.at[0, i, j, pl.ds(0, C)],
            h_snd.at[i, j],
            h_rcv.at[i, j],
            znext,
        )

    def halo_start(i):
        @pl.when(has_next)
        def _():
            for j in reversed(range(HJ)):
                halo(i, j).start()

    halo_start(0)

    mix_w = rcopy(wrst.at[s], wrst.at[s], t_snd.at[0], t_rcv.at[0], other)
    conv_w = rcopy(
        wct.at[s, pl.ds(0, G)], wct.at[s, pl.ds(0, G)], t_snd.at[1], t_rcv.at[1], other
    )
    mix_w.start()

    def phase_ready():
        prepare_conv(s)

    phase_ready()
    conv_w.start()

    for c in ldr + lds:
        c.wait()

    def mix_back():
        @pl.loop(0, 2 * NJ)
        def _(n):
            i, j = n // NJ, lax.rem(n, NJ)
            gh = dot(wrst[1], jnp.concatenate([gr[1, i, j], cs[i, j]], axis=0))
            high = gh.astype(BF)
            gb[1, i, j, pl.ds(0, C), :] = high
            gb[1, i, j, pl.ds(C, C), :] = (gh - high.astype(F32)).astype(BF)
            add_sum(0, gr[1, i, j])
            add_sum(1, cs[i, j])

    def add_sum(which, block):
        total = bsum[which]
        for k in range(TC // PW):
            total = total + block[:, k * PW : (k + 1) * PW].astype(F32)
        bsum[which] = total

    @pl.when(s == 1)
    def _():
        mix_back()
        for c in far_w[:6]:
            c.wait_recv()
        prepare_forward(0)

    for c in ldx + ldc:
        c.wait()

    def wide(tile):
        return jnp.concatenate([tile, tile], axis=1)

    def gate(layer, i, j):
        xx = rh[layer, i, j]
        out = []
        for g in range(2):
            lo = pl.ds(g * TC, TC)
            hi = pl.ds(C + g * TC, TC)
            t = jnp.tanh(dot(wcat[layer, lo, :], xx))
            q = 0.5 * jnp.tanh(0.5 * dot(wcat[layer, hi, :], xx)) + 0.5
            h = t * q
            hid[layer, i, j, lo, :] = h.astype(BF)
            out.append((q - h * t, h - h * q))
        return out

    def out_copy(kind, layer, i, j, src, dst):
        m = 2 * s + i
        return (
            copy(src, dst.at[m, :, rows_at(j * TC, TC, TC)], o_loc.at[kind, i, j]),
            rcopy(
                src,
                dst.at[m, :, rows_at(j * TC, TC, TC)],
                o_snd.at[kind, i, j],
                o_rcv.at[kind],
                other,
            ),
        )

    def out_start(kind, layer, i, j, src, dst):
        near, far = out_copy(kind, layer, i, j, src, dst)
        start_either(layer, near, far)

    def start_either(layer, near, far):
        @pl.when(s == layer)
        def _():
            near.start()

        @pl.when(s != layer)
        def _():
            far.start()

    def out_sent(kind, layer, i, j, src, dst):
        near, far = out_copy(kind, layer, i, j, src, dst)

        @pl.when(s == layer)
        def _():
            near.wait()

        @pl.when(s != layer)
        def _():
            far.wait_send()

    def out_arrived(kind, layer, dst):
        half = dst.at[pl.ds(0, 2)]

        @pl.when(s == layer)
        def _():
            copy(half, half, o_rcv.at[kind]).wait()

    def col_copy_f(i):
        return rcopy(colf_s.at[i], colf_r.at[i], cf_snd.at[i], cf_rcv.at[i], znext)

    def col_copy_b(i):
        return rcopy(colb_s.at[i], colb_r.at[i], cb_snd.at[i], cb_rcv.at[i], zprev)

    def pick_col(tile, lane):
        li = lax.broadcasted_iota(jnp.int32, (16, PW), 1)
        return dot_nt((li == lane).astype(F32).astype(BF), tile).astype(BF)

    def spread_col(rows):
        full = jnp.concatenate([rows] * (PW // 16), axis=0)
        parts = [
            dot_nt(eye[...], full[:, k * TC : (k + 1) * TC]) for k in range(C // TC)
        ]
        return jnp.concatenate(parts, axis=0)

    def fwd0(i, j, first=None):
        far = j >= HJ
        src_j = jnp.where(far, j - HJ, j)
        src_row = jnp.where(far, C, 0)
        mask = jnp.concatenate([mkb[0, i, j]] * (C // 16), axis=0)
        rh[0, i, j, pl.ds(0, C), :] = rh[0, i, src_j, rows_at(src_row, C, C), :] * mask
        parts = gate(0, i, j)
        for g in range(2):
            gb[0, i, j, pl.ds(g * TC, TC), :] = parts[g][0].astype(BF)
            gb[0, i, j, pl.ds(C + g * TC, TC), :] = parts[g][1].astype(BF)
        if first is not None:

            @pl.when(jnp.logical_and(first, s == 1))
            def _():
                for c in far_w[6:]:
                    c.wait_recv()

        rs = dot(wrs[0, pl.ds(0, C)], hid[0, i, j]) + wide(rsbias[0, pl.ds(0, C)])
        x1 = (rh[0, i, j, pl.ds(C, C), :].astype(F32) + rs).astype(BF)
        rh[1, i, j, pl.ds(C, C), :] = x1
        rh[1, i, j, pl.ds(G, KC), :] = rh[0, i, j, pl.ds(G, KC), :]
        out_start(0, 0, i, j, rh.at[1, i, j, pl.ds(C, C)], res_out)

        @pl.when(jnp.logical_and(j == NJ - 1, has_next))
        def _():
            colf_s[i] = pick_col(rh[1, i, j, pl.ds(C, C), pl.ds(TC - PW, PW)], PW - 1)
            col_copy_f(i).start()

    lane_c = lax.broadcasted_iota(jnp.int32, (C, PW), 1)

    def layer1(i, j):
        x1 = rh[1, i, j, pl.ds(C, C), :].astype(F32)
        jm = jnp.maximum(j - 1, 0)
        tile = rh[1, i, jm, pl.ds(C, C), pl.ds(TC - PW, PW)].astype(F32)
        tile = jnp.where(j == 0, htile[i].astype(F32), tile)
        turned = pltpu.roll(x1, 1, 1)
        first = jnp.where(lane_c == 0, pltpu.roll(tile, 1, 1), turned[:, :PW])
        shifted = jnp.concatenate([first, turned[:, PW:]], axis=1) * mkf[1, i, j, pl.ds(0, 1), :]
        rh[1, i, j, pl.ds(0, C), :] = shifted.astype(BF)
        gh = gb[1, i, j, pl.ds(0, C), :].astype(F32) + gb[1, i, j, pl.ds(C, C), :].astype(F32)
        parts = gate(1, i, j)
        for g in range(2):
            part = gh[g * TC : (g + 1) * TC]
            gb[1, i, j, pl.ds(g * TC, TC), :] = (part * parts[g][0]).astype(BF)
            gb[1, i, j, pl.ds(C + g * TC, TC), :] = (part * parts[g][1]).astype(BF)

    def layer1_back(i, j):
        dg = dot(wct[1], gb[1, i, j])
        past = dg[:C] * mkf[1, i, j, pl.ds(0, 1), :]
        turned = pltpu.roll(past, TC - 1, 1)
        last = jnp.where(lane_c == PW - 1, pltpu.roll(bcar[i].astype(F32), PW - 1, 1), turned[:, TC - PW :])
        back = jnp.concatenate([turned[:, : TC - PW], last], axis=1)
        gres = (gr[1, i, j].astype(F32) + dg[C:G] + back).astype(BF)
        gr[0, i, j] = gres
        add_sum(2, gres)
        bcar[i] = past[:, :PW].astype(BF)
        cg[i, j] = dg[G : G + KC]

        @pl.when(jnp.logical_and(j == 0, has_prev))
        def _():
            colb_s[i] = pick_col(past[:, :PW].astype(BF), 0)
            col_copy_b(i).start()

    def phase_near():
        @pl.loop(0, 2 * (NJ - HJ))
        def _(n):
            fwd0(n // (NJ - HJ), NJ - 1 - lax.rem(n, NJ - HJ), n == 0)

    phase_near()
    halo_start(1)

    @pl.when(s == 0)
    def _():
        for c in far_w:
            c.wait_recv()
        prepare_forward(1)

    mix_w.wait_recv()

    @pl.when(s == 0)
    def _():
        mix_back()

    def phase_main():
        @pl.loop(0, 2 * NJ)
        def _(n):
            q = n - 2
            i = jnp.where(n < 2, n, q // (NJ - 1))
            j = jnp.where(n < 2, NJ - 1, NJ - 2 - lax.rem(q, NJ - 1))

            @pl.when(jnp.logical_and(n >= 2, j >= 1))
            def _():
                @pl.when(jnp.logical_and(has_prev, j <= HJ))
                def _():
                    halo(i, j - 1).wait_recv()

                fwd0(i, j - 1)

            @pl.when(jnp.logical_and(j == 0, has_prev))
            def _():
                col_copy_f(i).wait_recv()
                htile[i] = spread_col(colf_r[i]).astype(BF)

            layer1(i, j)

    phase_main()

    sizes = [G, G, G, G, G, G, cr]
    offs = [G * k for k in range(7)]
    SKIP, RES, COND = 4, 5, 6
    ARA, ARB, ARZ, ARM, AGZ, AGB, AGA = range(7)

    def geo(p):
        size, off = sizes[p], offs[p]
        na, nb_ = size // r, size // (r * r)
        base_a = off + amem * na
        base_b = base_a + bmem * nb_
        return size, off, na, nb_, base_a, base_b

    def x_copy(layer, p):
        return rcopy(
            pb.at[0, pl.ds(offs[p], sizes[p])],
            prv.at[pl.ds(offs[p], sizes[p])],
            x_snd.at[layer, p],
            x_rcv.at[layer, p],
            other,
        )

    def gathered(layer, rows):
        return ag1.at[rows] if layer == 1 else pb.at[0, rows]

    def wait_rows(count, sem, layer):
        ref = pb.at[1 + layer, pl.ds(0, count)]
        copy(ref, ref, sem).wait()

    def sum_rows(layer, start, count, parts):
        total = pb[1 + layer, rows_at(start, count, 16), :].astype(F32)
        for part in parts:
            total = total + part.astype(F32)
        return total.astype(BF)

    def add_rows(layer, start, count, parts):
        pb[1 + layer, rows_at(start, count, 16), :] = sum_rows(layer, start, count, parts)

    def step0(layer, p):
        size, off, na, nb_, base_a, base_b = geo(p)
        x_copy(layer, p).wait()
        add_rows(layer, off, size, [prv[pl.ds(off, size), :]])
        if layer == 1:
            pl.semaphore_signal(credit.at[p], inc=1, device_id=other, device_id_type=MESH)
        for o in range(1, r):
            a2, dev = sa_dev(o)
            rcopy(
                pb.at[1 + layer, rows_at(off + a2 * na, na, 16)],
                ra_buf.at[layer, o - 1, pl.ds(off // r, na)],
                ar_snd.at[ARA, layer, p],
                ar_rcv.at[ARA, layer, p],
                dev,
            ).start()

    def step1(layer, p):
        size, off, na, nb_, base_a, base_b = geo(p)
        wait_rows((r - 1) * na, ar_rcv.at[ARA, layer, p], layer)
        wait_rows((r - 1) * na, ar_snd.at[ARA, layer, p], layer)
        add_rows(
            layer, base_a, na, [ra_buf[layer, o, pl.ds(off // r, na), :] for o in range(r - 1)]
        )
        for o in range(1, r):
            b2, dev = sb_dev(o)
            rcopy(
                pb.at[1 + layer, rows_at(base_a + b2 * nb_, nb_, 16)],
                rb_buf.at[layer, o - 1, pl.ds(off // (r * r), nb_)],
                ar_snd.at[ARB, layer, p],
                ar_rcv.at[ARB, layer, p],
                dev,
            ).start()

    def step2(layer, p):
        size, off, na, nb_, base_a, base_b = geo(p)
        wait_rows((r - 1) * nb_, ar_rcv.at[ARB, layer, p], layer)
        wait_rows((r - 1) * nb_, ar_snd.at[ARB, layer, p], layer)
        add_rows(
            layer,
            base_b,
            nb_,
            [rb_buf[layer, o, pl.ds(off // (r * r), nb_), :] for o in range(r - 1)],
        )

        @pl.when(depth == 0)
        def _():
            inward(layer, p, hops == 1)

    def arrived(layer, p, slot):
        size, off, na, nb_, base_a, base_b = geo(p)
        return rz_buf.at[layer, slot, pl.ds(off // (r * r), nb_)]

    def inward(layer, p, at_middle):
        size, off, na, nb_, base_a, base_b = geo(p)
        stage = ARM if at_middle else ARZ
        rcopy(
            pb.at[1 + layer, rows_at(base_b, nb_, 16)],
            arrived(layer, p, int(at_middle)),
            ar_snd.at[stage, layer, p],
            ar_rcv.at[stage, layer, p],
            inner,
        ).start()

    def spread(layer, p, stage, start, count, devs):
        for dev in devs:
            rcopy(
                gathered(layer, rows_at(start, count, 16)),
                gathered(layer, rows_at(start, count, 16)),
                ar_snd.at[stage, layer, p],
                ar_rcv.at[stage, layer, p],
                dev,
            ).start()

    def step3(layer, p):
        size, off, na, nb_, base_a, base_b = geo(p)
        for k in range(1, hops):

            @pl.when(depth == k)
            def _():
                wait_rows(nb_, ar_rcv.at[ARZ, layer, p], layer)
                add_rows(layer, base_b, nb_, [arrived(layer, p, 0)[...]])
                inward(layer, p, k == hops - 1)

    def outward(layer, p):
        size, off, na, nb_, base_a, base_b = geo(p)
        spread(layer, p, AGZ, base_b, nb_, [outer])

    def share(layer, p):
        size, off, na, nb_, base_a, base_b = geo(p)
        spread(layer, p, AGB, base_b, nb_, [sb_dev(o)[1] for o in range(1, r)])

    def step4(layer, p):
        size, off, na, nb_, base_a, base_b = geo(p)

        @pl.when(depth == hops - 1)
        def _():
            wait_rows(nb_, ar_rcv.at[ARM, layer, p], layer)
            wait_rows(nb_, ar_snd.at[ARM, layer, p], layer)
            gathered(layer, rows_at(base_b, nb_, 16))[...] = sum_rows(
                layer, base_b, nb_, [arrived(layer, p, 1)[...]]
            )
            if hops > 1:
                outward(layer, p)
            share(layer, p)

    def step5(layer, p):
        size, off, na, nb_, base_a, base_b = geo(p)
        for k in reversed(range(hops - 1)):

            @pl.when(depth == k)
            def _():
                wait_rows(nb_, ar_rcv.at[AGZ, layer, p], layer)
                wait_rows(nb_, ar_snd.at[ARZ, layer, p], layer)
                if k > 0:
                    outward(layer, p)
                share(layer, p)

    def step6(layer, p):
        size, off, na, nb_, base_a, base_b = geo(p)
        wait_rows((r - 1) * nb_, ar_rcv.at[AGB, layer, p], layer)
        wait_rows((r - 1) * nb_, ar_snd.at[AGB, layer, p], layer)

        @pl.when(depth > 0)
        def _():
            wait_rows(nb_, ar_snd.at[AGZ, layer, p], layer)

        spread(layer, p, AGA, base_a, na, [sa_dev(o)[1] for o in range(1, r)])

    def final_copies(layer, p):
        src = gathered(layer, pl.ds(offs[p], sizes[p]))
        dst = wg_out.at[s, pl.ds(offs[p], sizes[p])]
        return (
            copy(src, dst, f_loc.at[p]),
            rcopy(src, dst, f_snd.at[p], f_rcv.at[p], other),
        )

    def step7(layer, p):
        size, off, na, nb_, base_a, base_b = geo(p)
        wait_rows((r - 1) * na, ar_rcv.at[AGA, layer, p], layer)
        wait_rows((r - 1) * na, ar_snd.at[AGA, layer, p], layer)
        near, far = final_copies(layer, p)

        @pl.when(s == layer)
        def _():
            near.start()

        @pl.when(s != layer)
        def _():
            far.start()

    steps = [step0, step1, step2, step3, step4, step5, step6, step7]

    def at(n, table):
        for k, todo in table.items():

            @pl.when(n == k)
            def _(todo=todo):
                for st, layer, p in todo:
                    steps[st](layer, p)

    def task_start(layer, mine, pieces):
        if layer == 0:

            @pl.when(mine == 0)
            def _():
                for p in pieces:
                    pl.semaphore_wait(credit.at[p], 1)

        return jnp.where(mine == 1, s, 1 - s), mine * (1 + layer)

    def task_end(layer, mine, pieces):
        @pl.when(mine == 0)
        def _():
            for p in pieces:
                x_copy(layer, p).start()

    def conv_tasks(layer, table):
        @pl.loop(0, 4)
        def _(n):
            k = n // 2
            mine = lax.rem(n, 2)
            half = jnp.where(mine == 1, s, 1 - s)
            dst = mine * (1 + layer)
            for kk in range(2):
                if layer == 0:

                    @pl.when(n == 2 * kk)
                    def _():
                        for p in (2 * kk, 2 * kk + 1):
                            pl.semaphore_wait(credit.at[p], 1)

            ch = rows_at(half * C + k * TC, TC, TC)
            total = dot_nt(gb[layer, 0, 0], rh[layer, 0, 0, ch, :])
            for i in range(2):
                for j in range(NJ):
                    if i + j > 0:
                        total = total + dot_nt(gb[layer, i, j], rh[layer, i, j, ch, :])
            total = total.astype(BF)
            pb[dst, rows_at(k * 2 * G, G, G), :] = total[:, :PW]
            pb[dst, rows_at(k * 2 * G + G, G, G), :] = total[:, PW:]
            for kk in range(2):

                @pl.when(n == 2 * kk)
                def _():
                    for p in (2 * kk, 2 * kk + 1):
                        x_copy(layer, p).start()

            at(n, table)

    def mix_tasks(layer, piece, src, table):
        @pl.loop(0, 2)
        def _(n):
            half, dst = task_start(layer, n, [piece])
            ch = rows_at(half * TC, TC, TC)
            total = dot_nt(src(0, 0), hid[layer, 0, 0, ch, :])
            for i in range(2):
                for j in range(NJ):
                    if i + j > 0:
                        total = total + dot_nt(src(i, j), hid[layer, i, j, ch, :])
            total = total.astype(BF)
            pb[dst, pl.ds(offs[piece], C), :] = total[:, :PW]
            pb[dst, pl.ds(offs[piece] + C, C), :] = total[:, PW:]
            task_end(layer, n, [piece])
            at(n, table)

    def cond_tasks(layer, table):
        @pl.loop(0, 2)
        def _(n):
            half, dst = task_start(layer, n, [COND])
            gp_rows = rows_at(half * C, C, C)
            total = jnp.zeros((PW, C), F32)
            for i in range(2):
                for j in range(NJ):
                    total = total + dot_nt(
                        rh[layer, i, j, pl.ds(G, PW), :], gb[layer, i, j, gp_rows, :]
                    )
            cacc[...] = total
            which = jnp.where(half == 1, 1, 2 - 2 * layer)
            cacc[pl.ds(KC + 3, 1), :] = jnp.sum(bsum[which].T, axis=0, keepdims=True)
            for k in range(C // PW):
                pb[dst, pl.ds(offs[COND] + k * CROWS, CROWS), :] = cacc[
                    pl.ds(0, CROWS), k * PW : (k + 1) * PW
                ].astype(BF)
            if cr > 4 * CROWS:
                pb[dst, pl.ds(offs[COND] + 4 * CROWS, cr - 4 * CROWS), :] = jnp.zeros(
                    (cr - 4 * CROWS, PW), BF
                )
            task_end(layer, n, [COND])
            at(n, table)

    def fix_last(i):
        @pl.when(has_next)
        def _():
            col_copy_b(i).wait_recv()
            tile = gr[0, i, NJ - 1, :, pl.ds(TC - PW, PW)].astype(F32)
            add = jnp.where(lane_c == PW - 1, spread_col(colb_r[i]), 0.0)
            bsum[2] = bsum[2] + add
            gr[0, i, NJ - 1, :, pl.ds(TC - PW, PW)] = (tile + add).astype(BF)

    def skip_src(i, j):
        return cs[i, j]

    def run_steps(todo):
        for st, layer, p in todo:
            steps[st](layer, p)

    def phase_l1b():
        conv_w.wait_recv()

        @pl.loop(0, 2 * NJ)
        def _(n):
            layer1_back(n // NJ, NJ - 1 - lax.rem(n, NJ))
            at(n, T_L1B)


    def hb_copy(i, j):
        return rcopy(hs.at[i, j], hb.at[i, j], hb_snd.at[i, j], hb_rcv.at[i, j], zprev)

    def back0(i, j):
        gh = dot(wrst[0], jnp.concatenate([gr[0, i, j], cs[i, j]], axis=0))
        for g in range(2):
            part = gh[g * TC : (g + 1) * TC]
            for row in (g * TC, C + g * TC):
                rows = pl.ds(row, TC)
                gb[0, i, j, rows, :] = (part * gb[0, i, j, rows, :].astype(F32)).astype(BF)

    def grad0(i, j):
        dg = dot(wct[0], gb[0, i, j])
        past = dg[:C] * mkf[0, i, j, pl.ds(0, 1), :]
        gr[1, i, j] = (gr[0, i, j].astype(F32) + dg[C:G]).astype(BF)
        cg[i, j] = cg[i, j] + dg[G : G + KC]
        m = 2 * s + i
        cols = rows_at(j * TC, TC, TC)
        hc = KC // 2
        copy(
            cg.at[i, j, rows_at(s * hc, hc, 8)], cgrad_out.at[m, :, cols], c_loc.at[0]
        ).start()
        rcopy(
            cg.at[i, j, rows_at((1 - s) * hc, hc, 8)],
            cgrad_out.at[m, :, cols],
            c_loc.at[1],
            c_loc.at[2],
            other,
        ).start()
        return past

    def phase_b0a():
        @pl.loop(0, 2 * HJ)
        def _(n):
            back0(n // HJ, lax.rem(n, HJ))
            at(n, T_B0A)


    def phase_fix():
        for i in range(2):
            fix_last(i)
            for j in range(NJ):
                out_start(4, 1, i, j, gr.at[0, i, j], rgrad_out)

    def phase_b0b():
        @pl.loop(0, 2 * (NJ - HJ))
        def _(n):
            back0(n // (NJ - HJ), HJ + lax.rem(n, NJ - HJ))
            at(n, T_B0B)


    def phase_gh(i, table):
        @pl.loop(0, HJ)
        def _(j):
            past = grad0(i, j)

            @pl.when(has_prev)
            def _():
                hs[i, j] = past.astype(BF)
                hb_copy(i, j).start()

            at(j, table)


    order = {
        "W1C": lambda: conv_tasks(1, T_W1C),
        "SK1": lambda: mix_tasks(1, SKIP, skip_src, T_SK1),
        "RE1": lambda: mix_tasks(1, RES, lambda i, j: gr[1, i, j], T_RE1),
        "CO1": lambda: cond_tasks(1, T_CO1),
        "SK0": lambda: mix_tasks(0, SKIP, skip_src, T_SK0),
        "L1B": phase_l1b,
        "B0A": phase_b0a,
        "FIX": phase_fix,
        "B0B": phase_b0b,
        "GHA": lambda: phase_gh(0, T_GHA),
        "GHB": lambda: phase_gh(1, T_GHB),
        "RE0": lambda: mix_tasks(0, RES, lambda i, j: gr[0, i, j], T_RE0),
        "W0C": lambda: conv_tasks(0, T_W0C),
        "CO0": lambda: cond_tasks(0, T_CO0),
    }
    for name in ORDER:
        order[name]()

    def phase_g0():
        @pl.loop(0, 2 * (NJ - HJ))
        def _(n):
            i, k = n // (NJ - HJ), lax.rem(n, NJ - HJ)
            past = grad0(i, HJ + k)
            gr[1, i, k] = (gr[1, i, k].astype(F32) + past).astype(BF)
            out_start(5, 0, i, k, gr.at[1, i, k], rgrad_out)
            at(n, T_G0)

    phase_g0()

    def phase_rs():
        @pl.loop(0, 2 * NJ)
        def _(n):
            i, j = n // NJ, lax.rem(n, NJ)
            x1 = rh.at[1, i, j, pl.ds(C, C)]
            sk0 = rh.at[1, i, j, pl.ds(0, C)]
            sk1 = hid.at[1, i, j]
            skip = dot(wrs[0, pl.ds(C, C)], hid[0, i, j]) + wide(rsbias[0, pl.ds(C, C)])
            skip = skip.astype(BF)
            sk0[...] = skip
            out_start(1, 0, i, j, sk0, skip_out)
            rs = dot(wrs[1], sk1[...]) + wide(rsbias[1])
            sk1[...] = (skip.astype(F32) + rs[C:]).astype(BF)
            out_start(3, 1, i, j, sk1, skip_out)
            out_sent(0, 0, i, j, x1, res_out)
            x1[...] = (x1[...].astype(F32) + rs[:C]).astype(BF)
            out_start(2, 1, i, j, x1, res_out)
            at(n, T_RS)

    phase_rs()

    def phase_tail():
        run_steps(TAIL)

    phase_tail()

    for i in range(2):
        for k in range(HJ):
            j = NJ - HJ + k

            @pl.when(has_next)
            def _():
                hb_copy(i, k).wait_recv()
                gr[1, i, j] = (gr[1, i, j].astype(F32) + hb[i, k].astype(F32)).astype(BF)

            out_start(5, 0, i, j, gr.at[1, i, j], rgrad_out)

    def phase_last():
        run_steps(LAST)

    phase_last()

    @pl.loop(0, 2 * NJ)
    def _(n):
        i, j = n // NJ, lax.rem(n, NJ)
        blk = gr.at[0, i, j]
        out_sent(1, 0, i, j, blk, skip_out)
        out_sent(2, 1, i, j, blk, res_out)
        out_sent(3, 1, i, j, blk, skip_out)
        out_sent(4, 1, i, j, blk, rgrad_out)
        out_sent(5, 0, i, j, blk, rgrad_out)

    out_arrived(0, 0, res_out)
    out_arrived(1, 0, skip_out)
    out_arrived(2, 1, res_out)
    out_arrived(3, 1, skip_out)
    out_arrived(4, 1, rgrad_out)
    out_arrived(5, 0, rgrad_out)
    half = cgrad_out.at[pl.ds(0, 2)]
    for k in range(3):
        copy(half, half, c_loc.at[k]).wait()
    for p in range(7):
        near, far = final_copies(0, p)
        near.wait()
        far.wait()
    for c in far_w + [mix_w, conv_w]:
        c.wait_send()

    @pl.when(has_next)
    def _():
        for i in range(2):
            for j in range(HJ):
                halo(i, j).wait_send()
            col_copy_f(i).wait_send()

    @pl.when(has_prev)
    def _():
        for i in range(2):
            col_copy_b(i).wait_send()
            for j in range(HJ):
                hb_copy(i, j).wait_send()


def finalize(
    res, skip, rgrad, cgrad, wg,
    res_o, skip_o, rgrad_o, cgrad_o, conv_o, convb_o, condw_o, resw_o, resb_o, skipw_o, skipb_o,
    rbuf, sbuf, cbuf, rin, rwide, win, convf, mixf, condf, cbf, rbf, sbf, sem_in, sem_cp, sem_out,
):
    M, C, TL = res.shape
    G = 2 * C
    KC = condw_o.shape[0]
    copies = []
    loads = [pltpu.make_async_copy(wg.at[h], win.at[h], sem_in.at[h]) for h in range(2)]
    reads = [pltpu.make_async_copy(rgrad.at[m], rin.at[m], sem_in.at[2 + m]) for m in range(M)]
    for c in loads + reads:
        c.start()
    passing = []
    for k, (a, buf, o) in enumerate(
        ((res, rbuf, res_o), (skip, sbuf, skip_o), (cgrad, cbuf, cgrad_o))
    ):
        for m in range(M):
            c = pltpu.make_async_copy(a.at[m], buf.at[m], sem_cp.at[k, m])
            c.start()
            passing.append((c, buf.at[m], o.at[m], 8 + M + k * M + m))

    def put(src, dst, k):
        c = pltpu.make_async_copy(src, dst, sem_out.at[k])
        c.start()
        copies.append(c)

    for h in range(2):
        loads[h].wait()
        for q in range(C // PW):
            convf[h, :, q * PW : (q + 1) * PW] = win[h, pl.ds(q * G, G), :].astype(F32)
        put(convf.at[h], conv_o.at[h], h)
        for q in range(2):
            lanes = slice(h * 2 * PW + q * PW, h * 2 * PW + (q + 1) * PW)
            mixf[pl.ds(0, C), lanes] = win[h, pl.ds(5 * G + q * C, C), :].astype(F32)
            mixf[pl.ds(C, C), lanes] = win[h, pl.ds(4 * G + q * C, C), :].astype(F32)
        for q in range(C // PW):
            blk = win[h, pl.ds(6 * G + q * CROWS, CROWS), :].astype(F32)
            lanes = slice(h * C + q * PW, h * C + (q + 1) * PW)
            condf[:, lanes] = blk[:KC]
            cbf[:, lanes] = blk[KC : KC + 1]
            (sbf if h else rbf)[:, q * PW : (q + 1) * PW] = blk[KC + 3 : KC + 4]
    put(mixf.at[pl.ds(0, C)], resw_o, 2)
    put(mixf.at[pl.ds(C, C)], skipw_o, 3)
    put(condf, condw_o, 4)
    put(cbf, convb_o, 5)
    put(rbf, resb_o, 6)
    put(sbf, skipb_o, 7)
    for c, src, dst, k in passing:
        c.wait()
        put(src, dst, k)
    for m in range(M):
        reads[m].wait()
        rwide[m] = rin[m].astype(F32)
        put(rwide.at[m], rgrad_o.at[m], 8 + m)
    for c in copies:
        c.wait()


def local(nz, r, *args):
    audio, cond = args[0], args[1]
    M, _, C, TL = audio.shape
    KC = cond.shape[2]
    G = 2 * C
    NJ = TL // TC
    HJ = REACH0 // TC
    KP = G + PW
    cr = -(-4 * CROWS // (16 * r * r)) * 16 * r * r
    HR = 6 * G + cr
    any_ = pl.BlockSpec(memory_space=pl.ANY)
    smem = pl.BlockSpec(memory_space=pltpu.SMEM)
    V = pltpu.VMEM
    D = pltpu.SemaphoreType.DMA
    scratch = [
        V((2, G, KP), BF),
        V((2, G, C), BF),
        V((2, KP, G), BF),
        V((2, C, G), BF),
        V((2, 1, G), F32),
        V((2, 1, C), F32),
        V((2, 1, C), F32),
        V((2, G, PW), F32),
        V((2, 2, NJ, KP, TC), BF),
        V((2, 2, NJ, C, TC), BF),
        V((2, 2, NJ, G, TC), BF),
        V((2, 2, NJ, C, TC), BF),
        V((2, NJ, C, TC), BF),
        V((HR, PW), BF),
        V((2, NJ, KC, TC), F32),
        V((TC, TC), BF),
        V((3, C, PW), F32),
        V((2, 2, NJ, 8, TC), F32),
        V((2, 2, NJ, 16, TC), BF),
        V((2, C, PW), BF),
        V((2, C, PW), BF),
        V((2, 16, C), BF),
        V((2, 16, C), BF),
        V((2, 16, C), BF),
        V((2, 16, C), BF),
        V((2, HJ, C, TC), BF),
        V((2, HJ, C, TC), BF),
        V((3, HR, PW), BF),
        V((HR, PW), BF),
        V((2, r - 1, HR // r, PW), BF),
        V((2, r - 1, HR // (r * r), PW), BF),
        V((2, 2, HR // (r * r), PW), BF),
        V((PW, C), F32),
        D((8,)),
        D((2, NJ)),
        D((2, NJ)),
        D((2, NJ)),
        D((2, NJ)),
        D((8,)),
        D((8,)),
        D((2,)),
        D((2,)),
        D((2, HJ)),
        D((2, HJ)),
        D((2,)),
        D((2,)),
        D((2,)),
        D((2,)),
        D((2, HJ)),
        D((2, HJ)),
        D((6, 2, NJ)),
        D((6, 2, NJ)),
        D((6,)),
        D((3,)),
        D((2, 7)),
        D((2, 7)),
        D((7, 2, 7)),
        D((7, 2, 7)),
        D((7,)),
        D((7,)),
        D((7,)),
        pltpu.SemaphoreType.REGULAR((7,)),
    ]
    res, skip, rgrad, cgrad, wg = pl.pallas_call(
        functools.partial(kernel, nz, r, cr),
        out_shape=(
            jax.ShapeDtypeStruct((M, C, TL), BF),
            jax.ShapeDtypeStruct((M, C, TL), BF),
            jax.ShapeDtypeStruct((M, C, TL), BF),
            jax.ShapeDtypeStruct((M, KC // 2, TL), F32),
            jax.ShapeDtypeStruct((2, HR, PW), BF),
        ),
        in_specs=[any_, any_, smem] + [any_] * 9,
        out_specs=(any_,) * 5,
        scratch_shapes=scratch,
        compiler_params=pltpu.CompilerParams(
            collective_id=0, has_side_effects=True, vmem_limit_bytes=64 * 2**20 - 2**17
        ),
        cost_estimate=pl.CostEstimate(
            flops=40 * 10**9, bytes_accessed=36 * 10**6, transcendentals=4 * 10**6
        ),
    )(*args[:5], jnp.swapaxes(args[5], 1, 2), *args[6:])
    shapes = [
        ((M, C, TL), BF),
        ((M, C, TL), BF),
        ((M, C, TL), F32),
        ((M, KC // 2, TL), F32),
        ((2, G, C), F32),
        ((1, G), F32),
        ((KC, G), F32),
        ((C, C), F32),
        ((1, C), F32),
        ((C, C), F32),
        ((1, C), F32),
    ]
    done = pl.pallas_call(
        finalize,
        out_shape=tuple(jax.ShapeDtypeStruct(a, d) for a, d in shapes),
        in_specs=[any_] * 5,
        out_specs=(any_,) * len(shapes),
        scratch_shapes=[
            V((M, C, TL), BF),
            V((M, C, TL), BF),
            V((M, KC // 2, TL), F32),
            V((M, C, TL), BF),
            V((M, C, TL), F32),
            V((2, HR, PW), BF),
            V((2, G, C), F32),
            V((G, C), F32),
            V((KC, G), F32),
            V((1, G), F32),
            V((1, C), F32),
            V((1, C), F32),
            D((2 + M,)),
            D((3, M)),
            D((8 + 4 * M,)),
        ],
        compiler_params=pltpu.CompilerParams(vmem_limit_bytes=64 * 2**20 - 2**17),
    )(res, skip, rgrad, cgrad, wg)
    out = [v[None] for v in done]
    out[0], out[1], out[2] = (done[k][None, :, None] for k in range(3))
    out[3] = done[3][:, None]
    out[5], out[8], out[10] = done[5], done[8], done[10]
    out[6] = jnp.swapaxes(out[6], 1, 2)
    return tuple(out)


def solution(mesh):
    nz = mesh.shape["tm"]
    r = math.isqrt(mesh.shape["batch"])
    in_specs = (
        P(None, "batch", None, "tm"),
        P(None, "batch", None, "tm"),
        P(None, "batch", None),
        P("section", None, None, None),
        P("section", None),
        P("section", None, None),
        P("section", None, None),
        P("section", None),
        P("section", None, None),
        P("section", None),
        P(None, "batch", None, "tm"),
        P(None, "batch", None, "tm"),
    )
    out_specs = (
        P("section", None, "batch", None, "tm"),
        P("section", None, "batch", None, "tm"),
        P("section", None, "batch", None, "tm"),
        P(None, "batch", "section", "tm"),
        P("section", None, None, None),
        P("section", None),
        P("section", None, None),
        P("section", None, None),
        P("section", None),
        P("section", None, None),
        P("section", None),
    )
    return jax.shard_map(
        functools.partial(local, nz, r),
        mesh=mesh,
        in_specs=in_specs,
        out_specs=out_specs,
        check_vma=False,
    )
```
